32 devices in a mesh: dev: 32 (over z, y, x, core).
Axes of the slice: x: 2, y: 2, z: 4, core: 2. Of those that a mesh axis runs over, the one named last changes fastest.
Arguments:
- tokens: bfloat16 [8192, 192], P('dev'), may hold values from -6 to 6
- ranges: int32 [32, 2], replicated, may hold values from 0 to 7936, as said below
- attn_in: bfloat16 [2, 110592], P(None, 'dev'), may hold values from -0.4375 to 0.4375
- attn_out: bfloat16 [2, 36864], P(None, 'dev'), may hold values from -3.5 to 3.5
- mlp_in: bfloat16 [2, 147456], P(None, 'dev'), may hold values from -0.4375 to 0.4375
- mlp_out: bfloat16 [2, 147456], P(None, 'dev'), may hold values from -0.21875 to 0.21875
- vectors: bfloat16 [2, 2304], P(None, 'dev'), may hold values from -0.75 to 1.5, as said below
- cotangent: bfloat16 [8192, 192], P('dev'), may hold values from -6 to 6
Outputs:
- activations: bfloat16 [8192, 192], P('dev')
- input_grad: float32 [8192, 192], P('dev')
- attn_in_grad: float32 [2, 110592], P(None, 'dev')
- attn_out_grad: float32 [2, 36864], P(None, 'dev')
- mlp_in_grad: float32 [2, 147456], P(None, 'dev')
- mlp_out_grad: float32 [2, 147456], P(None, 'dev')
- vectors_grad: float32 [2, 2304], P(None, 'dev')
The draws below stay inside these ranges and needn't reach their ends.
Inputs may be any that keep to these rules, and one draw needn't show every extreme that they name: Row j gives the range of stream positions on device j; ranges follow one another from 0 to 7936; each device holds 240 to 256 tokens, some device exactly 256. `vectors`: norm gains lie within 0.5 to 1.5.
All inputs are finite; a program needn't handle non-finite values.
Results may differ from the reference program's by a relative error of at most 0.01.
Values may be sent and summed in bfloat16 or wider, within the bound.
A program may use at most 64 MiB of HBM per device.

```python
import math
import jax
import jax.numpy as jnp
from jax import lax

D = 192
HEADS = 3
HD = 64
FF = 768
LAYERS = 2
IMG_LEN = 197
SLOTS = 256
SPREAD = 4
TOKENS = 7936
IMAGES = 41
N_DEV = 32


def draw_ranges(key, part):
    steps_key = jax.random.fold_in(key, 11)
    pick_key = jax.random.fold_in(key, 12)
    shifts = jax.random.randint(steps_key, (N_DEV,), -SPREAD, SPREAD + 1)
    chosen = jax.random.randint(pick_key, (), 0, N_DEV)
    positions = jnp.arange(N_DEV)
    shifts = jnp.where(positions == chosen, SPREAD, shifts)
    shifts = jnp.where(positions == (chosen - 1) % N_DEV, -SPREAD, shifts)
    lengths = SLOTS - 2 * SPREAD + shifts - jnp.roll(shifts, 1)
    ends = jnp.cumsum(lengths)
    starts = ends - lengths
    return jnp.stack([starts, ends], axis=1).astype(jnp.int32)


def draw_vectors(key, part):
    columns = 8 * D + FF
    segment = jnp.arange(columns) // D
    is_gain = (segment == 0) | (segment == 5)
    gain_key = jax.random.fold_in(key, 21)
    bias_key = jax.random.fold_in(key, 22)
    gain_part = jnp.clip(1.0 + 0.2 * jax.random.normal(gain_key, (LAYERS, columns), jnp.float32), 0.5, 1.5)
    bias_part = jnp.clip(0.3 * jax.random.normal(bias_key, (LAYERS, columns), jnp.float32), -0.75, 0.75)
    return jnp.where(is_gain[None, :], gain_part, bias_part).astype(jnp.bfloat16)


def levels(own_key, extent, shards, least, largest):
    factor_of, own = 1.0, jax.random.fold_in(own_key, 6)
    for dim, blocks in shards:
        steps = jnp.exp(jax.random.uniform(jax.random.fold_in(own, dim), (blocks,), jnp.float32, least / len(shards), largest / len(shards)))
        factor_of = factor_of * jnp.repeat(steps, extent[dim] // blocks).reshape([-1 if axis == dim else 1 for axis in range(len(extent))])
    return factor_of


def bell_draw(own_key, extent, deviation, reach, shards=(), held_as=jnp.bfloat16):
    level = levels(own_key, extent, shards, -0.22, 0.18) if shards else 1.0
    values = jax.random.normal(own_key, extent, jnp.float32) * deviation * level
    return jnp.minimum(jnp.maximum(values, -reach), reach).astype(held_as)


def setup_inputs(seed: int = 0) -> dict:
    keys = jax.random.split(jax.random.key(seed), 9)
    tokens = bell_draw(keys[0], (N_DEV * SLOTS, D), 1.0, 6.0, ((0, 32),))
    ranges = draw_ranges(jax.random.fold_in(keys[8], 71), 0)
    attn_in = bell_draw(keys[2], (LAYERS, 3 * D * D), D ** -0.5, 0.4375, ((1, 32),))
    attn_out = bell_draw(keys[3], (LAYERS, D * D), (D // 64) ** -0.5, 3.5, ((1, 32),))
    mlp_in = bell_draw(keys[4], (LAYERS, D * FF), D ** -0.5, 0.4375, ((1, 32),))
    mlp_out = bell_draw(keys[5], (LAYERS, FF * D), FF ** -0.5, 0.21875, ((1, 32),))
    vectors = draw_vectors(jax.random.fold_in(keys[8], 71), 0)
    cotangent = bell_draw(keys[7], (N_DEV * SLOTS, D), 1.0, 6.0, ((0, 32),))
    return {"tokens": tokens, "ranges": ranges, "attn_in": attn_in, "attn_out": attn_out, "mlp_in": mlp_in, "mlp_out": mlp_out, "vectors": vectors, "cotangent": cotangent}


@jax.custom_vjp
def low(v):
    return lax.optimization_barrier(v.astype(jnp.bfloat16)).astype(jnp.float32)

@jax.custom_vjp
def low_back(v):
    return v

def low_keep(v):
    return (low(v), None)

def low_pass(kept, grad):
    return (grad,)

def back_keep(v):
    return (v, None)

def back_low(kept, grad):
    return (low(grad),)
low.defvjp(low_keep, low_pass)
low_back.defvjp(back_keep, back_low)
group_images = 16
masked_fill = -1e+30

def matmul(left, right):
    return jnp.dot(left, right, precision=lax.Precision.HIGHEST)

def layer_norm(hidden, gain_vec, bias_vec):
    row_mean = lax.optimization_barrier(jnp.mean(hidden, axis=-1, keepdims=True))
    centered = hidden - row_mean
    variance = lax.optimization_barrier(jnp.mean(centered * centered, axis=-1, keepdims=True))
    return centered * lax.rsqrt(variance + 1e-06) * gain_vec + bias_vec

def block_layer(hidden, key_valid, weights):
    w_in, w_out, w_one, w_two, vector_all = weights
    ln1_gain = vector_all[0:D]
    ln1_bias = vector_all[D:2 * D]
    q_bias = vector_all[2 * D:3 * D]
    v_bias = vector_all[3 * D:4 * D]
    out_bias = vector_all[4 * D:5 * D]
    ln2_gain = vector_all[5 * D:6 * D]
    ln2_bias = vector_all[6 * D:7 * D]
    two_bias = vector_all[7 * D:8 * D]
    one_bias = vector_all[8 * D:]
    group_count, seq_len, model_width = hidden.shape
    flat_rows = hidden.reshape(group_count * seq_len, model_width)
    normed = low(layer_norm(flat_rows, ln1_gain, ln1_bias))
    projected = matmul(normed, w_in)
    queries = low_back(low(projected[:, 0:D] + q_bias)).reshape(group_count, seq_len, HEADS, HD)
    key_rows = low_back(low(projected[:, D:2 * D])).reshape(group_count, seq_len, HEADS, HD)
    values = low_back(low(projected[:, 2 * D:3 * D] + v_bias)).reshape(group_count, seq_len, HEADS, HD)
    scores = jnp.einsum('gqhd,gkhd->ghqk', queries, key_rows, precision=lax.Precision.HIGHEST) * (1.0 / math.sqrt(HD))
    scores = low_back(scores)
    scores = jnp.where(key_valid[:, None, None, :], scores, masked_fill)
    softmax_weights = jax.nn.softmax(scores, axis=-1)
    context = jnp.einsum('ghqk,gkhd->gqhd', low(softmax_weights), values, precision=lax.Precision.HIGHEST)
    context = low_back(low(context.reshape(group_count * seq_len, model_width)))
    branch_one = low_back(matmul(context, w_out) + out_bias)
    mid_stream = flat_rows + branch_one
    normed_two = low(layer_norm(mid_stream, ln2_gain, ln2_bias))
    pre_gelu = low_back(matmul(normed_two, w_one) + one_bias)
    activation = low(jax.nn.gelu(pre_gelu, approximate=False))
    branch_two = low_back(matmul(activation, w_two) + two_bias)
    return (mid_stream + branch_two).reshape(group_count, seq_len, model_width)

def reference(tokens, ranges, attn_in, attn_out, mlp_in, mlp_out, vectors, cotangent):
    group_total = -(-IMAGES // group_images)
    padded_len = group_total * group_images * IMG_LEN
    position = jnp.arange(padded_len, dtype=jnp.int32)
    starts = ranges[:, 0].astype(jnp.int32)
    ends = ranges[:, 1].astype(jnp.int32)
    owner = lax.optimization_barrier(jnp.sum((position[:, None] >= ends[None, :]).astype(jnp.int32), axis=1))
    owner = jnp.minimum(owner, N_DEV - 1).astype(jnp.int32)
    inside = position < TOKENS
    slot_index = jnp.where(inside, owner * SLOTS + position - starts[owner], 0).astype(jnp.int32)

    def forward(tokens_full, in_weights, out_weights, one_weights, two_weights, vector_rows):
        packed = tokens_full[slot_index].reshape(group_total, group_images, IMG_LEN, D)
        valid = inside.reshape(group_total, group_images, IMG_LEN)

        def run_group(payload):
            hidden, key_valid = payload
            for layer_index in range(LAYERS):
                weights = (in_weights[layer_index].reshape(D, 3 * D), out_weights[layer_index].reshape(D, D), one_weights[layer_index].reshape(D, FF), two_weights[layer_index].reshape(FF, D), vector_rows[layer_index])
                hidden = block_layer(hidden, key_valid, weights)
            return hidden
        result = lax.map(jax.checkpoint(run_group), (packed, valid))
        result = result.reshape(padded_len, D)
        result = jnp.where(inside[:, None], result, 0.0)
        return jnp.zeros((N_DEV * SLOTS, D), jnp.float32).at[slot_index].add(result)
    output, pullback = jax.vjp(forward, tokens.astype(jnp.float32), attn_in.astype(jnp.float32), attn_out.astype(jnp.float32), mlp_in.astype(jnp.float32), mlp_out.astype(jnp.float32), vectors.astype(jnp.float32))
    grads = pullback(cotangent.astype(jnp.float32))
    return (output.astype(jnp.bfloat16), grads[0], grads[1], grads[2], grads[3], grads[4], grads[5])
```

```python
import functools
import math

import jax
import jax.numpy as jnp
from jax import lax
from jax.experimental import pallas as pl
from jax.experimental.pallas import tpu as pltpu
from jax.sharding import PartitionSpec as P

HD = 64
IMG_LEN = 197
ROWS = 208
IMAGES_HERE = 2
BLOCK = 16
MESH_ID = pl.DeviceIdType.MESH
bf16, f32 = jnp.bfloat16, jnp.float32
eps_norm = 1e-06
masked_fill = -1e30
vmem_bytes = 56 * 2**20


def mm(a, b):
    return jnp.dot(a, b, preferred_element_type=f32)


def mm_nt(a, b):
    return lax.dot_general(a, b, (((1,), (1,)), ((), ())), preferred_element_type=f32)


def mm_tn(a, b):
    return lax.dot_general(a, b, (((0,), (0,)), ((), ())), preferred_element_type=f32)


def norm_forward(x, gain, bias):
    centered = x - jnp.mean(x, axis=-1, keepdims=True)
    inverse = lax.rsqrt(jnp.mean(centered * centered, axis=-1, keepdims=True) + eps_norm)
    hat = centered * inverse
    return (hat * gain + bias).astype(bf16), hat, inverse


def norm_backward(dh, hat, inverse, gain):
    scaled = dh * gain
    dv = inverse * (
        scaled
        - jnp.mean(scaled, axis=-1, keepdims=True)
        - hat * jnp.mean(scaled * hat, axis=-1, keepdims=True)
    )
    return dv, rows_sum(dh * hat), rows_sum(dh)


def rows_sum(x):
    return jnp.sum(x, axis=0, keepdims=True)


WAYS = 3


def remote(src, dst, send, recv, dev):
    return pltpu.make_async_remote_copy(
        src_ref=src, dst_ref=dst, send_sem=send, recv_sem=recv,
        device_id=(dev,), device_id_type=MESH_ID,
    )


class Place:
    def __init__(self, n):
        self.n = n
        me = self.me = lax.axis_index("dev")
        self.bits = [lax.rem(lax.div(me, 2**b), 2) for b in range(5)]
        self.c, self.x, self.y = self.bits[:3]
        self.z = lax.div(me, 8)
        self.core = self.flip(0)
        self.along_z = [self.flip(3), self.flip(4), self.flip(3, 4)]
        self.along_xy = [self.flip(1), self.flip(2), self.flip(1, 2)]
        self.up, self.down = lax.rem(me + 1, n), lax.rem(me + n - 1, n)

    def flip(self, *which):
        return self.me + sum((1 - 2 * self.bits[b]) * 2**b for b in which)

    def peers(self):
        return [self.core] + self.along_z + self.along_xy + [self.up, self.down]


class Gather:
    def __init__(self, place, buf, send, recv):
        self.place, self.buf, self.send, self.recv = place, buf, send, recv
        self.sent = []

    def go(self, at, dev):
        k = len(self.sent)
        copy = remote(at, at, self.send.at[k], self.recv.at[k], dev)
        copy.start()
        self.sent.append(copy)

    def begin(self):
        p = self.place
        for dev in p.along_z:
            self.go(self.buf.at[p.z, p.y, p.x, p.c], dev)

    def middle(self):
        p = self.place
        for copy in self.sent[:WAYS]:
            copy.wait_recv()
        for dev in p.along_xy:
            self.go(self.buf.at[:, p.y, p.x, p.c], dev)

    def core(self):
        p = self.place
        for copy in self.sent[WAYS:2 * WAYS]:
            copy.wait_recv()
        self.go(self.buf.at[:, :, :, p.c], p.core)

    def done(self):
        self.sent[-1].wait_recv()


class Scatter:
    def __init__(self, place, grads, half, mid, ours, last, send, recv, out):
        self.place, self.grads, self.half, self.mid = place, grads, half, mid
        self.ours, self.last, self.send, self.recv, self.out = ours, last, send, recv, out
        self.out_xy, self.in_xy = mid
        self.out_z, self.in_z = last
        self.sent = []

    def go(self, src, dst, dev):
        k = len(self.sent)
        copy = remote(src, dst, self.send.at[k], self.recv.at[k], dev)
        copy.start()
        self.sent.append(copy)

    def begin(self):
        p = self.place
        self.go(self.grads.at[:, :, :, 1 - p.c], self.half, p.core)

    def middle(self):
        p = self.place
        self.sent[0].wait_recv()
        self.out_xy[...] = (
            self.grads[:, :, :, p.c].astype(f32) + self.half[...].astype(f32)
        ).astype(bf16)
        for k, (dy, dx) in enumerate(((0, 1), (1, 0), (1, 1))):
            y = 1 - p.y if dy else p.y
            x = 1 - p.x if dx else p.x
            self.go(self.out_xy.at[:, y, x], self.in_xy.at[k], p.along_xy[k])

    def end(self):
        p = self.place
        for copy in self.sent[1:1 + WAYS]:
            copy.wait_recv()
        total = self.grads[:, p.y, p.x, p.c].astype(f32) + self.half[:, p.y, p.x].astype(f32)
        for k in range(WAYS):
            total += self.in_xy[k].astype(f32)
        self.ours[...] = total
        self.out_z[...] = total.astype(bf16)
        for k, dev in enumerate(p.along_z):
            self.go(self.out_z.at[lax.div(dev, 8)], self.in_z.at[k], dev)

    def done(self):
        for copy in self.sent[1 + WAYS:]:
            copy.wait_recv()
        total = self.ours[self.place.z]
        for k in range(WAYS):
            total += self.in_z[k].astype(f32)
        self.out[...] = total


def natural(c):
    return jnp.where((c & 7) < 6, 6 * (c >> 3) + (c & 7), -1)


def iota(shape, dim):
    return lax.broadcasted_iota(jnp.int32, shape, dim)


def norm_padded(x, gain, bias, real, d):
    centered = (x - jnp.sum(x, axis=-1, keepdims=True) * (1.0 / d)) * real
    inverse = lax.rsqrt(jnp.sum(centered * centered, axis=-1, keepdims=True) * (1.0 / d) + eps_norm)
    hat = centered * inverse
    return (hat * gain + bias).astype(bf16), hat, inverse


def norm_padded_back(dh, hat, inverse, gain, d):
    scaled = dh * gain
    dv = inverse * (
        scaled
        - jnp.sum(scaled, axis=-1, keepdims=True) * (1.0 / d)
        - hat * (jnp.sum(scaled * hat, axis=-1, keepdims=True) * (1.0 / d))
    )
    return dv, rows_sum(dh * hat), rows_sum(dh)


def fused_kernel(n, layers, d, ranges, *refs):
    refs = list(refs)
    take = lambda count: [refs.pop(0) for _ in range(count)]
    tok, cot, a_in, a_out, m_in, m_out, vecs = take(7)
    red_i, red_m, red_o, act_out, dx_out = take(5)
    wire_i, wire_m, wire_o = take(3)
    grad_i, grad_m, grad_o = take(3)
    half_i, half_m, half_o = take(3)
    mid_i, mid_m, mid_o = take(3)
    inxy_i, inxy_m, inxy_o = take(3)
    ours_i, ours_m, ours_o = take(3)
    outz_i, outz_m, outz_o = take(3)
    inz_i, inz_m, inz_o = take(3)
    tok_up, cot_up, act_up, act_in, dx_up, dx_in = take(6)
    w_in_s, w_one_s, w_out_s, w_two_s = take(4)
    hat1_s, h1_s, qkv_s, p_s, o_s, hat2_s, h2_s, slope_s, a_s, inv_s = take(10)
    dqkv_s, do_s, stage, flat_ai, flat_ao, flat_mi, flat_mo, vec_s = take(8)
    gsend, grecv, ssend, srecv, hsend, hrecv = take(6)
    slots = tok.shape[1]
    heads = d // HD
    wide = 8 * n
    hidden_units = 4 * d
    rows = IMAGES_HERE * ROWS
    place = Place(n)
    me = place.me

    barrier = pltpu.get_barrier_semaphore()
    for other in place.peers():
        pl.semaphore_signal(barrier, inc=1, device_id=(other,), device_id_type=MESH_ID)

    lane = iota((1, wide), 1)
    real = jnp.where((lane & 7) < 6, 1.0, 0.0)
    ones_lane = jnp.where((lane & 7) == 6, 1.0, 0.0)
    spread = jnp.where(iota((d, wide), 0) == natural(iota((1, wide), 1)), 1.0, 0.0).astype(bf16)

    part = vecs.shape[1]
    vec_s[...] = jnp.zeros_like(vec_s)
    vec_s[0:layers, 0:part] = vecs[...].astype(f32)
    columns = 8 * d + hidden_units
    pick_vec = jnp.where(
        iota((vec_s.shape[1], columns), 0) == iota((1, columns), 1) - part * me, 1.0, 0.0
    ).astype(bf16)
    lines = mm(vec_s[...].astype(bf16), pick_vec)
    flat_ai[...] = a_in[...].astype(f32)
    flat_ao[...] = a_out[...].astype(f32)
    flat_mi[...] = m_in[...].astype(f32)
    flat_mo[...] = m_out[...].astype(f32)
    here = (place.z, place.y, place.x, place.c)
    big, small = stage
    for l in range(layers):
        row = slice(l, l + 1)
        small[...] = jnp.zeros_like(small)
        for r in range(6):
            small[r:r + 1, :] = flat_ao[row, r * d:(r + 1) * d]
        for r in range(24):
            small[8 + r:9 + r, :] = flat_mo[row, r * d:(r + 1) * d]
        for r, block in ((6, 4), (32, 0), (33, 1), (34, 5), (35, 6), (36, 7)):
            small[r:r + 1, :] = lines[row, block * d:(block + 1) * d]
        padded = mm(small[...].astype(bf16), spread)
        wire_o[(l,) + here] = padded[:32].astype(bf16)
        big[0] = jnp.zeros_like(big[0])
        big[1] = jnp.zeros_like(big[1])
        for r in range(6):
            big[0, r:r + 1, :] = flat_ai[row, r * 3 * d:r * 3 * d + 2 * d]
            big[0, 8 + r:9 + r, :d] = flat_ai[row, r * 3 * d + 2 * d:(r + 1) * 3 * d]
            big[1, r:r + 1, :] = flat_mi[row, r * 4 * d:r * 4 * d + 2 * d]
            big[1, 8 + r:9 + r, :] = flat_mi[row, r * 4 * d + 2 * d:(r + 1) * 4 * d]
        big[0, 6:7, :d] = lines[row, 2 * d:3 * d]
        big[0, 14:15, :d] = lines[row, 3 * d:4 * d]
        big[0, 7:8, :wide] = padded[32:33]
        big[0, 15:16, :wide] = padded[33:34]
        big[1, 6:7, :] = lines[row, 8 * d:10 * d]
        big[1, 14:15, :] = lines[row, 10 * d:12 * d]
        big[1, 7:8, :wide] = padded[34:35]
        big[1, 7:8, wide:] = padded[35:36, :2 * d - wide]
        big[1, 15:16, :2 * wide - 2 * d] = padded[35:36, 2 * d - wide:]
        big[1, 15:16, 2 * wide - 2 * d:] = padded[36:37]
        wire_i[(l,) + here] = big[0].astype(bf16)
        wire_m[(l,) + here] = big[1].astype(bf16)

    wires = (wire_i, wire_m, wire_o)
    gathers = [
        [Gather(place, wires[k].at[l], gsend.at[l, k], grecv.at[l, k]) for k in range(3)]
        for l in range(layers)
    ]
    scatters = [
        [
            Scatter(
                place, grads.at[l], half.at[l], (mid.at[l], inxy.at[l]), ours.at[l],
                (outz.at[l], inz.at[l]), ssend.at[l, k], srecv.at[l, k], red.at[l],
            )
            for k, (grads, half, mid, inxy, ours, outz, inz, red) in enumerate((
                (grad_i, half_i, mid_i, inxy_i, ours_i, outz_i, inz_i, red_i),
                (grad_m, half_m, mid_m, inxy_m, ours_m, outz_m, inz_m, red_m),
                (grad_o, half_o, mid_o, inxy_o, ours_o, outz_o, inz_o, red_o),
            ))
        ]
        for l in range(layers)
    ]
    halo = [
        remote(tok, tok_up, hsend.at[0], hrecv.at[0], place.down),
        remote(cot, cot_up, hsend.at[1], hrecv.at[1], place.down),
        remote(act_up, act_in, hsend.at[2], hrecv.at[2], place.up),
        remote(dx_up, dx_in, hsend.at[3], hrecv.at[3], place.up),
    ]
    (gi0, gm0, go0), (gi1, gm1, go1) = gathers
    (si0, sm0, so0), (si1, sm1, so1) = scatters

    pl.semaphore_wait(barrier, len(place.peers()))
    gi0.begin()
    halo[0].start()

    first, last = ranges[0, me], ranges[1, me]
    total = ranges[1, n - 1]
    image = (first + IMG_LEN - 1) // IMG_LEN
    picks, valid_keys = [], []
    for k in range(IMAGES_HERE):
        begin = (image + k) * IMG_LEN
        count = jnp.where(begin < last, jnp.minimum(IMG_LEN, total - begin), 0)
        r = iota((ROWS, 2 * slots), 0)
        c = iota((ROWS, 2 * slots), 1)
        t = begin + r
        column = jnp.where(t < last, t - first, t - last + slots)
        column = jnp.where(r < count, column, -1)
        picks.append(jnp.where(column == c, 1.0, 0.0).astype(bf16))
        valid_keys.append(iota((ROWS, ROWS), 1) < count)
    pick = jnp.concatenate(picks, axis=0)
    x = mm_nt(pick[:, :slots], mm_tn(spread, tok[...]).astype(bf16))

    gi0.middle()
    go0.begin()
    gm0.begin()
    halo[0].wait_recv()
    x += mm_nt(pick[:, slots:], mm_tn(spread, tok_up[...]).astype(bf16))
    gi0.core()
    go0.middle()
    gm0.middle()
    gi1.begin()
    halo[1].start()

    def unpack_in(l):
        v = wire_i[l].reshape(2 * n * 8, 2 * d).astype(f32).reshape(n, 2, 8, 2 * d)
        w_in_s[l, :, :2 * d] = v[:, 0].reshape(wide, 2 * d).astype(bf16)
        w_in_s[l, :, 2 * d:] = v[:, 1].reshape(wide, 2 * d).astype(bf16)
        s = jnp.sum(v, axis=0)
        return s[0, 7:8, :wide], s[1, 7:8, :wide] + ones_lane

    def unpack_one(l):
        v = wire_m[l].reshape(2 * n * 8, 2 * d).astype(f32).reshape(n, 2, 8, 2 * d)
        w_one_s[l, :, :2 * d] = v[:, 0].reshape(wide, 2 * d).astype(bf16)
        w_one_s[l, :, 2 * d:] = v[:, 1].reshape(wide, 2 * d).astype(bf16)
        s = jnp.sum(v, axis=0)
        bias = jnp.concatenate([s[0, 7:8, wide:], s[1, 7:8, :2 * wide - 2 * d]], axis=1)
        return s[0, 7:8, :wide], bias + ones_lane, s[1, 7:8, 2 * wide - 2 * d:]

    def unpack_out(l):
        v = wire_o[l].reshape(4 * n * 8, wide).astype(f32).reshape(n, 4, 8, wide)
        w_out_s[l] = mm(spread, v[:, 0].reshape(wide, wide).astype(bf16)).astype(bf16)
        w_two_s[l] = v[:, 1:].reshape(hidden_units, wide).astype(bf16)
        return jnp.sum(v[:, 0], axis=0)[6:7, :]

    gain1, gain2 = [None] * layers, [None] * layers
    beats = [
        [lambda: (go0.core(), gi1.middle()), lambda: (gm0.core(), go1.begin(), gm1.begin()),
         lambda: gi1.core(), lambda: (go1.middle(), gm1.middle())],
        [lambda: go1.core(), lambda: gm1.core(), lambda: None, lambda: None],
    ]
    for l in range(layers):
        gi, gm, go = gathers[l]
        gi.done()
        gain1[l], bias = unpack_in(l)
        h, hat, inv = norm_padded(x, gain1[l], bias, real, d)
        hat1_s[l], h1_s[l], inv_s[l, 0] = hat, h, inv
        projected = mm(h, w_in_s[l, :, :3 * d])
        qkv_s[l, :, :d] = (projected[:, :d].astype(bf16).astype(f32)
                           * (1.0 / math.sqrt(HD))).astype(bf16)
        qkv_s[l, :, d:] = projected[:, d:].astype(bf16)
        beats[l][0]()
        for i in range(IMAGES_HERE):
            at = slice(i * ROWS, (i + 1) * ROWS)
            for head in range(heads):
                q = qkv_s[l, at, head * HD:(head + 1) * HD]
                key = qkv_s[l, at, d + head * HD:d + (head + 1) * HD]
                val = qkv_s[l, at, 2 * d + head * HD:2 * d + (head + 1) * HD]
                scores = jnp.where(valid_keys[i], mm_nt(q, key), masked_fill)
                e = jnp.exp(scores - jnp.max(scores, axis=-1, keepdims=True))
                p = e * (1.0 / jnp.sum(e, axis=-1, keepdims=True))
                p_s[l, i, head] = p
                o_s[l, at, head * HD:(head + 1) * HD] = mm(p.astype(bf16), val).astype(bf16)
            beats[l][1 + i]()
        go.done()
        b_out = unpack_out(l)
        x1 = x + (mm(o_s[l], w_out_s[l]) + b_out)
        gm.done()
        gain2[l], bias, b_two = unpack_one(l)
        h2, hat, inv = norm_padded(x1, gain2[l], bias, real, d)
        hat2_s[l], h2_s[l], inv_s[l, 1] = hat, h2, inv
        u = mm(h2, w_one_s[l])
        beats[l][3]()
        phi = 0.5 * (1.0 + lax.erf(u * (1.0 / math.sqrt(2.0))))
        a_s[l] = (u * phi).astype(bf16)
        slope_s[l] = phi + u * (jnp.exp(-0.5 * u * u) * (1.0 / math.sqrt(2.0 * math.pi)))
        x = x1 + (mm(a_s[l], w_two_s[l]) + b_two)

    x_low = mm_nt(x.astype(bf16), spread).astype(bf16)
    act_up[...] = mm_tn(x_low, pick[:, slots:]).astype(bf16)
    halo[2].start()
    act_own = mm_tn(x_low, pick[:, :slots]).astype(bf16)

    halo[1].wait_recv()
    dx = mm_nt(pick[:, :slots], mm_tn(spread, cot[...]).astype(bf16))
    dx += mm_nt(pick[:, slots:], mm_tn(spread, cot_up[...]).astype(bf16))

    row_of = iota((wide, 1), 0) & 7

    def fold(a, b):
        v = jnp.concatenate([a.reshape(n, 1, 8, 2 * d), b.reshape(n, 1, 8, 2 * d)], axis=1)
        return v.reshape(2 * n * 8, 2 * d).astype(bf16).reshape(4, 2, 2, 2, BLOCK, 2 * d)

    beats = [
        [lambda: (so1.end(), si1.middle()), lambda: (si1.end(), so1.done()),
         lambda: (sm0.middle(), si1.done()), lambda: so0.middle(), lambda: sm0.end()],
        [lambda: None, lambda: None, lambda: sm1.middle(), lambda: so1.middle(), lambda: (sm1.end())],
    ]
    spare = jnp.zeros((rows, d), bf16)
    for l in reversed(range(layers)):
        si, sm, so = scatters[l]
        dm = dx.astype(bf16)
        g_b2 = rows_sum(dm.astype(f32))
        du = (mm_nt(dm, w_two_s[l]) * slope_s[l]).astype(bf16)
        beats[l][0]()
        g_one = mm_tn(h2_s[l], du)
        dh2 = mm_nt(du, w_one_s[l])
        dv, g_g2, g_c2 = norm_padded_back(dh2, hat2_s[l], inv_s[l, 1], gain2[l], d)
        line = jnp.concatenate([g_g2, g_c2, g_b2], axis=1)
        g_one = jnp.where(row_of == 7, line, g_one)
        grad_m[l] = fold(g_one[:, :2 * d], g_one[:, 2 * d:])
        sm.begin()
        dx1 = dx + dv
        db = dx1.astype(bf16)
        g_bo = rows_sum(db.astype(f32))
        do_s[...] = mm_nt(db, w_out_s[l]).astype(bf16)
        beats[l][1]()
        g_two = mm_tn(a_s[l], dm)
        g_out = mm_tn(spread, mm_tn(o_s[l], db).astype(bf16))
        g_out = jnp.where(row_of == 6, g_bo, g_out)
        v = jnp.concatenate([g_out.reshape(n, 1, 8, wide), g_two.reshape(n, 3, 8, wide)], axis=1)
        grad_o[l] = v.reshape(4 * n * 8, wide).astype(bf16).reshape(4, 2, 2, 2, 2 * BLOCK, wide)
        so.begin()
        beats[l][2]()
        dqkv_s[:, 3 * d:] = spare
        for i in range(IMAGES_HERE):
            at = slice(i * ROWS, (i + 1) * ROWS)
            for head in range(heads):
                q_at = slice(head * HD, (head + 1) * HD)
                k_at = slice(d + head * HD, d + (head + 1) * HD)
                v_at = slice(2 * d + head * HD, 2 * d + (head + 1) * HD)
                do = do_s[at, q_at]
                p = p_s[l, i, head]
                dp = mm_nt(do, qkv_s[l, at, v_at])
                ds = (p * (dp - jnp.sum(p * dp, axis=-1, keepdims=True))).astype(bf16)
                dqkv_s[at, q_at] = (mm(ds, qkv_s[l, at, k_at]) * (1.0 / math.sqrt(HD))).astype(bf16)
                dqkv_s[at, k_at] = mm_tn(ds, qkv_s[l, at, q_at]).astype(bf16)
                dqkv_s[at, v_at] = mm_tn(p.astype(bf16), do).astype(bf16)
            beats[l][3 + i]()
        dh = mm_nt(dqkv_s[...], w_in_s[l])
        dv, g_g1, g_c1 = norm_padded_back(dh, hat1_s[l], inv_s[l, 0], gain1[l], d)
        g_in = mm_tn(h1_s[l], dqkv_s[...])
        blank = jnp.zeros((1, 2 * d - wide), f32)
        line = jnp.concatenate([g_g1, blank, g_c1, blank], axis=1)
        g_in = jnp.where(row_of == 7, line, g_in)
        grad_i[l] = fold(g_in[:, :2 * d], g_in[:, 2 * d:])
        si.begin()
        dx = dx1 + dv

    high = dx.astype(bf16)
    low = (dx - high.astype(f32)).astype(bf16)
    high = mm_nt(high, spread).astype(bf16)
    low = mm_nt(low, spread).astype(bf16)
    dx_up[...] = mm_tn(high, pick[:, slots:]).astype(bf16)
    halo[3].start()
    so0.end()
    si0.middle()
    sm0.done()
    dx_own = mm_tn(high, pick[:, :slots]) + mm_tn(low, pick[:, :slots])
    sm1.done()
    so0.done()
    si0.end()
    halo[2].wait_recv()
    act_out[...] = act_own + act_in[...]
    halo[3].wait_recv()
    dx_out[...] = dx_own + dx_in[...].astype(f32)
    si0.done()
    for copy in halo:
        copy.wait_send()
    for group in gathers + scatters:
        for each in group:
            for copy in each.sent:
                copy.wait_send()


def fused(n, ranges, tok, cot, flats):
    d, slots = tok.shape
    layers = flats[0].shape[0]
    wide = 8 * n
    hidden_units = 4 * d
    rows = IMAGES_HERE * ROWS
    shapes = ((BLOCK, 2 * d), (BLOCK, 2 * d), (2 * BLOCK, wide))
    boxes = lambda lead, kind: [pltpu.VMEM((layers,) + lead + s, kind) for s in shapes]
    vm = pl.BlockSpec(memory_space=pltpu.VMEM)
    scratch = (
        boxes((4, 2, 2, 2), bf16) + boxes((4, 2, 2, 2), bf16)
        + boxes((4, 2, 2), bf16) + boxes((4, 2, 2), bf16) + boxes((WAYS, 4), bf16)
        + boxes((4,), f32) + boxes((4,), bf16) + boxes((WAYS,), bf16)
        + [pltpu.VMEM((d, slots), bf16)] * 6
        + [
            pltpu.VMEM((layers, wide, 4 * d), bf16),
            pltpu.VMEM((layers, wide, hidden_units), bf16),
            pltpu.VMEM((layers, d, wide), bf16),
            pltpu.VMEM((layers, hidden_units, wide), bf16),
            pltpu.VMEM((layers, rows, wide), f32),
            pltpu.VMEM((layers, rows, wide), bf16),
            pltpu.VMEM((layers, rows, 3 * d), bf16),
            pltpu.VMEM((layers, IMAGES_HERE, d // HD, ROWS, ROWS), f32),
            pltpu.VMEM((layers, rows, d), bf16),
            pltpu.VMEM((layers, rows, wide), f32),
            pltpu.VMEM((layers, rows, wide), bf16),
            pltpu.VMEM((layers, rows, hidden_units), f32),
            pltpu.VMEM((layers, rows, hidden_units), bf16),
            pltpu.VMEM((layers, 2, rows, 1), f32),
            pltpu.VMEM((rows, 4 * d), bf16),
            pltpu.VMEM((rows, d), bf16),
            (pltpu.VMEM((2, BLOCK, 2 * d), f32), pltpu.VMEM((3 * BLOCK, d), f32)),
        ]
        + [pltpu.VMEM(f.shape, f32) for f in flats[:4]]
        + [pltpu.VMEM((BLOCK, 128), f32)]
        + [pltpu.SemaphoreType.DMA((layers, 3, 2 * WAYS + 1))] * 4
        + [pltpu.SemaphoreType.DMA((4,))] * 2
    )
    return pl.pallas_call(
        functools.partial(fused_kernel, n, layers, d),
        out_shape=tuple(jax.ShapeDtypeStruct((layers,) + s, f32) for s in shapes)
        + (jax.ShapeDtypeStruct((d, slots), bf16), jax.ShapeDtypeStruct((d, slots), f32)),
        in_specs=[pl.BlockSpec(memory_space=pltpu.SMEM)] + [vm] * 7,
        out_specs=(vm,) * 5,
        scratch_shapes=scratch,
        compiler_params=pltpu.CompilerParams(
            collective_id=0, has_side_effects=True, vmem_limit_bytes=vmem_bytes
        ),
        name="two_layers",
    )(ranges.T, tok, cot, *flats)


def split_mm_nt(a, b):
    high = a.astype(bf16)
    low = (a - high.astype(f32)).astype(bf16)
    return mm_nt(high, b) + mm_nt(low, b)


def flatten_kernel(n, layers, d, red_i, red_m, red_o, act_in, dx_in, act, dx, g_in, g_out, g_one, g_two, g_vec, line_s, out_s):
    me = lax.axis_index("dev")
    wide = 8 * n
    act[...] = act_in[...]
    dx[...] = dx_in[...]
    spread = jnp.where(iota((d, wide), 0) == natural(iota((1, wide), 1)), 1.0, 0.0).astype(bf16)
    line_s[...] = jnp.zeros_like(line_s)
    for l in range(layers):
        row = slice(l, l + 1)
        for r in range(6):
            g_in[row, r * 3 * d:r * 3 * d + 2 * d] = red_i[l, r:r + 1, :]
            g_in[row, r * 3 * d + 2 * d:(r + 1) * 3 * d] = red_i[l, 8 + r:9 + r, :d]
            g_one[row, r * 4 * d:r * 4 * d + 2 * d] = red_m[l, r:r + 1, :]
            g_one[row, r * 4 * d + 2 * d:(r + 1) * 4 * d] = red_m[l, 8 + r:9 + r, :]
        out_s[...] = split_mm_nt(red_o[l], spread)
        for r in range(6):
            g_out[row, r * d:(r + 1) * d] = out_s[r:r + 1, :]
        for r in range(24):
            g_two[row, r * d:(r + 1) * d] = out_s[8 + r:9 + r, :]
        line_s[row, 0:256] = red_i[l, 7:8, :wide]
        line_s[row, 256:512] = red_i[l, 15:16, :wide]
        line_s[row, 512:768] = red_o[l, 6:7, :]
        line_s[row, 768:1152] = red_m[l, 7:8, :]
        line_s[row, 1152:1536] = red_m[l, 15:16, :]
        line_s[row, 1536:1920] = red_m[l, 6:7, :]
        line_s[row, 1920:2304] = red_m[l, 14:15, :]
        line_s[row, 2304:2304 + d] = red_i[l, 6:7, :d]
        line_s[row, 2560:2560 + d] = red_i[l, 14:15, :d]
    part = g_vec.shape[1]
    total = line_s.shape[1]
    c = iota((1, total), 1)
    goal = jnp.full((1, total), -1, jnp.int32)
    for start, block in ((0, 0), (256, 1), (512, 4), (768, 5), (1024, 6), (1280, 7)):
        inside = (c >= start) & (c < start + wide)
        own = natural(c - start)
        goal = jnp.where(inside & (own >= 0), block * d + own, goal)
    goal = jnp.where((c >= 1536) & (c < 1536 + 4 * d), c - 1536 + 8 * d, goal)
    goal = jnp.where((c >= 2304) & (c < 2304 + d), c - 2304 + 2 * d, goal)
    goal = jnp.where((c >= 2560) & (c < 2560 + d), c - 2560 + 3 * d, goal)
    choose = jnp.where(iota((128, total), 0) == goal - part * me, 1.0, 0.0).astype(bf16)
    g_vec[...] = split_mm_nt(line_s[...], choose)[0:layers, 0:part]


def local_fused(tokens, ranges, attn_in, attn_out, mlp_in, mlp_out, vectors, cotangent):
    n = lax.axis_size("dev")
    slots, d = tokens.shape
    layers, part = vectors.shape
    flats = (attn_in, attn_out, mlp_in, mlp_out, vectors)
    sums = fused(n, ranges, tokens.T, cotangent.T, flats)
    vm = pl.BlockSpec(memory_space=pltpu.VMEM)
    act, dx, *grads = pl.pallas_call(
        functools.partial(flatten_kernel, n, layers, d),
        out_shape=(
            jax.ShapeDtypeStruct((d, slots), bf16), jax.ShapeDtypeStruct((d, slots), f32),
        ) + tuple(jax.ShapeDtypeStruct(f.shape, f32) for f in flats),
        in_specs=[vm] * 5,
        out_specs=(vm,) * 7,
        scratch_shapes=[pltpu.VMEM((BLOCK, 2816), f32), pltpu.VMEM((2 * BLOCK, d), f32)],
        compiler_params=pltpu.CompilerParams(vmem_limit_bytes=vmem_bytes),
        name="flatten",
    )(*sums)
    return (act.T, dx.T, *grads)


def compute_kernel(n, layers, width, hidden_units, ranges, *refs):
    refs = list(refs)
    take = lambda count: [refs.pop(0) for _ in range(count)]
    (w_full,) = take(1)
    tok, cot, tok_up, cot_up = take(4)
    (grad_out,) = take(1)
    act_own, act_up, dx_own, dx_up = take(4)
    w_all, w_one_s, w_two_s, hat1_s, h1_s, qkv_s, p_s, o_s, hat2_s, h2_s, slope_s, a_s = take(12)
    inv_s, dqkv_s, do_s, grad_s, perm = take(5)
    slots = tok.shape[1]
    heads = width // HD
    d = width
    me = lax.axis_index("dev")
    first, last = ranges[me, 0], ranges[me, 1]
    total = ranges[n - 1, 1]
    image = (first + IMG_LEN - 1) // IMG_LEN
    rows = IMAGES_HERE * ROWS

    picks, valid_keys = [], []
    for k in range(IMAGES_HERE):
        begin = (image + k) * IMG_LEN
        count = jnp.where(begin < last, jnp.minimum(IMG_LEN, total - begin), 0)
        r = lax.broadcasted_iota(jnp.int32, (ROWS, 2 * slots), 0)
        c = lax.broadcasted_iota(jnp.int32, (ROWS, 2 * slots), 1)
        t = begin + r
        column = jnp.where(t < last, t - first, t - last + slots)
        column = jnp.where(r < count, column, -1)
        picks.append(jnp.where(column == c, 1.0, 0.0).astype(bf16))
        valid_keys.append(lax.broadcasted_iota(jnp.int32, (ROWS, ROWS), 1) < count)
    pick = jnp.concatenate(picks, axis=0)
    x = mm_nt(pick[:, :slots], tok[...]) + mm_nt(pick[:, slots:], tok_up[...])

    unit = lax.broadcasted_iota(jnp.int32, (1, hidden_units), 1)
    group = sum(jnp.where(unit >= j * d, 1, 0) for j in range(1, 4))
    origin = 4 * (unit - group * d) + group
    f = lax.broadcasted_iota(jnp.int32, (hidden_units, hidden_units), 0)
    perm[...] = jnp.where(f == origin, 1.0, 0.0).astype(bf16)

    vec = [None] * layers
    b_one = [None] * layers
    for l in range(layers):
        w_all[l] = w_full[l]
        w_one_s[l] = mm(w_all[l, :d, 4 * d:8 * d], perm[...]).astype(bf16)
        for j in range(4):
            w_two_s[l, j * d:(j + 1) * d, :] = w_all[l, :d, (8 + j) * d:(9 + j) * d]
        tail = w_all[l, d:d + BLOCK, :]
        vec[l] = tail.astype(f32)[0:1, :]
        b_one[l] = mm(tail[:, 8 * d:], perm[...])[0:1, :]

    def v_of(l, index):
        return vec[l][:, index * d:(index + 1) * d]

    for l in range(layers):
        h, hat, inv = norm_forward(x, v_of(l, 0), v_of(l, 1))
        hat1_s[l], h1_s[l], inv_s[l, 0] = hat, h, inv
        projected = mm(h, w_all[l, :d, :3 * d])
        qkv_s[l, :, :d] = ((projected[:, :d] + v_of(l, 2)).astype(bf16).astype(f32)
                           * (1.0 / math.sqrt(HD))).astype(bf16)
        qkv_s[l, :, d:2 * d] = projected[:, d:2 * d].astype(bf16)
        qkv_s[l, :, 2 * d:] = (projected[:, 2 * d:] + v_of(l, 3)).astype(bf16)
        for i in range(IMAGES_HERE):
            at = slice(i * ROWS, (i + 1) * ROWS)
            for head in range(heads):
                q = qkv_s[l, at, head * HD:(head + 1) * HD]
                key = qkv_s[l, at, d + head * HD:d + (head + 1) * HD]
                val = qkv_s[l, at, 2 * d + head * HD:2 * d + (head + 1) * HD]
                scores = jnp.where(valid_keys[i], mm_nt(q, key), masked_fill)
                e = jnp.exp(scores - jnp.max(scores, axis=-1, keepdims=True))
                p = e * (1.0 / jnp.sum(e, axis=-1, keepdims=True))
                p_s[l, i, head] = p
                o_s[l, at, head * HD:(head + 1) * HD] = mm(p.astype(bf16), val).astype(bf16)
        x1 = x + (mm(o_s[l], w_all[l, :d, 3 * d:4 * d]) + v_of(l, 4))
        h2, hat, inv = norm_forward(x1, v_of(l, 5), v_of(l, 6))
        hat2_s[l], h2_s[l], inv_s[l, 1] = hat, h2, inv
        u = mm(h2, w_one_s[l]) + b_one[l]
        phi = 0.5 * (1.0 + lax.erf(u * (1.0 / math.sqrt(2.0))))
        a_s[l] = (u * phi).astype(bf16)
        slope_s[l] = phi + u * (jnp.exp(-0.5 * u * u) * (1.0 / math.sqrt(2.0 * math.pi)))
        x = x1 + (mm(a_s[l], w_two_s[l]) + v_of(l, 7))

    x_low = x.astype(bf16)
    act_own[...] = mm_tn(x_low, pick[:, :slots]).astype(bf16)
    act_up[...] = mm_tn(x_low, pick[:, slots:]).astype(bf16)

    dx = mm_nt(pick[:, :slots], cot[...]) + mm_nt(pick[:, slots:], cot_up[...])
    for l in reversed(range(layers)):
        dm = dx.astype(bf16)
        g_two = mm_tn(a_s[l], dm)
        for j in range(4):
            grad_s[l, :d, (8 + j) * d:(9 + j) * d] = g_two[j * d:(j + 1) * d, :].astype(bf16)
        g_b2 = rows_sum(dm.astype(f32))
        du = (mm_nt(dm, w_two_s[l]) * slope_s[l]).astype(bf16)
        g_b1 = mm_nt(jnp.broadcast_to(rows_sum(du.astype(f32)), (BLOCK, hidden_units)).astype(bf16),
                     perm[...])[0:1, :]
        g_one = mm_tn(h2_s[l], du).astype(bf16)
        grad_s[l, :d, 4 * d:8 * d] = mm_nt(g_one, perm[...]).astype(bf16)
        dh2 = mm_nt(du, w_one_s[l])
        dv, g_g2, g_c2 = norm_backward(dh2, hat2_s[l], inv_s[l, 1], v_of(l, 5))
        dx1 = dx + dv
        db = dx1.astype(bf16)
        g_bo = rows_sum(db.astype(f32))
        grad_s[l, :d, 3 * d:4 * d] = mm_tn(o_s[l], db).astype(bf16)
        do_s[...] = mm_nt(db, w_all[l, :d, 3 * d:4 * d]).astype(bf16)
        for i in range(IMAGES_HERE):
            at = slice(i * ROWS, (i + 1) * ROWS)
            for head in range(heads):
                q_at = slice(head * HD, (head + 1) * HD)
                k_at = slice(d + head * HD, d + (head + 1) * HD)
                v_at = slice(2 * d + head * HD, 2 * d + (head + 1) * HD)
                do = do_s[at, q_at]
                p = p_s[l, i, head]
                dp = mm_nt(do, qkv_s[l, at, v_at])
                ds = (p * (dp - jnp.sum(p * dp, axis=-1, keepdims=True))).astype(bf16)
                dqkv_s[at, q_at] = (mm(ds, qkv_s[l, at, k_at]) * (1.0 / math.sqrt(HD))).astype(bf16)
                dqkv_s[at, k_at] = mm_tn(ds, qkv_s[l, at, q_at]).astype(bf16)
                dqkv_s[at, v_at] = mm_tn(p.astype(bf16), do).astype(bf16)
        g_bq = rows_sum(dqkv_s[:, :d].astype(f32))
        g_bv = rows_sum(dqkv_s[:, 2 * d:].astype(f32))
        grad_s[l, :d, :3 * d] = mm_tn(h1_s[l], dqkv_s[...]).astype(bf16)
        dh = mm_nt(dqkv_s[...], w_all[l, :d, :3 * d])
        dv, g_g1, g_c1 = norm_backward(dh, hat1_s[l], inv_s[l, 0], v_of(l, 0))
        dx = dx1 + dv
        line = jnp.concatenate([g_g1, g_c1, g_bq, g_bv, g_bo, g_g2, g_c2, g_b2, g_b1], axis=1)
        grad_s[l, d:d + BLOCK, :] = jnp.broadcast_to(line, (BLOCK, line.shape[1])).astype(bf16)

    high = dx.astype(bf16)
    low = (dx - high.astype(f32)).astype(bf16)
    dx_own[...] = mm_tn(high, pick[:, :slots]) + mm_tn(low, pick[:, :slots])
    dx_up[...] = mm_tn(high, pick[:, slots:]).astype(bf16)
    grad_out[...] = grad_s[...]


def compute(n, ranges, weights, tok, cot, tok_up, cot_up, layers):
    d, slots = tok.shape
    hidden_units = 4 * d
    rows = IMAGES_HERE * ROWS
    tall = d + BLOCK
    wide = 12 * d
    args = list(weights) + [tok, cot, tok_up, cot_up]
    outs = [jax.ShapeDtypeStruct((layers, tall, wide), bf16)]
    outs += [
        jax.ShapeDtypeStruct((d, slots), kind) for kind in (bf16, bf16, f32, bf16)
    ]
    vm = pl.BlockSpec(memory_space=pltpu.VMEM)
    return pl.pallas_call(
        functools.partial(compute_kernel, n, layers, d, hidden_units),
        out_shape=tuple(outs),
        in_specs=[pl.BlockSpec(memory_space=pltpu.SMEM)] + [vm] * len(args),
        out_specs=(vm,) * len(outs),
        scratch_shapes=[
            pltpu.VMEM((layers, tall, wide), bf16),
            pltpu.VMEM((layers, d, hidden_units), bf16),
            pltpu.VMEM((layers, hidden_units, d), bf16),
            pltpu.VMEM((layers, rows, d), f32),
            pltpu.VMEM((layers, rows, d), bf16),
            pltpu.VMEM((layers, rows, 3 * d), bf16),
            pltpu.VMEM((layers, IMAGES_HERE, d // HD, ROWS, ROWS), f32),
            pltpu.VMEM((layers, rows, d), bf16),
            pltpu.VMEM((layers, rows, d), f32),
            pltpu.VMEM((layers, rows, d), bf16),
            pltpu.VMEM((layers, rows, hidden_units), f32),
            pltpu.VMEM((layers, rows, hidden_units), bf16),
            pltpu.VMEM((layers, 2, rows, 1), f32),
            pltpu.VMEM((rows, 3 * d), bf16),
            pltpu.VMEM((rows, d), bf16),
            pltpu.VMEM((layers, tall, wide), bf16),
            pltpu.VMEM((hidden_units, hidden_units), bf16),
        ],
        compiler_params=pltpu.CompilerParams(vmem_limit_bytes=vmem_bytes),
        name="two_layers",
    )(ranges, *args)


def rows_of(flats, d):
    w_in, w_out, w_one, w_two = flats
    layers = w_in.shape[0]
    return jnp.concatenate(
        [
            w_in.reshape(layers, -1, 3 * d),
            w_out.reshape(layers, -1, d),
            w_one.reshape(layers, -1, 4 * d),
            w_two.reshape(layers, -1, 4 * d),
        ],
        axis=2,
    )


def flats_of(block, d):
    layers = block.shape[0]
    ends = (0, 3 * d, 4 * d, 8 * d, 12 * d)
    return [block[:, :, lo:hi].reshape(layers, -1) for lo, hi in zip(ends, ends[1:])]


def local_other(tokens, ranges, attn_in, attn_out, mlp_in, mlp_out, vectors, cotangent):
    n = lax.axis_size("dev")
    slots, d = tokens.shape
    layers, part = vectors.shape
    tokens, cotangent = tokens.T, cotangent.T
    flats = (attn_in, attn_out, mlp_in, mlp_out)
    whole = [
        jnp.stack([lax.all_gather(flat[l], "dev", axis=0, tiled=True) for l in range(layers)])
        for flat in flats + (vectors,)
    ]
    line = whole.pop()
    spare = jnp.zeros((layers, BLOCK - 1, 12 * d), bf16)
    block = jnp.concatenate([rows_of(whole, d), line[:, None, :], spare], axis=1)
    down = [(i, (i + n - 1) % n) for i in range(n)]
    tok_up, cot_up = lax.ppermute(tokens, "dev", down), lax.ppermute(cotangent, "dev", down)
    grad, act, act_up, dx, dx_up = compute(
        n, ranges, (block,), tokens, cotangent, tok_up, cot_up, layers
    )
    up = [(i, (i + 1) % n) for i in range(n)]
    act = act + lax.ppermute(act_up, "dev", up)
    dx = dx + lax.ppermute(dx_up, "dev", up)
    terms = flats_of(grad[:, :d], d) + [grad[:, d]]
    grads = [
        jnp.stack([
            lax.psum_scatter(term[l].astype(f32), "dev", scatter_dimension=0, tiled=True)
            for l in range(layers)
        ])
        for term in terms
    ]
    return (act.T, dx.T, *grads)


def solution(mesh):
    flat = P(None, "dev")
    rows = P("dev", None)

    def local(*args):
        n = lax.axis_size("dev")
        slots, d = args[0].shape
        layers = args[2].shape[0]
        fast = n == 32 and d == 6 * n and layers == 2 and slots == 256
        return local_fused(*args) if fast else local_other(*args)

    return jax.shard_map(
        local,
        mesh=mesh,
        in_specs=(rows, P(), flat, flat, flat, flat, flat, rows),
        out_specs=(rows, rows, flat, flat, flat, flat, flat),
        check_vma=False,
    )
```

```python
import functools
import math

import jax
import jax.numpy as jnp
from jax import lax
from jax.experimental import pallas as pl
from jax.experimental.pallas import tpu as pltpu
from jax.sharding import PartitionSpec as P

HD = 64
IMG_LEN = 197
ROWS = 208
IMAGES_HERE = 2
BLOCK = 16
MESH_ID = pl.DeviceIdType.MESH
bf16, f32 = jnp.bfloat16, jnp.float32
eps_norm = 1e-06
masked_fill = -1e30
vmem_bytes = 56 * 2**20


def mm(a, b):
    return jnp.dot(a, b, preferred_element_type=f32)


def mm_nt(a, b):
    return lax.dot_general(a, b, (((1,), (1,)), ((), ())), preferred_element_type=f32)


def mm_tn(a, b):
    return lax.dot_general(a, b, (((0,), (0,)), ((), ())), preferred_element_type=f32)


def norm_forward(x, gain, bias):
    centered = x - jnp.mean(x, axis=-1, keepdims=True)
    inverse = lax.rsqrt(jnp.mean(centered * centered, axis=-1, keepdims=True) + eps_norm)
    hat = centered * inverse
    return (hat * gain + bias).astype(bf16), hat, inverse


def norm_backward(dh, hat, inverse, gain):
    scaled = dh * gain
    dv = inverse * (
        scaled
        - jnp.mean(scaled, axis=-1, keepdims=True)
        - hat * jnp.mean(scaled * hat, axis=-1, keepdims=True)
    )
    return dv, rows_sum(dh * hat), rows_sum(dh)


def rows_sum(x):
    return jnp.sum(x, axis=0, keepdims=True)


WAYS = 3


def remote(src, dst, send, recv, dev):
    return pltpu.make_async_remote_copy(
        src_ref=src, dst_ref=dst, send_sem=send, recv_sem=recv,
        device_id=(dev,), device_id_type=MESH_ID,
    )


class Place:
    def __init__(self, n):
        self.n = n
        me = self.me = lax.axis_index("dev")
        self.bits = [lax.rem(lax.div(me, 2**b), 2) for b in range(5)]
        self.c, self.x, self.y = self.bits[:3]
        self.z = lax.div(me, 8)
        self.core = self.flip(0)
        self.along_z = [self.flip(3), self.flip(4), self.flip(3, 4)]
        self.along_xy = [self.flip(1), self.flip(2), self.flip(1, 2)]
        self.chips = [self.flip(*[b + 1 for b in range(4) if m >> b & 1]) for m in range(1, 16)]
        self.up, self.down = lax.rem(me + 1, n), lax.rem(me + n - 1, n)

    def flip(self, *which):
        return self.me + sum((1 - 2 * self.bits[b]) * 2**b for b in which)

    def peers(self):
        return [self.core] + self.chips + [self.up, self.down]


class Gather:
    def __init__(self, place, buf, send, recv):
        self.place, self.buf, self.send, self.recv = place, buf, send, recv
        self.sent = []

    def go(self, at, dev):
        k = len(self.sent)
        copy = remote(at, at, self.send.at[k], self.recv.at[k], dev)
        copy.start()
        self.sent.append(copy)

    def begin(self):
        p = self.place
        for dev in p.along_z:
            self.go(self.buf.at[p.z, p.y, p.x, p.c], dev)

    def middle(self):
        p = self.place
        for copy in self.sent[:WAYS]:
            copy.wait_recv()
        for dev in p.along_xy:
            self.go(self.buf.at[:, p.y, p.x, p.c], dev)

    def core(self):
        p = self.place
        for copy in self.sent[WAYS:2 * WAYS]:
            copy.wait_recv()
        self.go(self.buf.at[:, :, :, p.c], p.core)

    def done(self):
        self.sent[-1].wait_recv()


class Scatter:
    def __init__(self, place, grads, half, mid, ours, last, send, recv, out):
        self.place, self.grads, self.half, self.mid = place, grads, half, mid
        self.ours, self.last, self.send, self.recv, self.out = ours, last, send, recv, out
        self.out_xy, self.in_xy = mid
        self.out_z, self.in_z = last
        self.sent = []

    def go(self, src, dst, dev):
        k = len(self.sent)
        copy = remote(src, dst, self.send.at[k], self.recv.at[k], dev)
        copy.start()
        self.sent.append(copy)

    def begin(self):
        p = self.place
        self.go(self.grads.at[:, :, :, 1 - p.c], self.half, p.core)

    def middle(self):
        p = self.place
        self.sent[0].wait_recv()
        self.out_xy[...] = (
            self.grads[:, :, :, p.c].astype(f32) + self.half[...].astype(f32)
        ).astype(bf16)
        for k, (dy, dx) in enumerate(((0, 1), (1, 0), (1, 1))):
            y = 1 - p.y if dy else p.y
            x = 1 - p.x if dx else p.x
            self.go(self.out_xy.at[:, y, x], self.in_xy.at[k], p.along_xy[k])

    def end(self):
        p = self.place
        for copy in self.sent[1:1 + WAYS]:
            copy.wait_recv()
        total = self.grads[:, p.y, p.x, p.c].astype(f32) + self.half[:, p.y, p.x].astype(f32)
        for k in range(WAYS):
            total += self.in_xy[k].astype(f32)
        self.ours[...] = total
        self.out_z[...] = total.astype(bf16)
        for k, dev in enumerate(p.along_z):
            self.go(self.out_z.at[lax.div(dev, 8)], self.in_z.at[k], dev)

    def done(self):
        for copy in self.sent[1 + WAYS:]:
            copy.wait_recv()
        total = self.ours[self.place.z]
        for k in range(WAYS):
            total += self.in_z[k].astype(f32)
        self.out[...] = total


class Direct(Scatter):
    def middle(self):
        p = self.place
        self.sent[0].wait_recv()
        self.out_xy[...] = (
            self.grads[:, :, :, p.c].astype(f32) + self.half[...].astype(f32)
        ).astype(bf16)
        for k, dev in enumerate(p.chips):
            at = (lax.div(dev, 8), lax.rem(lax.div(dev, 4), 2), lax.rem(lax.div(dev, 2), 2))
            self.go(self.out_xy.at[at], self.in_xy.at[k], dev)

    def done(self):
        p = self.place
        total = self.grads[p.z, p.y, p.x, p.c].astype(f32) + self.half[p.z, p.y, p.x].astype(f32)
        for k, copy in enumerate(self.sent[1:]):
            copy.wait_recv()
            total += self.in_xy[k].astype(f32)
        self.out[...] = total


def natural(c):
    return jnp.where((c & 7) < 6, 6 * (c >> 3) + (c & 7), -1)


def iota(shape, dim):
    return lax.broadcasted_iota(jnp.int32, shape, dim)


def norm_padded(x, gain, bias, real, d):
    centered = (x - jnp.sum(x, axis=-1, keepdims=True) * (1.0 / d)) * real
    inverse = lax.rsqrt(jnp.sum(centered * centered, axis=-1, keepdims=True) * (1.0 / d) + eps_norm)
    hat = centered * inverse
    return (hat * gain + bias).astype(bf16), hat, inverse


def norm_padded_back(dh, hat, inverse, gain, d):
    scaled = dh * gain
    dv = inverse * (
        scaled
        - jnp.sum(scaled, axis=-1, keepdims=True) * (1.0 / d)
        - hat * (jnp.sum(scaled * hat, axis=-1, keepdims=True) * (1.0 / d))
    )
    return dv, rows_sum(dh * hat), rows_sum(dh)


def sublanes(x, shift):
    return pltpu.roll(x, shift, 1)


def unfold(tiles, s):
    a, b, c = tiles
    return jnp.where(s < 2, sublanes(a, 2), jnp.where(s < 4, sublanes(b, 4), sublanes(c, 6)))


def fold(tiles, extra, s):
    return [jnp.where(s < 6, t, sublanes(extra, 6 - 2 * k)) for k, t in enumerate(tiles)]


def fused_kernel(n, layers, d, ranges, *refs):
    refs = list(refs)
    take = lambda count: [refs.pop(0) for _ in range(count)]
    tok, cot, a_in, a_out, m_in, m_out, vecs = take(7)
    reds, (act_out, dx_out) = take(3), take(2)
    wires, grads, halves, mids, inxys, ours, outzs, inzs = [take(3) for _ in range(8)]
    (in_direct,) = take(1)
    tok_up, cot_up, act_up, act_in, dx_up, dx_in = take(6)
    w_in_s, w_one_s, w_out_s, w_two_s, two_s = take(5)
    vec_n, vec_g, b_one_s, line_n, line_g = take(5)
    hat1_s, h1_s, qkv_s, p_s, o_s, hat2_s, h2_s, slope_s, a_s, inv_s = take(10)
    dqkv_s, do_s, pack_a, pack_b, pack_c, flat_ai, flat_ao, flat_mi, flat_mo, vec_s = take(10)
    gsend, grecv, ssend, srecv, hsend, hrecv = take(6)
    wire_a, wire_b, wire_c = wires
    slots = tok.shape[1]
    heads = d // HD
    wide = 8 * n
    hidden_units = 4 * d
    rows = IMAGES_HERE * ROWS
    place = Place(n)
    me = place.me

    barrier = pltpu.get_barrier_semaphore()
    for other in place.peers():
        pl.semaphore_signal(barrier, inc=1, device_id=(other,), device_id_type=MESH_ID)

    part = vecs.shape[1]
    here = (place.z, place.y, place.x, place.c)
    vec_s[...] = jnp.zeros_like(vec_s)
    vec_s[0:layers, 0:part] = vecs[...].astype(f32)
    moved = pltpu.roll(vec_s[...], 8 * lax.rem(me, 8), 1)
    vec_s[...] = moved
    flat_ai[...] = a_in[...].astype(f32)
    flat_mo[...] = m_out[...].astype(f32)
    pack_b[...] = jnp.zeros_like(pack_b)

    def pack_first(l):
        row = slice(l, l + 1)
        for r in range(6):
            base, k, i = r * 3 * d, r // 2, r % 2
            pack_a[r:r + 1, :] = flat_ai[row, base:base + 256]
            pack_a[8 + r:9 + r, :128] = flat_ai[row, base + 256:base + 384]
            low, lanes = 6 + i + (8 if k == 2 else 0), slice(128 * (k % 2), 128 * (k % 2) + 128)
            pack_a[low:low + 1, lanes] = flat_ai[row, base + 384:base + 512]
            pack_a[8 + r:9 + r, 128:192] = flat_ai[row, base + 512:base + 576]
        pack_a[14:15, 128:192] = vec_s[row, :64]
        pack_a[15:16, 128:192] = vec_s[row, 64:128]
        for r in range(8):
            pack_a[8 + r:9 + r, 192:] = flat_mo[row, (16 + r) * d + 128:(17 + r) * d]
        wire_a[(l,) + here] = pack_a[...].astype(bf16)

    def pack_second(l):
        row = slice(l, l + 1)
        for r in range(6):
            base, k, i = r * 4 * d, r // 2, r % 2
            lanes = slice(128 * k, 128 * k + 128)
            pack_b[r:r + 1, :] = flat_mi[row, base:base + 384]
            pack_b[6 + i:7 + i, lanes] = flat_mi[row, base + 384:base + 512]
            pack_b[8 + r:9 + r, :256] = flat_mi[row, base + 512:base + 768]
            pack_b[8 + r:9 + r, 256:] = flat_ao[row, r * d:r * d + 128]
            pack_b[14 + i:15 + i, 128 * k:128 * k + 64] = flat_ao[row, r * d + 128:(r + 1) * d]
        wire_b[(l,) + here] = pack_b[...].astype(bf16)

    def pack_third(l):
        row = slice(l, l + 1)
        for r in range(24):
            g, i = r // 8, r % 8
            low, lane = i + (8 if g == 2 else 0), 128 * (g % 2)
            pack_c[low:low + 1, lane:lane + 128] = flat_mo[row, r * d:r * d + 128]
            if g < 2:
                pack_c[8 + i:9 + i, 128 + 64 * g:192 + 64 * g] = flat_mo[row, r * d + 128:(r + 1) * d]
        wire_c[(l,) + here] = pack_c[...].astype(bf16)

    gathers = [
        [Gather(place, wires[k].at[l], gsend.at[l, k], grecv.at[l, k]) for k in range(3)]
        for l in range(layers)
    ]
    scatters = [
        [
            (Direct if k == 0 and l == 0 else Scatter)(
                place, grads[k].at[l], halves[k].at[l],
                (mids[k].at[l], in_direct if k == 0 and l == 0 else inxys[k].at[l]),
                ours[k].at[l], (outzs[k].at[l], inzs[k].at[l]), ssend.at[l, k], srecv.at[l, k], reds[k].at[l],
            )
            for k in range(3)
        ]
        for l in range(layers)
    ]
    halo = [
        remote(tok, tok_up, hsend.at[0], hrecv.at[0], place.down),
        remote(cot, cot_up, hsend.at[1], hrecv.at[1], place.down),
        remote(act_up, act_in, hsend.at[2], hrecv.at[2], place.up),
        remote(dx_up, dx_in, hsend.at[3], hrecv.at[3], place.up),
    ]
    (ga0, gb0, gc0), (ga1, gb1, gc1) = gathers
    (sa0, sb0, sc0), (sa1, sb1, sc1) = scatters

    pack_first(0)
    pl.semaphore_wait(barrier, len(place.peers()))
    ga0.begin()
    halo[0].start()
    flat_ao[...] = a_out[...].astype(f32)
    flat_mi[...] = m_in[...].astype(f32)
    pack_second(0)
    gb0.begin()
    pack_third(0)
    gc0.begin()
    pack_first(1)
    ga1.begin()
    pack_second(1)
    gb1.begin()
    pack_third(1)
    gc1.begin()

    lane = iota((1, wide), 1)
    real = jnp.where((lane & 7) < 6, 1.0, 0.0)
    spread = jnp.where(iota((d, wide), 0) == natural(iota((1, wide), 1)), 1.0, 0.0).astype(bf16)
    owner = lane >> 3
    window = jnp.where((lane & 7) >= 6, owner + (owner >> 3) + (lane & 1), -1)
    windows = [
        jnp.where(3 * iota((BLOCK, wide), 0) + k == window, 1.0, 0.0).astype(bf16) for k in range(3)
    ]
    sub = iota((1, 8, 1), 1)

    first, last = ranges[0, me], ranges[1, me]
    total = ranges[1, n - 1]
    image = (first + IMG_LEN - 1) // IMG_LEN
    picks, valid_keys = [], []
    for k in range(IMAGES_HERE):
        begin = (image + k) * IMG_LEN
        count = jnp.where(begin < last, jnp.minimum(IMG_LEN, total - begin), 0)
        r = iota((ROWS, 2 * slots), 0)
        c = iota((ROWS, 2 * slots), 1)
        t = begin + r
        column = jnp.where(t < last, t - first, t - last + slots)
        column = jnp.where(r < count, column, -1)
        picks.append(jnp.where(column == c, 1.0, 0.0).astype(bf16))
        valid_keys.append(iota((ROWS, ROWS), 1) < count)
    pick = jnp.concatenate(picks, axis=0)
    x = mm_nt(pick[:, :slots], mm_tn(spread, tok[...]).astype(bf16))

    ga0.middle()
    gb0.middle()
    halo[0].wait_recv()
    x += mm_nt(pick[:, slots:], mm_tn(spread, tok_up[...]).astype(bf16))
    gc0.middle()
    ga0.core()
    ga1.middle()

    def tiles_of(wire, l):
        v = wire[l]
        width = v.shape[-1]
        v = v.reshape(n * BLOCK, width).astype(f32).reshape(n, 2, 8, width)
        return [v[:, i, :, k:k + 128] for i in range(2) for k in range(0, width, 128)]

    def flat(t):
        return t.reshape(wide, t.shape[-1]).astype(bf16)

    def unpack_a(l):
        t0, t1, t2, t4 = tiles_of(wire_a, l)
        for k, t in enumerate((t0, t1, t2, unfold((t0, t1, t2), sub), t4)):
            w_in_s[l, :, 128 * k:128 * k + 128] = flat(t)
        t4 = flat(t4)
        lines = jnp.concatenate([mm(each, t4)[:, :64] for each in windows], axis=1)
        vec_n[l] = lines
        vec_g[l] = mm(lines.astype(bf16), spread)
        for k in range(4):
            b_one_s[l, 0:1, k * d:(k + 1) * d] = lines[8 + k:9 + k]

    def unpack_b(l):
        t0, t1, t2, t4, t5, t6 = tiles_of(wire_b, l)
        for k, t in enumerate((t0, t1, t2, unfold((t0, t1, t2), sub), t4, t5)):
            w_one_s[l, :, 128 * k:128 * k + 128] = flat(t)
        t7 = unfold((t4, t5, t6), sub)
        out = jnp.concatenate([flat(t6), flat(t7)], axis=1)
        out = mm(spread, out)[:, :d].astype(bf16)
        w_out_s[l] = mm(out, spread).astype(bf16)

    def unpack_c(l):
        t0, t1, t2, t3 = tiles_of(wire_c, l)
        last = tiles_of(wire_a, l)[3]
        side = pltpu.roll(t3, 64, 2), pltpu.roll(last, 64, 2)
        pile = lambda ts: jnp.stack(ts, axis=1).reshape(hidden_units, 128).astype(bf16)
        two_s[:, :128] = pile((t0, t1, t2))
        two_s[:, 128:] = pile((t3,) + side)
        w_two_s[l] = mm(two_s[:, :d], spread).astype(bf16)

    beats = [
        [lambda: gb0.core(), lambda: (gc0.core(), gb1.middle()), lambda: (ga1.core(), gc1.middle(), halo[1].start())],
        [lambda: gb1.core(), lambda: gc1.core(), lambda: None],
    ]
    for l in range(layers):
        ga, gb, gc = gathers[l]
        ga.done()
        unpack_a(l)
        h, hat, inv = norm_padded(x, vec_g[l, 0:1], vec_g[l, 1:2], real, d)
        hat1_s[l], h1_s[l], inv_s[l, 0] = hat, h, inv
        projected = mm(h, w_in_s[l, :, :3 * d])
        qkv_s[l, :, :d] = ((projected[:, :d] + vec_n[l, 2:3]).astype(bf16).astype(f32)
                           * (1.0 / math.sqrt(HD))).astype(bf16)
        qkv_s[l, :, d:2 * d] = projected[:, d:2 * d].astype(bf16)
        qkv_s[l, :, 2 * d:] = (projected[:, 2 * d:] + vec_n[l, 3:4]).astype(bf16)
        for i in range(IMAGES_HERE):
            at = slice(i * ROWS, (i + 1) * ROWS)
            for head in range(heads):
                q = qkv_s[l, at, head * HD:(head + 1) * HD]
                key = qkv_s[l, at, d + head * HD:d + (head + 1) * HD]
                val = qkv_s[l, at, 2 * d + head * HD:2 * d + (head + 1) * HD]
                scores = jnp.where(valid_keys[i], mm_nt(q, key), masked_fill)
                e = jnp.exp(scores - jnp.max(scores, axis=-1, keepdims=True))
                p = e * (1.0 / jnp.sum(e, axis=-1, keepdims=True))
                p_s[l, i, head] = p
                o_s[l, at, head * HD:(head + 1) * HD] = mm(p.astype(bf16), val).astype(bf16)
            beats[l][i]()
        gb.done()
        unpack_b(l)
        x1 = x + (mm(o_s[l], w_out_s[l]) + vec_g[l, 4:5])
        h2, hat, inv = norm_padded(x1, vec_g[l, 5:6], vec_g[l, 6:7], real, d)
        hat2_s[l], h2_s[l], inv_s[l, 1] = hat, h2, inv
        u = mm(h2, w_one_s[l]) + b_one_s[l, 0:1]
        phi = 0.5 * (1.0 + lax.erf(u * (1.0 / math.sqrt(2.0))))
        a_s[l] = (u * phi).astype(bf16)
        slope_s[l] = phi + u * (jnp.exp(-0.5 * u * u) * (1.0 / math.sqrt(2.0 * math.pi)))
        beats[l][2]()
        gc.done()
        unpack_c(l)
        x = x1 + (mm(a_s[l], w_two_s[l]) + vec_g[l, 7:8])

    x_low = mm_nt(x.astype(bf16), spread).astype(bf16)
    act_up[...] = mm_tn(x_low, pick[:, slots:]).astype(bf16)
    halo[2].start()
    act_own = mm_tn(x_low, pick[:, :slots]).astype(bf16)

    halo[1].wait_recv()
    dx = mm_nt(pick[:, :slots], mm_tn(spread, cot[...]).astype(bf16))
    dx += mm_nt(pick[:, slots:], mm_tn(spread, cot_up[...]).astype(bf16))

    def cut(w, pieces):
        return [w[:, 128 * k:128 * k + 128].reshape(n, 8, 128) for k in range(pieces)]

    def block(tiles):
        half = len(tiles) // 2
        v = [jnp.concatenate(tiles[i * half:(i + 1) * half], axis=-1)[:, None] for i in range(2)]
        v = jnp.concatenate(v, axis=1).reshape(n * BLOCK, 128 * half).astype(bf16)
        return v.reshape(4, 2, 2, 2, BLOCK, 128 * half)

    beats = [
        [lambda: (sa1.middle(), sb1.end()), lambda: (sc1.done(), sc0.middle()),
         lambda: (sa1.end(), sb1.done(), sb0.middle()), lambda: sc0.end()],
        [lambda: None, lambda: sc1.middle(), lambda: sb1.middle(), lambda: sc1.end()],
    ]
    dqkv_s[:, 3 * d:] = jnp.zeros((rows, d), bf16)
    low_lanes = iota((1, 1, 128), 2) < 64
    line_g[...] = jnp.zeros_like(line_g)
    line_n[...] = jnp.zeros_like(line_n)
    for l in reversed(range(layers)):
        sa, sb, sc = scatters[l]
        dm = dx.astype(bf16)
        line_g[7:8] = rows_sum(dm.astype(f32))
        g_two = mm_tn(a_s[l], mm_nt(dm, spread).astype(bf16)).reshape(n, 3, 8, d)
        side = jnp.concatenate([g_two[..., 128:], jnp.zeros((n, 3, 8, 256 - d), f32)], axis=-1)
        turned = pltpu.roll(side[:, 1], 64, 2)
        tail = pltpu.roll(side[:, 2], 64, 2)
        grads[2][l] = block([g_two[:, 0, :, :128], g_two[:, 1, :, :128], g_two[:, 2, :, :128],
                             jnp.where(low_lanes, side[:, 0], turned)])
        sc.begin()
        du = (mm_nt(dm, w_two_s[l]) * slope_s[l]).astype(bf16)
        beats[l][0]()
        g_b1 = rows_sum(du.astype(f32))
        for k in range(4):
            line_n[8 + k:9 + k] = g_b1[:, k * d:(k + 1) * d]
        dh2 = mm_nt(du, w_one_s[l])
        dv, g_g2, g_c2 = norm_padded_back(dh2, hat2_s[l], inv_s[l, 1], vec_g[l, 5:6], d)
        line_g[5:6], line_g[6:7] = g_g2, g_c2
        dx1 = dx + dv
        db = dx1.astype(bf16)
        line_g[4:5] = rows_sum(db.astype(f32))
        g_out = mm_tn(o_s[l], mm_nt(db, spread).astype(bf16))
        g_out = jnp.concatenate([g_out, jnp.zeros((d, 256 - d), f32)], axis=1).astype(bf16)
        t6, t7 = cut(mm_tn(spread, g_out), 2)
        t0, t1, t2, t3, t4, t5 = cut(mm_tn(h2_s[l], du), 6)
        grads[1][l] = block(fold((t0, t1, t2), t3, sub) + fold((t4, t5, t6), t7, sub))
        beats[l][1]()
        sb.begin()
        do_s[...] = mm_nt(db, w_out_s[l]).astype(bf16)
        for i in range(IMAGES_HERE):
            at = slice(i * ROWS, (i + 1) * ROWS)
            for head in range(heads):
                q_at = slice(head * HD, (head + 1) * HD)
                k_at = slice(d + head * HD, d + (head + 1) * HD)
                v_at = slice(2 * d + head * HD, 2 * d + (head + 1) * HD)
                do = do_s[at, q_at]
                p = p_s[l, i, head]
                dp = mm_nt(do, qkv_s[l, at, v_at])
                ds = (p * (dp - jnp.sum(p * dp, axis=-1, keepdims=True))).astype(bf16)
                dqkv_s[at, q_at] = (mm(ds, qkv_s[l, at, k_at]) * (1.0 / math.sqrt(HD))).astype(bf16)
                dqkv_s[at, k_at] = mm_tn(ds, qkv_s[l, at, q_at]).astype(bf16)
                dqkv_s[at, v_at] = mm_tn(p.astype(bf16), do).astype(bf16)
            beats[l][2 + i]()
        dqkv = dqkv_s[:, :640]
        line_n[2:3] = rows_sum(dqkv_s[:, :d].astype(f32))
        line_n[3:4] = rows_sum(dqkv_s[:, 2 * d:3 * d].astype(f32))
        dh = mm_nt(dqkv, w_in_s[l])
        dv, g_g1, g_c1 = norm_padded_back(dh, hat1_s[l], inv_s[l, 0], vec_g[l, 0:1], d)
        line_g[0:1], line_g[1:2] = g_g1, g_c1
        lines = (line_n[...] + mm_nt(line_g[...].astype(bf16), spread)).astype(bf16)
        vec_rows = sum(mm_tn(windows[k], lines[:, 64 * k:64 * k + 64]) for k in range(3))
        vec_rows = jnp.concatenate([vec_rows, jnp.zeros((wide, 64), f32)], axis=1).reshape(n, 8, 128)
        t0, t1, t2, t3, t4 = cut(mm_tn(h1_s[l], dqkv), 5)
        t4 = jnp.where(low_lanes, t4 + vec_rows, tail)
        grads[0][l] = block(fold((t0, t1, t2), t3, sub) + [t4])
        sa.begin()
        dx = dx1 + dv

    high = dx.astype(bf16)
    low = (dx - high.astype(f32)).astype(bf16)
    high = mm_nt(high, spread).astype(bf16)
    dx_up[...] = mm_tn(high, pick[:, slots:]).astype(bf16)
    halo[3].start()
    sa0.middle()
    sb0.end()
    low = mm_nt(low, spread).astype(bf16)
    dx_own = mm_tn(high, pick[:, :slots]) + mm_tn(low, pick[:, :slots])
    sa1.done()
    sc0.done()
    halo[2].wait_recv()
    act_out[...] = act_own + act_in[...]
    halo[3].wait_recv()
    dx_out[...] = dx_own + dx_in[...].astype(f32)
    sb0.done()
    sa0.done()
    for copy in halo:
        copy.wait_send()
    for group in gathers + scatters:
        for each in group:
            for copy in each.sent:
                copy.wait_send()


def fused(n, ranges, tok, cot, flats):
    d, slots = tok.shape
    layers = flats[0].shape[0]
    wide = 8 * n
    hidden_units = 4 * d
    rows = IMAGES_HERE * ROWS
    shapes = ((BLOCK, 256), (BLOCK, 384), (BLOCK, 256))
    boxes = lambda lead, kind: [pltpu.VMEM((layers,) + lead + s, kind) for s in shapes]
    vm = pl.BlockSpec(memory_space=pltpu.VMEM)
    scratch = (
        boxes((4, 2, 2, 2), bf16) + boxes((4, 2, 2, 2), bf16)
        + boxes((4, 2, 2), bf16) + boxes((4, 2, 2), bf16) + boxes((WAYS, 4), bf16)
        + boxes((4,), f32) + boxes((4,), bf16) + boxes((WAYS,), bf16)
        + [pltpu.VMEM((15,) + shapes[0], bf16)]
        + [pltpu.VMEM((d, slots), bf16)] * 6
        + [
            pltpu.VMEM((layers, wide, 640), bf16),
            pltpu.VMEM((layers, wide, hidden_units), bf16),
            pltpu.VMEM((layers, d, wide), bf16),
            pltpu.VMEM((layers, hidden_units, wide), bf16),
            pltpu.VMEM((hidden_units, 256), bf16),
            pltpu.VMEM((layers, BLOCK, d), f32),
            pltpu.VMEM((layers, BLOCK, wide), f32),
            pltpu.VMEM((layers, 8, hidden_units), f32),
            pltpu.VMEM((BLOCK, d), f32),
            pltpu.VMEM((BLOCK, wide), f32),
            pltpu.VMEM((layers, rows, wide), f32),
            pltpu.VMEM((layers, rows, wide), bf16),
            pltpu.VMEM((layers, rows, 3 * d), bf16),
            pltpu.VMEM((layers, IMAGES_HERE, d // HD, ROWS, ROWS), f32),
            pltpu.VMEM((layers, rows, d), bf16),
            pltpu.VMEM((layers, rows, wide), f32),
            pltpu.VMEM((layers, rows, wide), bf16),
            pltpu.VMEM((layers, rows, hidden_units), f32),
            pltpu.VMEM((layers, rows, hidden_units), bf16),
            pltpu.VMEM((layers, 2, rows, 1), f32),
            pltpu.VMEM((rows, 4 * d), bf16),
            pltpu.VMEM((rows, d), bf16),
        ]
        + [pltpu.VMEM(s, f32) for s in shapes]
        + [pltpu.VMEM(f.shape, f32) for f in flats[:4]]
        + [pltpu.VMEM((8, 128), f32)]
        + [pltpu.SemaphoreType.DMA((layers, 3, 16))] * 4
        + [pltpu.SemaphoreType.DMA((4,))] * 2
    )
    return pl.pallas_call(
        functools.partial(fused_kernel, n, layers, d),
        out_shape=tuple(jax.ShapeDtypeStruct((layers,) + s, f32) for s in shapes)
        + (jax.ShapeDtypeStruct((d, slots), bf16), jax.ShapeDtypeStruct((d, slots), f32)),
        in_specs=[pl.BlockSpec(memory_space=pltpu.SMEM)] + [vm] * 7,
        out_specs=(vm,) * 5,
        scratch_shapes=scratch,
        compiler_params=pltpu.CompilerParams(
            collective_id=0, has_side_effects=True, vmem_limit_bytes=vmem_bytes
        ),
        name="two_layers",
    )(ranges.T, tok, cot, *flats)


def flatten_kernel(n, layers, d, red_a, red_b, red_c, act_in, dx_in, act, dx, g_in, g_out, g_one, g_two, g_vec, vec_s):
    me = lax.axis_index("dev")
    act[...] = act_in[...]
    dx[...] = dx_in[...]
    vec_s[...] = jnp.zeros_like(vec_s)
    for l in range(layers):
        row = slice(l, l + 1)
        for r in range(6):
            k, i = r // 2, r % 2
            base = r * 3 * d
            g_in[row, base:base + 256] = red_a[l, r:r + 1, :]
            g_in[row, base + 256:base + 384] = red_a[l, 8 + r:9 + r, :128]
            low, lane = 6 + i + (8 if k == 2 else 0), 128 * (k % 2)
            g_in[row, base + 384:base + 512] = red_a[l, low:low + 1, lane:lane + 128]
            g_in[row, base + 512:base + 576] = red_a[l, 8 + r:9 + r, 128:192]
            base = r * 4 * d
            g_one[row, base:base + 384] = red_b[l, r:r + 1, :]
            g_one[row, base + 384:base + 512] = red_b[l, 6 + i:7 + i, 128 * k:128 * k + 128]
            g_one[row, base + 512:base + 768] = red_b[l, 8 + r:9 + r, :256]
            base = r * d
            g_out[row, base:base + 128] = red_b[l, 8 + r:9 + r, 256:]
            g_out[row, base + 128:base + 192] = red_b[l, 14 + i:15 + i, 128 * k:128 * k + 64]
        for r in range(24):
            g, i = r // 8, r % 8
            base, low, lane = r * d, i + (8 if g == 2 else 0), 128 * (g % 2)
            g_two[row, base:base + 128] = red_c[l, low:low + 1, lane:lane + 128]
            if g < 2:
                g_two[row, base + 128:base + 192] = red_c[l, 8 + i:9 + i, 128 + 64 * g:192 + 64 * g]
            else:
                g_two[row, base + 128:base + 192] = red_a[l, 8 + i:9 + i, 192:]
        vec_s[row, :64] = red_a[l, 14:15, 128:192]
        vec_s[row, 64:] = red_a[l, 15:16, 128:192]
    part = g_vec.shape[1]
    moved = pltpu.roll(vec_s[...], lax.rem(128 - 8 * lax.rem(me, 8), 128), 1)
    g_vec[...] = moved[0:layers, 0:part]


def local_fused(tokens, ranges, attn_in, attn_out, mlp_in, mlp_out, vectors, cotangent):
    n = lax.axis_size("dev")
    slots, d = tokens.shape
    layers, part = vectors.shape
    flats = (attn_in, attn_out, mlp_in, mlp_out, vectors)
    sums = fused(n, ranges, tokens.T, cotangent.T, flats)
    vm = pl.BlockSpec(memory_space=pltpu.VMEM)
    act, dx, *grads = pl.pallas_call(
        functools.partial(flatten_kernel, n, layers, d),
        out_shape=(
            jax.ShapeDtypeStruct((d, slots), bf16), jax.ShapeDtypeStruct((d, slots), f32),
        ) + tuple(jax.ShapeDtypeStruct(f.shape, f32) for f in flats),
        in_specs=[vm] * 5,
        out_specs=(vm,) * 7,
        scratch_shapes=[pltpu.VMEM((8, 128), f32)],
        compiler_params=pltpu.CompilerParams(vmem_limit_bytes=vmem_bytes),
        name="flatten",
    )(*sums)
    return (act.T, dx.T, *grads)


def compute_kernel(n, layers, width, hidden_units, ranges, *refs):
    refs = list(refs)
    take = lambda count: [refs.pop(0) for _ in range(count)]
    (w_full,) = take(1)
    tok, cot, tok_up, cot_up = take(4)
    (grad_out,) = take(1)
    act_own, act_up, dx_own, dx_up = take(4)
    w_all, w_one_s, w_two_s, hat1_s, h1_s, qkv_s, p_s, o_s, hat2_s, h2_s, slope_s, a_s = take(12)
    inv_s, dqkv_s, do_s, grad_s, perm = take(5)
    slots = tok.shape[1]
    heads = width // HD
    d = width
    me = lax.axis_index("dev")
    first, last = ranges[me, 0], ranges[me, 1]
    total = ranges[n - 1, 1]
    image = (first + IMG_LEN - 1) // IMG_LEN
    rows = IMAGES_HERE * ROWS

    picks, valid_keys = [], []
    for k in range(IMAGES_HERE):
        begin = (image + k) * IMG_LEN
        count = jnp.where(begin < last, jnp.minimum(IMG_LEN, total - begin), 0)
        r = lax.broadcasted_iota(jnp.int32, (ROWS, 2 * slots), 0)
        c = lax.broadcasted_iota(jnp.int32, (ROWS, 2 * slots), 1)
        t = begin + r
        column = jnp.where(t < last, t - first, t - last + slots)
        column = jnp.where(r < count, column, -1)
        picks.append(jnp.where(column == c, 1.0, 0.0).astype(bf16))
        valid_keys.append(lax.broadcasted_iota(jnp.int32, (ROWS, ROWS), 1) < count)
    pick = jnp.concatenate(picks, axis=0)
    x = mm_nt(pick[:, :slots], tok[...]) + mm_nt(pick[:, slots:], tok_up[...])

    unit = lax.broadcasted_iota(jnp.int32, (1, hidden_units), 1)
    group = sum(jnp.where(unit >= j * d, 1, 0) for j in range(1, 4))
    origin = 4 * (unit - group * d) + group
    f = lax.broadcasted_iota(jnp.int32, (hidden_units, hidden_units), 0)
    perm[...] = jnp.where(f == origin, 1.0, 0.0).astype(bf16)

    vec = [None] * layers
    b_one = [None] * layers
    for l in range(layers):
        w_all[l] = w_full[l]
        w_one_s[l] = mm(w_all[l, :d, 4 * d:8 * d], perm[...]).astype(bf16)
        for j in range(4):
            w_two_s[l, j * d:(j + 1) * d, :] = w_all[l, :d, (8 + j) * d:(9 + j) * d]
        tail = w_all[l, d:d + BLOCK, :]
        vec[l] = tail.astype(f32)[0:1, :]
        b_one[l] = mm(tail[:, 8 * d:], perm[...])[0:1, :]

    def v_of(l, index):
        return vec[l][:, index * d:(index + 1) * d]

    for l in range(layers):
        h, hat, inv = norm_forward(x, v_of(l, 0), v_of(l, 1))
        hat1_s[l], h1_s[l], inv_s[l, 0] = hat, h, inv
        projected = mm(h, w_all[l, :d, :3 * d])
        qkv_s[l, :, :d] = ((projected[:, :d] + v_of(l, 2)).astype(bf16).astype(f32)
                           * (1.0 / math.sqrt(HD))).astype(bf16)
        qkv_s[l, :, d:2 * d] = projected[:, d:2 * d].astype(bf16)
        qkv_s[l, :, 2 * d:] = (projected[:, 2 * d:] + v_of(l, 3)).astype(bf16)
        for i in range(IMAGES_HERE):
            at = slice(i * ROWS, (i + 1) * ROWS)
            for head in range(heads):
                q = qkv_s[l, at, head * HD:(head + 1) * HD]
                key = qkv_s[l, at, d + head * HD:d + (head + 1) * HD]
                val = qkv_s[l, at, 2 * d + head * HD:2 * d + (head + 1) * HD]
                scores = jnp.where(valid_keys[i], mm_nt(q, key), masked_fill)
                e = jnp.exp(scores - jnp.max(scores, axis=-1, keepdims=True))
                p = e * (1.0 / jnp.sum(e, axis=-1, keepdims=True))
                p_s[l, i, head] = p
                o_s[l, at, head * HD:(head + 1) * HD] = mm(p.astype(bf16), val).astype(bf16)
        x1 = x + (mm(o_s[l], w_all[l, :d, 3 * d:4 * d]) + v_of(l, 4))
        h2, hat, inv = norm_forward(x1, v_of(l, 5), v_of(l, 6))
        hat2_s[l], h2_s[l], inv_s[l, 1] = hat, h2, inv
        u = mm(h2, w_one_s[l]) + b_one[l]
        phi = 0.5 * (1.0 + lax.erf(u * (1.0 / math.sqrt(2.0))))
        a_s[l] = (u * phi).astype(bf16)
        slope_s[l] = phi + u * (jnp.exp(-0.5 * u * u) * (1.0 / math.sqrt(2.0 * math.pi)))
        x = x1 + (mm(a_s[l], w_two_s[l]) + v_of(l, 7))

    x_low = x.astype(bf16)
    act_own[...] = mm_tn(x_low, pick[:, :slots]).astype(bf16)
    act_up[...] = mm_tn(x_low, pick[:, slots:]).astype(bf16)

    dx = mm_nt(pick[:, :slots], cot[...]) + mm_nt(pick[:, slots:], cot_up[...])
    for l in reversed(range(layers)):
        dm = dx.astype(bf16)
        g_two = mm_tn(a_s[l], dm)
        for j in range(4):
            grad_s[l, :d, (8 + j) * d:(9 + j) * d] = g_two[j * d:(j + 1) * d, :].astype(bf16)
        g_b2 = rows_sum(dm.astype(f32))
        du = (mm_nt(dm, w_two_s[l]) * slope_s[l]).astype(bf16)
        g_b1 = mm_nt(jnp.broadcast_to(rows_sum(du.astype(f32)), (BLOCK, hidden_units)).astype(bf16),
                     perm[...])[0:1, :]
        g_one = mm_tn(h2_s[l], du).astype(bf16)
        grad_s[l, :d, 4 * d:8 * d] = mm_nt(g_one, perm[...]).astype(bf16)
        dh2 = mm_nt(du, w_one_s[l])
        dv, g_g2, g_c2 = norm_backward(dh2, hat2_s[l], inv_s[l, 1], v_of(l, 5))
        dx1 = dx + dv
        db = dx1.astype(bf16)
        g_bo = rows_sum(db.astype(f32))
        grad_s[l, :d, 3 * d:4 * d] = mm_tn(o_s[l], db).astype(bf16)
        do_s[...] = mm_nt(db, w_all[l, :d, 3 * d:4 * d]).astype(bf16)
        for i in range(IMAGES_HERE):
            at = slice(i * ROWS, (i + 1) * ROWS)
            for head in range(heads):
                q_at = slice(head * HD, (head + 1) * HD)
                k_at = slice(d + head * HD, d + (head + 1) * HD)
                v_at = slice(2 * d + head * HD, 2 * d + (head + 1) * HD)
                do = do_s[at, q_at]
                p = p_s[l, i, head]
                dp = mm_nt(do, qkv_s[l, at, v_at])
                ds = (p * (dp - jnp.sum(p * dp, axis=-1, keepdims=True))).astype(bf16)
                dqkv_s[at, q_at] = (mm(ds, qkv_s[l, at, k_at]) * (1.0 / math.sqrt(HD))).astype(bf16)
                dqkv_s[at, k_at] = mm_tn(ds, qkv_s[l, at, q_at]).astype(bf16)
                dqkv_s[at, v_at] = mm_tn(p.astype(bf16), do).astype(bf16)
        g_bq = rows_sum(dqkv_s[:, :d].astype(f32))
        g_bv = rows_sum(dqkv_s[:, 2 * d:].astype(f32))
        grad_s[l, :d, :3 * d] = mm_tn(h1_s[l], dqkv_s[...]).astype(bf16)
        dh = mm_nt(dqkv_s[...], w_all[l, :d, :3 * d])
        dv, g_g1, g_c1 = norm_backward(dh, hat1_s[l], inv_s[l, 0], v_of(l, 0))
        dx = dx1 + dv
        line = jnp.concatenate([g_g1, g_c1, g_bq, g_bv, g_bo, g_g2, g_c2, g_b2, g_b1], axis=1)
        grad_s[l, d:d + BLOCK, :] = jnp.broadcast_to(line, (BLOCK, line.shape[1])).astype(bf16)

    high = dx.astype(bf16)
    low = (dx - high.astype(f32)).astype(bf16)
    dx_own[...] = mm_tn(high, pick[:, :slots]) + mm_tn(low, pick[:, :slots])
    dx_up[...] = mm_tn(high, pick[:, slots:]).astype(bf16)
    grad_out[...] = grad_s[...]


def compute(n, ranges, weights, tok, cot, tok_up, cot_up, layers):
    d, slots = tok.shape
    hidden_units = 4 * d
    rows = IMAGES_HERE * ROWS
    tall = d + BLOCK
    wide = 12 * d
    args = list(weights) + [tok, cot, tok_up, cot_up]
    outs = [jax.ShapeDtypeStruct((layers, tall, wide), bf16)]
    outs += [
        jax.ShapeDtypeStruct((d, slots), kind) for kind in (bf16, bf16, f32, bf16)
    ]
    vm = pl.BlockSpec(memory_space=pltpu.VMEM)
    return pl.pallas_call(
        functools.partial(compute_kernel, n, layers, d, hidden_units),
        out_shape=tuple(outs),
        in_specs=[pl.BlockSpec(memory_space=pltpu.SMEM)] + [vm] * len(args),
        out_specs=(vm,) * len(outs),
        scratch_shapes=[
            pltpu.VMEM((layers, tall, wide), bf16),
            pltpu.VMEM((layers, d, hidden_units), bf16),
            pltpu.VMEM((layers, hidden_units, d), bf16),
            pltpu.VMEM((layers, rows, d), f32),
            pltpu.VMEM((layers, rows, d), bf16),
            pltpu.VMEM((layers, rows, 3 * d), bf16),
            pltpu.VMEM((layers, IMAGES_HERE, d // HD, ROWS, ROWS), f32),
            pltpu.VMEM((layers, rows, d), bf16),
            pltpu.VMEM((layers, rows, d), f32),
            pltpu.VMEM((layers, rows, d), bf16),
            pltpu.VMEM((layers, rows, hidden_units), f32),
            pltpu.VMEM((layers, rows, hidden_units), bf16),
            pltpu.VMEM((layers, 2, rows, 1), f32),
            pltpu.VMEM((rows, 3 * d), bf16),
            pltpu.VMEM((rows, d), bf16),
            pltpu.VMEM((layers, tall, wide), bf16),
            pltpu.VMEM((hidden_units, hidden_units), bf16),
        ],
        compiler_params=pltpu.CompilerParams(vmem_limit_bytes=vmem_bytes),
        name="two_layers",
    )(ranges, *args)


def rows_of(flats, d):
    w_in, w_out, w_one, w_two = flats
    layers = w_in.shape[0]
    return jnp.concatenate(
        [
            w_in.reshape(layers, -1, 3 * d),
            w_out.reshape(layers, -1, d),
            w_one.reshape(layers, -1, 4 * d),
            w_two.reshape(layers, -1, 4 * d),
        ],
        axis=2,
    )


def flats_of(block, d):
    layers = block.shape[0]
    ends = (0, 3 * d, 4 * d, 8 * d, 12 * d)
    return [block[:, :, lo:hi].reshape(layers, -1) for lo, hi in zip(ends, ends[1:])]


def local_other(tokens, ranges, attn_in, attn_out, mlp_in, mlp_out, vectors, cotangent):
    n = lax.axis_size("dev")
    slots, d = tokens.shape
    layers, part = vectors.shape
    tokens, cotangent = tokens.T, cotangent.T
    flats = (attn_in, attn_out, mlp_in, mlp_out)
    whole = [
        jnp.stack([lax.all_gather(flat[l], "dev", axis=0, tiled=True) for l in range(layers)])
        for flat in flats + (vectors,)
    ]
    line = whole.pop()
    spare = jnp.zeros((layers, BLOCK - 1, 12 * d), bf16)
    block = jnp.concatenate([rows_of(whole, d), line[:, None, :], spare], axis=1)
    down = [(i, (i + n - 1) % n) for i in range(n)]
    tok_up, cot_up = lax.ppermute(tokens, "dev", down), lax.ppermute(cotangent, "dev", down)
    grad, act, act_up, dx, dx_up = compute(
        n, ranges, (block,), tokens, cotangent, tok_up, cot_up, layers
    )
    up = [(i, (i + 1) % n) for i in range(n)]
    act = act + lax.ppermute(act_up, "dev", up)
    dx = dx + lax.ppermute(dx_up, "dev", up)
    terms = flats_of(grad[:, :d], d) + [grad[:, d]]
    grads = [
        jnp.stack([
            lax.psum_scatter(term[l].astype(f32), "dev", scatter_dimension=0, tiled=True)
            for l in range(layers)
        ])
        for term in terms
    ]
    return (act.T, dx.T, *grads)


def solution(mesh):
    flat = P(None, "dev")
    rows = P("dev", None)

    def local(*args):
        n = lax.axis_size("dev")
        slots, d = args[0].shape
        layers = args[2].shape[0]
        fast = n == 32 and d == 6 * n and layers == 2 and slots == 256
        return local_fused(*args) if fast else local_other(*args)

    return jax.shard_map(
        local,
        mesh=mesh,
        in_specs=(rows, P(), flat, flat, flat, flat, flat, rows),
        out_specs=(rows, rows, flat, flat, flat, flat, flat),
        check_vma=False,
    )
```

```python
import functools
import math

import jax
import jax.numpy as jnp
from jax import lax
from jax.experimental import pallas as pl
from jax.experimental.pallas import tpu as pltpu
from jax.sharding import PartitionSpec as P

HD = 64
IMG_LEN = 197
ROWS = 208
IMAGES_HERE = 2
BLOCK = 16
MESH_ID = pl.DeviceIdType.MESH
bf16, f32 = jnp.bfloat16, jnp.float32
eps_norm = 1e-06
masked_fill = -1e30
vmem_bytes = 56 * 2**20


def mm(a, b):
    return jnp.dot(a, b, preferred_element_type=f32)


def mm_nt(a, b):
    return lax.dot_general(a, b, (((1,), (1,)), ((), ())), preferred_element_type=f32)


def mm_tn(a, b):
    return lax.dot_general(a, b, (((0,), (0,)), ((), ())), preferred_element_type=f32)


def norm_forward(x, gain, bias):
    centered = x - jnp.mean(x, axis=-1, keepdims=True)
    inverse = lax.rsqrt(jnp.mean(centered * centered, axis=-1, keepdims=True) + eps_norm)
    hat = centered * inverse
    return (hat * gain + bias).astype(bf16), hat, inverse


def norm_backward(dh, hat, inverse, gain):
    scaled = dh * gain
    dv = inverse * (
        scaled
        - jnp.mean(scaled, axis=-1, keepdims=True)
        - hat * jnp.mean(scaled * hat, axis=-1, keepdims=True)
    )
    return dv, rows_sum(dh * hat), rows_sum(dh)


def rows_sum(x):
    return jnp.sum(x, axis=0, keepdims=True)


def remote(src, dst, send, recv, dev):
    return pltpu.make_async_remote_copy(
        src_ref=src, dst_ref=dst, send_sem=send, recv_sem=recv,
        device_id=(dev,), device_id_type=MESH_ID,
    )


class Place:
    def __init__(self, n):
        self.n = n
        me = self.me = lax.axis_index("dev")
        self.bits = [lax.rem(lax.div(me, 2**b), 2) for b in range(5)]
        self.c, self.x, self.y = self.bits[:3]
        self.z = lax.div(me, 8)
        self.core = self.flip(0)
        self.along_z = [self.flip(3), self.flip(4), self.flip(3, 4)]
        self.along_xy = [self.flip(1), self.flip(2), self.flip(1, 2)]
        self.chips = [self.flip(*[b + 1 for b in range(4) if m >> b & 1]) for m in range(1, 16)]
        self.up, self.down = lax.rem(me + 1, n), lax.rem(me + n - 1, n)

    def flip(self, *which):
        return self.me + sum((1 - 2 * self.bits[b]) * 2**b for b in which)

    def peers(self):
        return [self.core] + self.chips + [self.up, self.down]


def taken(ref, sem):
    pltpu.make_async_copy(ref, ref, sem).wait()


class Sender:
    def go(self, src, dst, k, dev):
        remote(src, dst, self.send.at[k], self.recv.at[k], dev).start()

    def arrived(self, k):
        taken(self.size_of[k], self.recv.at[k])

    def left(self):
        for k, ref in enumerate(self.size_of):
            taken(ref, self.send.at[k])


class Gather(Sender):
    def __init__(self, place, buf, room, send, recv):
        self.place, self.buf, self.send, self.recv = place, buf, send, recv
        three, nine = buf.at[pl.ds(0, 3), 0, 0, 0], room.at[:, pl.ds(1, 3)]
        self.size_of = [three, three, nine, buf.at[:, :, :, 0]]

    def begin(self):
        p = self.place
        own = self.buf.at[0, p.y, p.x, p.c]
        for k, dev in enumerate(p.along_z):
            self.go(own, self.buf.at[k + 1, p.y, p.x, p.c], 0, dev)
        for dev in p.along_xy:
            self.go(own, own, 1, dev)

    def middle(self):
        p = self.place
        self.arrived(0)
        got = self.buf.at[pl.ds(1, 3), p.y, p.x, p.c]
        for dev in p.along_xy:
            self.go(got, got, 2, dev)

    def core(self):
        p = self.place
        self.arrived(1)
        self.arrived(2)
        half = self.buf.at[:, :, :, p.c]
        self.go(half, half, 3, p.core)

    def done(self):
        self.arrived(3)


class Scatter(Sender):
    def __init__(self, place, grads, half, out_xy, in_xy, out_z, in_z, send, recv, out):
        self.place, self.grads, self.half = place, grads, half
        self.out_xy, self.in_xy, self.out_z, self.in_z = out_xy, in_xy, out_z, in_z
        self.send, self.recv, self.out = send, recv, out
        self.size_of = [half, in_xy.at[:, pl.ds(1, 3)], in_xy.at[:, 0], in_z]

    def begin(self):
        p = self.place
        self.go(self.grads.at[:, :, :, 1 - p.c], self.half, 0, p.core)

    def pair(self):
        self.arrived(0)
        self.out_xy[...] = (
            self.grads[:, :, :, self.place.c].astype(f32) + self.half[...].astype(f32)
        ).astype(bf16)

    def middle(self):
        p = self.place
        self.pair()
        goals = [(p.y, 1 - p.x), (1 - p.y, p.x), (1 - p.y, 1 - p.x)]
        for k, (y, x) in enumerate(goals):
            self.go(self.out_xy.at[pl.ds(1, 3), y, x], self.in_xy.at[k, pl.ds(1, 3)], 1, p.along_xy[k])
        for k, (y, x) in enumerate(goals):
            self.go(self.out_xy.at[0, y, x], self.in_xy.at[k, 0], 2, p.along_xy[k])

    def ours(self, z):
        p = self.place
        return self.grads[z, p.y, p.x, p.c].astype(f32) + self.half[z, p.y, p.x].astype(f32)

    def end(self):
        p = self.place
        self.arrived(1)
        for z in range(1, 4):
            total = self.ours(z)
            for k in range(3):
                total += self.in_xy[k, z].astype(f32)
            self.out_z[z - 1] = total.astype(bf16)
            self.go(self.out_z.at[z - 1], self.in_z.at[z - 1], 3, p.along_z[z - 1])

    def done(self):
        self.arrived(2)
        total = self.ours(0)
        for k in range(3):
            total += self.in_xy[k, 0].astype(f32)
        self.arrived(3)
        for k in range(3):
            total += self.in_z[k].astype(f32)
        self.out[...] = total


class Direct(Scatter):
    def __init__(self, *args):
        super().__init__(*args)
        self.size_of = [self.half, self.in_xy]

    def middle(self):
        p = self.place
        self.pair()
        for m, dev in enumerate(p.chips, 1):
            y = 1 - p.y if m & 2 else p.y
            x = 1 - p.x if m & 1 else p.x
            self.go(self.out_xy.at[m >> 2, y, x], self.in_xy.at[m - 1], 1, dev)

    def done(self):
        total = self.ours(0)
        self.arrived(1)
        for k in range(15):
            total += self.in_xy[k].astype(f32)
        self.out[...] = total


def natural(c, z):
    return jnp.where((c & 7) < 6, 6 * ((c >> 3) ^ (8 * z)) + (c & 7), -1)


def iota(shape, dim):
    return lax.broadcasted_iota(jnp.int32, shape, dim)


def norm_padded(x, gain, bias, real, d):
    centered = (x - jnp.sum(x, axis=-1, keepdims=True) * (1.0 / d)) * real
    inverse = lax.rsqrt(jnp.sum(centered * centered, axis=-1, keepdims=True) * (1.0 / d) + eps_norm)
    hat = centered * inverse
    return (hat * gain + bias).astype(bf16), hat, inverse


def norm_padded_back(dh, hat, inverse, gain, d):
    scaled = dh * gain
    dv = inverse * (
        scaled
        - jnp.sum(scaled, axis=-1, keepdims=True) * (1.0 / d)
        - hat * (jnp.sum(scaled * hat, axis=-1, keepdims=True) * (1.0 / d))
    )
    return dv, rows_sum(dh * hat), rows_sum(dh)


def sublanes(x, shift):
    return pltpu.roll(x, shift, 1)


def unfold(tiles, s):
    a, b, c = tiles
    return jnp.where(s < 2, sublanes(a, 2), jnp.where(s < 4, sublanes(b, 4), sublanes(c, 6)))


def fold(tiles, extra, s):
    return [jnp.where(s < 6, t, sublanes(extra, 6 - 2 * k)) for k, t in enumerate(tiles)]


def fused_kernel(n, layers, d, ranges, *refs):
    refs = list(refs)
    take = lambda count: [refs.pop(0) for _ in range(count)]
    tok, cot, a_in, a_out, m_in, m_out, vecs = take(7)
    reds, (act_out, dx_out) = take(3), take(2)
    wires, grads, halves, outxys, inxys, outzs, inzs = [take(3) for _ in range(7)]
    (in_direct,) = take(1)
    tok_near, cot_near, act_near, act_in, dx_near, dx_in = take(6)
    w_in_s, w_one_s, w_out_s, w_two_s, two_s, g_two_s = take(6)
    vec_n, vec_g, b_one_s, line_n, line_g = take(5)
    hat1_s, h1_s, qkv_s, p_s, o_s, hat2_s, h2_s, slope_s, a_s, inv_s = take(10)
    dqkv_s, do_s, pack_a, pack_b, pack_c, flat_ai, flat_ao, flat_mi, flat_mo, vec_s = take(10)
    gsend, grecv, ssend, srecv, hsend, hrecv = take(6)
    wire_a, wire_b, wire_c = wires
    slots = tok.shape[1]
    heads = d // HD
    wide = 8 * n
    hidden_units = 4 * d
    rows = IMAGES_HERE * ROWS
    place = Place(n)
    me = place.me

    barrier = pltpu.get_barrier_semaphore()
    for other in place.peers():
        pl.semaphore_signal(barrier, inc=1, device_id=(other,), device_id_type=MESH_ID)

    part = vecs.shape[1]
    here = (0, place.y, place.x, place.c)
    z_of = [place.z] + [lax.div(dev, 8) for dev in place.along_z]
    vec_s[...] = jnp.zeros_like(vec_s)
    vec_s[0:layers, 0:part] = vecs[...].astype(f32)
    moved = pltpu.roll(vec_s[...], 8 * lax.rem(me, 8), 1)
    vec_s[...] = moved
    flat_ai[...] = a_in[...].astype(f32)
    flat_mo[...] = m_out[...].astype(f32)
    pack_b[...] = jnp.zeros_like(pack_b)

    def pack_first(l):
        row = slice(l, l + 1)
        for r in range(6):
            base, k, i = r * 3 * d, r // 2, r % 2
            pack_a[r:r + 1, :] = flat_ai[row, base:base + 256]
            pack_a[8 + r:9 + r, :128] = flat_ai[row, base + 256:base + 384]
            low, lanes = 6 + i + (8 if k == 2 else 0), slice(128 * (k % 2), 128 * (k % 2) + 128)
            pack_a[low:low + 1, lanes] = flat_ai[row, base + 384:base + 512]
            pack_a[8 + r:9 + r, 128:192] = flat_ai[row, base + 512:base + 576]
        pack_a[14:15, 128:192] = vec_s[row, :64]
        pack_a[15:16, 128:192] = vec_s[row, 64:128]
        for r in range(8):
            pack_a[8 + r:9 + r, 192:] = flat_mo[row, (16 + r) * d + 128:(17 + r) * d]
        wire_a[(l,) + here] = pack_a[...].astype(bf16)

    def pack_second(l):
        row = slice(l, l + 1)
        for r in range(6):
            base, k, i = r * 4 * d, r // 2, r % 2
            lanes = slice(128 * k, 128 * k + 128)
            pack_b[r:r + 1, :] = flat_mi[row, base:base + 384]
            pack_b[6 + i:7 + i, lanes] = flat_mi[row, base + 384:base + 512]
            pack_b[8 + r:9 + r, :256] = flat_mi[row, base + 512:base + 768]
            pack_b[8 + r:9 + r, 256:] = flat_ao[row, r * d:r * d + 128]
            pack_b[14 + i:15 + i, 128 * k:128 * k + 64] = flat_ao[row, r * d + 128:(r + 1) * d]
        wire_b[(l,) + here] = pack_b[...].astype(bf16)

    def pack_third(l):
        row = slice(l, l + 1)
        for r in range(24):
            g, i = r // 8, r % 8
            low, lane = i + (8 if g == 2 else 0), 128 * (g % 2)
            pack_c[low:low + 1, lane:lane + 128] = flat_mo[row, r * d:r * d + 128]
            if g < 2:
                pack_c[8 + i:9 + i, 128 + 64 * g:192 + 64 * g] = flat_mo[row, r * d + 128:(r + 1) * d]
        wire_c[(l,) + here] = pack_c[...].astype(bf16)

    gathers = [
        [
            Gather(place, wires[k].at[l], inxys[k].at[l], gsend.at[l, k], grecv.at[l, k])
            for k in range(3)
        ]
        for l in range(layers)
    ]
    scatters = [
        [
            (Direct if k == 0 and l == 0 else Scatter)(
                place, grads[k].at[l], halves[k].at[l], outxys[k].at[l],
                in_direct if k == 0 and l == 0 else inxys[k].at[l],
                outzs[k].at[l], inzs[k].at[l], ssend.at[l, k], srecv.at[l, k], reds[k].at[l],
            )
            for k in range(3)
        ]
        for l in range(layers)
    ]
    side = slots // 2
    first_half, second_half = pl.ds(0, side), pl.ds(side, side)

    def pair(src, dst, at):
        return [
            remote(src.at[:, a], dst.at[:, b], hsend.at[at + i], hrecv.at[at + i], dev)
            for i, (a, b, dev) in enumerate((
                (first_half, first_half, place.down), (second_half, second_half, place.up),
            ))
        ]

    tok_halo, cot_halo = pair(tok, tok_near, 0), pair(cot, cot_near, 2)
    back = lambda src, dst, at: [
        remote(src.at[:, first_half], dst.at[:, first_half], hsend.at[at], hrecv.at[at], place.up),
        remote(src.at[:, second_half], dst.at[:, second_half], hsend.at[at + 1], hrecv.at[at + 1], place.down),
    ]
    act_halo, dx_halo = back(act_near, act_in, 4), back(dx_near, dx_in, 6)
    (ga0, gb0, gc0), (ga1, gb1, gc1) = gathers
    (sa0, sb0, sc0), (sa1, sb1, sc1) = scatters

    pack_first(0)
    pl.semaphore_wait(barrier, len(place.peers()))
    ga0.begin()
    for copy in tok_halo:
        copy.start()
    flat_ao[...] = a_out[...].astype(f32)
    flat_mi[...] = m_in[...].astype(f32)
    pack_second(0)
    gb0.begin()
    pack_third(0)
    gc0.begin()
    pack_first(1)
    ga1.begin()
    pack_second(1)
    gb1.begin()
    pack_third(1)
    gc1.begin()
    for copy in cot_halo:
        copy.start()

    lane = iota((1, wide), 1)
    real = jnp.where((lane & 7) < 6, 1.0, 0.0)
    spread = jnp.where(iota((d, wide), 0) == natural(iota((1, wide), 1), place.z), 1.0, 0.0).astype(bf16)
    owner = (lane >> 3) ^ (8 * place.z)
    window = jnp.where((lane & 7) >= 6, owner + (owner >> 3) + (lane & 1), -1)
    windows = [
        jnp.where(3 * iota((BLOCK, wide), 0) + k == window, 1.0, 0.0).astype(bf16) for k in range(3)
    ]
    sub = iota((1, 8, 1), 1)

    first, last, below = ranges[0, me], ranges[1, me], ranges[0, place.down]
    total = ranges[1, n - 1]
    centre = IMG_LEN // 2
    image = (first + IMG_LEN - 1 - centre) // IMG_LEN
    picks, valid_keys = [], []
    for k in range(IMAGES_HERE):
        begin = (image + k) * IMG_LEN
        mine = (begin < total) & (jnp.minimum(begin + centre, total - 1) < last)
        count = jnp.where(mine, jnp.minimum(IMG_LEN, total - begin), 0)
        r = iota((ROWS, 2 * slots), 0)
        c = iota((ROWS, 2 * slots), 1)
        t = begin + r
        column = jnp.where(
            t < first, t - below + slots, jnp.where(t < last, t - first, t - last + slots)
        )
        column = jnp.where(r < count, column, -1)
        picks.append(jnp.where(column == c, 1.0, 0.0).astype(bf16))
        valid_keys.append(iota((ROWS, ROWS), 1) < count)
    pick = jnp.concatenate(picks, axis=0)
    x = mm_nt(pick[:, :slots], mm_tn(spread, tok[...]).astype(bf16))

    ga0.middle()
    gb0.middle()
    gc0.middle()
    ga0.core()
    ga1.middle()
    for copy in tok_halo:
        copy.wait_recv()
    x += mm_nt(pick[:, slots:], mm_tn(spread, tok_near[...]).astype(bf16))

    def tiles_of(wire, l):
        v = wire[l]
        width = v.shape[-1]
        v = v.reshape(n * BLOCK, width).astype(f32).reshape(n, 2, 8, width)
        return [v[:, i, :, k:k + 128] for i in range(2) for k in range(0, width, 128)]

    def flat(t):
        return t.reshape(wide, t.shape[-1]).astype(bf16)

    def unpack_a(l):
        t0, t1, t2, t4 = tiles_of(wire_a, l)
        for k, t in enumerate((t0, t1, t2, unfold((t0, t1, t2), sub), t4)):
            w_in_s[l, :, 128 * k:128 * k + 128] = flat(t)
        t4 = flat(t4)
        lines = jnp.concatenate([mm(each, t4)[:, :64] for each in windows], axis=1)
        vec_n[l] = lines
        vec_g[l] = mm(lines.astype(bf16), spread)
        for k in range(4):
            b_one_s[l, 0:1, k * d:(k + 1) * d] = lines[8 + k:9 + k]

    def unpack_b(l):
        t0, t1, t2, t4, t5, t6 = tiles_of(wire_b, l)
        for k, t in enumerate((t0, t1, t2, unfold((t0, t1, t2), sub), t4, t5)):
            w_one_s[l, :, 128 * k:128 * k + 128] = flat(t)
        t7 = unfold((t4, t5, t6), sub)
        out = jnp.concatenate([flat(t6), flat(t7)], axis=1)
        out = mm(spread, out)[:, :d].astype(bf16)
        w_out_s[l] = mm(out, spread).astype(bf16)

    def unpack_c(l):
        t0, t1, t2, t3 = tiles_of(wire_c, l)
        last = tiles_of(wire_a, l)[3]
        side = pltpu.roll(t3, 64, 2), pltpu.roll(last, 64, 2)
        pile = lambda ts: jnp.stack(ts, axis=1).reshape(4, d, 128).astype(bf16)
        left, right = pile((t0, t1, t2)), pile((t3,) + side)
        for k in range(4):
            at = pl.ds(pl.multiple_of(z_of[k] * d, BLOCK), d)
            two_s[at, :128] = left[k]
            two_s[at, 128:] = right[k]
        w_two_s[l] = mm(two_s[:, :d], spread).astype(bf16)

    beats = [
        [lambda: gb1.middle(), lambda: gc1.middle(), lambda: gb0.core(), lambda: gc0.core(), lambda: ga1.core()],
        [lambda: gb1.core(), lambda: gc1.core(), lambda: None, lambda: None, lambda: None],
    ]
    for l in range(layers):
        ga, gb, gc = gathers[l]
        ga.done()
        unpack_a(l)
        h, hat, inv = norm_padded(x, vec_g[l, 0:1], vec_g[l, 1:2], real, d)
        hat1_s[l], h1_s[l], inv_s[l, 0] = hat, h, inv
        projected = mm(h, w_in_s[l, :, :3 * d])
        qkv_s[l, :, :d] = ((projected[:, :d] + vec_n[l, 2:3]).astype(bf16).astype(f32)
                           * (1.0 / math.sqrt(HD))).astype(bf16)
        qkv_s[l, :, d:2 * d] = projected[:, d:2 * d].astype(bf16)
        qkv_s[l, :, 2 * d:] = (projected[:, 2 * d:] + vec_n[l, 3:4]).astype(bf16)
        beats[l][0]()
        for i in range(IMAGES_HERE):
            at = slice(i * ROWS, (i + 1) * ROWS)
            for head in range(heads):
                q = qkv_s[l, at, head * HD:(head + 1) * HD]
                key = qkv_s[l, at, d + head * HD:d + (head + 1) * HD]
                val = qkv_s[l, at, 2 * d + head * HD:2 * d + (head + 1) * HD]
                scores = jnp.where(valid_keys[i], mm_nt(q, key), masked_fill)
                e = jnp.exp(scores - jnp.max(scores, axis=-1, keepdims=True))
                p = e * (1.0 / jnp.sum(e, axis=-1, keepdims=True))
                p_s[l, i, head] = p
                o_s[l, at, head * HD:(head + 1) * HD] = mm(p.astype(bf16), val).astype(bf16)
            beats[l][1 + i]()
        gb.done()
        beats[l][3]()
        unpack_b(l)
        x1 = x + (mm(o_s[l], w_out_s[l]) + vec_g[l, 4:5])
        h2, hat, inv = norm_padded(x1, vec_g[l, 5:6], vec_g[l, 6:7], real, d)
        hat2_s[l], h2_s[l], inv_s[l, 1] = hat, h2, inv
        u = mm(h2, w_one_s[l]) + b_one_s[l, 0:1]
        phi = 0.5 * (1.0 + lax.erf(u * (1.0 / math.sqrt(2.0))))
        a_s[l] = (u * phi).astype(bf16)
        slope_s[l] = phi + u * (jnp.exp(-0.5 * u * u) * (1.0 / math.sqrt(2.0 * math.pi)))
        beats[l][4]()
        gc.done()
        unpack_c(l)
        x = x1 + (mm(a_s[l], w_two_s[l]) + vec_g[l, 7:8])

    x_low = mm_nt(x.astype(bf16), spread).astype(bf16)
    act_near[...] = mm_tn(x_low, pick[:, slots:]).astype(bf16)
    for copy in act_halo:
        copy.start()
    act_own = mm_tn(x_low, pick[:, :slots]).astype(bf16)

    for copy in cot_halo:
        copy.wait_recv()
    dx = mm_nt(pick[:, :slots], mm_tn(spread, cot[...]).astype(bf16))
    dx += mm_nt(pick[:, slots:], mm_tn(spread, cot_near[...]).astype(bf16))

    def cut(w, pieces):
        return [w[:, 128 * k:128 * k + 128].reshape(n, 8, 128) for k in range(pieces)]

    def block(tiles):
        half = len(tiles) // 2
        v = [jnp.concatenate(tiles[i * half:(i + 1) * half], axis=-1)[:, None] for i in range(2)]
        v = jnp.concatenate(v, axis=1).reshape(n * BLOCK, 128 * half).astype(bf16)
        return v.reshape(4, 2, 2, 2, BLOCK, 128 * half)

    beats = [
        [lambda: (sa1.middle(), sc1.end()), lambda: sc0.middle(),
         lambda: (sb1.end(), sb0.middle()), lambda: None],
        [lambda: None, lambda: sc1.middle(), lambda: sb1.middle(), lambda: None],
    ]
    dqkv_s[:, 3 * d:] = jnp.zeros((rows, d), bf16)
    low_lanes = iota((1, 1, 128), 2) < 64
    line_g[...] = jnp.zeros_like(line_g)
    line_n[...] = jnp.zeros_like(line_n)
    for l in reversed(range(layers)):
        sa, sb, sc = scatters[l]
        dm = dx.astype(bf16)
        line_g[7:8] = rows_sum(dm.astype(f32))
        g_two_s[...] = mm_tn(a_s[l], mm_nt(dm, spread).astype(bf16))
        g_two = jnp.concatenate(
            [g_two_s[pl.ds(pl.multiple_of(z * d, BLOCK), d), :] for z in z_of], axis=0
        ).reshape(n, 3, 8, d)
        side = jnp.concatenate([g_two[..., 128:], jnp.zeros((n, 3, 8, 256 - d), f32)], axis=-1)
        turned = pltpu.roll(side[:, 1], 64, 2)
        tail = pltpu.roll(side[:, 2], 64, 2)
        grads[2][l] = block([g_two[:, 0, :, :128], g_two[:, 1, :, :128], g_two[:, 2, :, :128],
                             jnp.where(low_lanes, side[:, 0], turned)])
        sc.begin()
        du = (mm_nt(dm, w_two_s[l]) * slope_s[l]).astype(bf16)
        beats[l][0]()
        g_b1 = rows_sum(du.astype(f32))
        for k in range(4):
            line_n[8 + k:9 + k] = g_b1[:, k * d:(k + 1) * d]
        dh2 = mm_nt(du, w_one_s[l])
        dv, g_g2, g_c2 = norm_padded_back(dh2, hat2_s[l], inv_s[l, 1], vec_g[l, 5:6], d)
        line_g[5:6], line_g[6:7] = g_g2, g_c2
        dx1 = dx + dv
        db = dx1.astype(bf16)
        line_g[4:5] = rows_sum(db.astype(f32))
        g_out = mm_tn(o_s[l], mm_nt(db, spread).astype(bf16))
        g_out = jnp.concatenate([g_out, jnp.zeros((d, 256 - d), f32)], axis=1).astype(bf16)
        t6, t7 = cut(mm_tn(spread, g_out), 2)
        t0, t1, t2, t3, t4, t5 = cut(mm_tn(h2_s[l], du), 6)
        grads[1][l] = block(fold((t0, t1, t2), t3, sub) + fold((t4, t5, t6), t7, sub))
        beats[l][1]()
        sb.begin()
        do_s[...] = mm_nt(db, w_out_s[l]).astype(bf16)
        for i in range(IMAGES_HERE):
            at = slice(i * ROWS, (i + 1) * ROWS)
            for head in range(heads):
                q_at = slice(head * HD, (head + 1) * HD)
                k_at = slice(d + head * HD, d + (head + 1) * HD)
                v_at = slice(2 * d + head * HD, 2 * d + (head + 1) * HD)
                do = do_s[at, q_at]
                p = p_s[l, i, head]
                dp = mm_nt(do, qkv_s[l, at, v_at])
                ds = (p * (dp - jnp.sum(p * dp, axis=-1, keepdims=True))).astype(bf16)
                dqkv_s[at, q_at] = (mm(ds, qkv_s[l, at, k_at]) * (1.0 / math.sqrt(HD))).astype(bf16)
                dqkv_s[at, k_at] = mm_tn(ds, qkv_s[l, at, q_at]).astype(bf16)
                dqkv_s[at, v_at] = mm_tn(p.astype(bf16), do).astype(bf16)
            beats[l][2 + i]()
        dqkv = dqkv_s[:, :640]
        line_n[2:3] = rows_sum(dqkv_s[:, :d].astype(f32))
        line_n[3:4] = rows_sum(dqkv_s[:, 2 * d:3 * d].astype(f32))
        dh = mm_nt(dqkv, w_in_s[l])
        dv, g_g1, g_c1 = norm_padded_back(dh, hat1_s[l], inv_s[l, 0], vec_g[l, 0:1], d)
        line_g[0:1], line_g[1:2] = g_g1, g_c1
        lines = (line_n[...] + mm_nt(line_g[...].astype(bf16), spread)).astype(bf16)
        vec_rows = sum(mm_tn(windows[k], lines[:, 64 * k:64 * k + 64]) for k in range(3))
        vec_rows = jnp.concatenate([vec_rows, jnp.zeros((wide, 64), f32)], axis=1).reshape(n, 8, 128)
        t0, t1, t2, t3, t4 = cut(mm_tn(h1_s[l], dqkv), 5)
        t4 = jnp.where(low_lanes, t4 + vec_rows, tail)
        grads[0][l] = block(fold((t0, t1, t2), t3, sub) + [t4])
        sa.begin()
        dx = dx1 + dv

    high = dx.astype(bf16)
    low = (dx - high.astype(f32)).astype(bf16)
    high = mm_nt(high, spread).astype(bf16)
    dx_near[...] = mm_tn(high, pick[:, slots:]).astype(bf16)
    for copy in dx_halo:
        copy.start()
    sa1.end()
    sa0.middle()
    sc0.end()
    low = mm_nt(low, spread).astype(bf16)
    dx_own = mm_tn(high, pick[:, :slots]) + mm_tn(low, pick[:, :slots])
    sc1.done()
    sb0.end()
    sb1.done()
    for copy in act_halo:
        copy.wait_recv()
    act_out[...] = act_own + act_in[...]
    for copy in dx_halo:
        copy.wait_recv()
    dx_out[...] = dx_own + dx_in[...].astype(f32)
    sa1.done()
    sc0.done()
    sb0.done()
    sa0.done()
    for copy in tok_halo + cot_halo + act_halo + dx_halo:
        copy.wait_send()
    for group in gathers + scatters:
        for each in group:
            each.left()


def fused(n, ranges, tok, cot, flats):
    d, slots = tok.shape
    layers = flats[0].shape[0]
    wide = 8 * n
    hidden_units = 4 * d
    rows = IMAGES_HERE * ROWS
    shapes = ((BLOCK, 256), (BLOCK, 384), (BLOCK, 256))
    boxes = lambda lead, kind: [pltpu.VMEM((layers,) + lead + s, kind) for s in shapes]
    vm = pl.BlockSpec(memory_space=pltpu.VMEM)
    scratch = (
        boxes((4, 2, 2, 2), bf16) + boxes((4, 2, 2, 2), bf16)
        + boxes((4, 2, 2), bf16) + boxes((4, 2, 2), bf16) + boxes((3, 4), bf16)
        + boxes((3,), bf16) + boxes((3,), bf16)
        + [pltpu.VMEM((15,) + shapes[0], bf16)]
        + [pltpu.VMEM((d, slots), bf16)] * 6
        + [
            pltpu.VMEM((layers, wide, 640), bf16),
            pltpu.VMEM((layers, wide, hidden_units), bf16),
            pltpu.VMEM((layers, d, wide), bf16),
            pltpu.VMEM((layers, hidden_units, wide), bf16),
            pltpu.VMEM((hidden_units, 256), bf16),
            pltpu.VMEM((hidden_units, d), f32),
            pltpu.VMEM((layers, BLOCK, d), f32),
            pltpu.VMEM((layers, BLOCK, wide), f32),
            pltpu.VMEM((layers, 8, hidden_units), f32),
            pltpu.VMEM((BLOCK, d), f32),
            pltpu.VMEM((BLOCK, wide), f32),
            pltpu.VMEM((layers, rows, wide), f32),
            pltpu.VMEM((layers, rows, wide), bf16),
            pltpu.VMEM((layers, rows, 3 * d), bf16),
            pltpu.VMEM((layers, IMAGES_HERE, d // HD, ROWS, ROWS), f32),
            pltpu.VMEM((layers, rows, d), bf16),
            pltpu.VMEM((layers, rows, wide), f32),
            pltpu.VMEM((layers, rows, wide), bf16),
            pltpu.VMEM((layers, rows, hidden_units), f32),
            pltpu.VMEM((layers, rows, hidden_units), bf16),
            pltpu.VMEM((layers, 2, rows, 1), f32),
            pltpu.VMEM((rows, 4 * d), bf16),
            pltpu.VMEM((rows, d), bf16),
        ]
        + [pltpu.VMEM(s, f32) for s in shapes]
        + [pltpu.VMEM(f.shape, f32) for f in flats[:4]]
        + [pltpu.VMEM((8, 128), f32)]
        + [pltpu.SemaphoreType.DMA((layers, 3, 4))] * 4
        + [pltpu.SemaphoreType.DMA((8,))] * 2
    )
    return pl.pallas_call(
        functools.partial(fused_kernel, n, layers, d),
        out_shape=tuple(jax.ShapeDtypeStruct((layers,) + s, f32) for s in shapes)
        + (jax.ShapeDtypeStruct((d, slots), bf16), jax.ShapeDtypeStruct((d, slots), f32)),
        in_specs=[pl.BlockSpec(memory_space=pltpu.SMEM)] + [vm] * 7,
        out_specs=(vm,) * 5,
        scratch_shapes=scratch,
        compiler_params=pltpu.CompilerParams(
            collective_id=0, has_side_effects=True, vmem_limit_bytes=vmem_bytes
        ),
        name="two_layers",
    )(ranges.T, tok, cot, *flats)


def flatten_kernel(n, layers, d, red_a, red_b, red_c, act_in, dx_in, act, dx, g_in, g_out, g_one, g_two, g_vec, vec_s):
    me = lax.axis_index("dev")
    act[...] = act_in[...]
    dx[...] = dx_in[...]
    vec_s[...] = jnp.zeros_like(vec_s)
    for l in range(layers):
        row = slice(l, l + 1)
        for r in range(6):
            k, i = r // 2, r % 2
            base = r * 3 * d
            g_in[row, base:base + 256] = red_a[l, r:r + 1, :]
            g_in[row, base + 256:base + 384] = red_a[l, 8 + r:9 + r, :128]
            low, lane = 6 + i + (8 if k == 2 else 0), 128 * (k % 2)
            g_in[row, base + 384:base + 512] = red_a[l, low:low + 1, lane:lane + 128]
            g_in[row, base + 512:base + 576] = red_a[l, 8 + r:9 + r, 128:192]
            base = r * 4 * d
            g_one[row, base:base + 384] = red_b[l, r:r + 1, :]
            g_one[row, base + 384:base + 512] = red_b[l, 6 + i:7 + i, 128 * k:128 * k + 128]
            g_one[row, base + 512:base + 768] = red_b[l, 8 + r:9 + r, :256]
            base = r * d
            g_out[row, base:base + 128] = red_b[l, 8 + r:9 + r, 256:]
            g_out[row, base + 128:base + 192] = red_b[l, 14 + i:15 + i, 128 * k:128 * k + 64]
        for r in range(24):
            g, i = r // 8, r % 8
            base, low, lane = r * d, i + (8 if g == 2 else 0), 128 * (g % 2)
            g_two[row, base:base + 128] = red_c[l, low:low + 1, lane:lane + 128]
            if g < 2:
                g_two[row, base + 128:base + 192] = red_c[l, 8 + i:9 + i, 128 + 64 * g:192 + 64 * g]
            else:
                g_two[row, base + 128:base + 192] = red_a[l, 8 + i:9 + i, 192:]
        vec_s[row, :64] = red_a[l, 14:15, 128:192]
        vec_s[row, 64:] = red_a[l, 15:16, 128:192]
    part = g_vec.shape[1]
    moved = pltpu.roll(vec_s[...], lax.rem(128 - 8 * lax.rem(me, 8), 128), 1)
    g_vec[...] = moved[0:layers, 0:part]


def local_fused(tokens, ranges, attn_in, attn_out, mlp_in, mlp_out, vectors, cotangent):
    n = lax.axis_size("dev")
    slots, d = tokens.shape
    layers, part = vectors.shape
    flats = (attn_in, attn_out, mlp_in, mlp_out, vectors)
    sums = fused(n, ranges, tokens.T, cotangent.T, flats)
    vm = pl.BlockSpec(memory_space=pltpu.VMEM)
    act, dx, *grads = pl.pallas_call(
        functools.partial(flatten_kernel, n, layers, d),
        out_shape=(
            jax.ShapeDtypeStruct((d, slots), bf16), jax.ShapeDtypeStruct((d, slots), f32),
        ) + tuple(jax.ShapeDtypeStruct(f.shape, f32) for f in flats),
        in_specs=[vm] * 5,
        out_specs=(vm,) * 7,
        scratch_shapes=[pltpu.VMEM((8, 128), f32)],
        compiler_params=pltpu.CompilerParams(vmem_limit_bytes=vmem_bytes),
        name="flatten",
    )(*sums)
    return (act.T, dx.T, *grads)


def compute_kernel(n, layers, width, hidden_units, ranges, *refs):
    refs = list(refs)
    take = lambda count: [refs.pop(0) for _ in range(count)]
    (w_full,) = take(1)
    tok, cot, tok_up, cot_up = take(4)
    (grad_out,) = take(1)
    act_own, act_up, dx_own, dx_up = take(4)
    w_all, w_one_s, w_two_s, hat1_s, h1_s, qkv_s, p_s, o_s, hat2_s, h2_s, slope_s, a_s = take(12)
    inv_s, dqkv_s, do_s, grad_s, perm = take(5)
    slots = tok.shape[1]
    heads = width // HD
    d = width
    me = lax.axis_index("dev")
    first, last = ranges[me, 0], ranges[me, 1]
    total = ranges[n - 1, 1]
    image = (first + IMG_LEN - 1) // IMG_LEN
    rows = IMAGES_HERE * ROWS

    picks, valid_keys = [], []
    for k in range(IMAGES_HERE):
        begin = (image + k) * IMG_LEN
        count = jnp.where(begin < last, jnp.minimum(IMG_LEN, total - begin), 0)
        r = lax.broadcasted_iota(jnp.int32, (ROWS, 2 * slots), 0)
        c = lax.broadcasted_iota(jnp.int32, (ROWS, 2 * slots), 1)
        t = begin + r
        column = jnp.where(t < last, t - first, t - last + slots)
        column = jnp.where(r < count, column, -1)
        picks.append(jnp.where(column == c, 1.0, 0.0).astype(bf16))
        valid_keys.append(lax.broadcasted_iota(jnp.int32, (ROWS, ROWS), 1) < count)
    pick = jnp.concatenate(picks, axis=0)
    x = mm_nt(pick[:, :slots], tok[...]) + mm_nt(pick[:, slots:], tok_up[...])

    unit = lax.broadcasted_iota(jnp.int32, (1, hidden_units), 1)
    group = sum(jnp.where(unit >= j * d, 1, 0) for j in range(1, 4))
    origin = 4 * (unit - group * d) + group
    f = lax.broadcasted_iota(jnp.int32, (hidden_units, hidden_units), 0)
    perm[...] = jnp.where(f == origin, 1.0, 0.0).astype(bf16)

    vec = [None] * layers
    b_one = [None] * layers
    for l in range(layers):
        w_all[l] = w_full[l]
        w_one_s[l] = mm(w_all[l, :d, 4 * d:8 * d], perm[...]).astype(bf16)
        for j in range(4):
            w_two_s[l, j * d:(j + 1) * d, :] = w_all[l, :d, (8 + j) * d:(9 + j) * d]
        tail = w_all[l, d:d + BLOCK, :]
        vec[l] = tail.astype(f32)[0:1, :]
        b_one[l] = mm(tail[:, 8 * d:], perm[...])[0:1, :]

    def v_of(l, index):
        return vec[l][:, index * d:(index + 1) * d]

    for l in range(layers):
        h, hat, inv = norm_forward(x, v_of(l, 0), v_of(l, 1))
        hat1_s[l], h1_s[l], inv_s[l, 0] = hat, h, inv
        projected = mm(h, w_all[l, :d, :3 * d])
        qkv_s[l, :, :d] = ((projected[:, :d] + v_of(l, 2)).astype(bf16).astype(f32)
                           * (1.0 / math.sqrt(HD))).astype(bf16)
        qkv_s[l, :, d:2 * d] = projected[:, d:2 * d].astype(bf16)
        qkv_s[l, :, 2 * d:] = (projected[:, 2 * d:] + v_of(l, 3)).astype(bf16)
        for i in range(IMAGES_HERE):
            at = slice(i * ROWS, (i + 1) * ROWS)
            for head in range(heads):
                q = qkv_s[l, at, head * HD:(head + 1) * HD]
                key = qkv_s[l, at, d + head * HD:d + (head + 1) * HD]
                val = qkv_s[l, at, 2 * d + head * HD:2 * d + (head + 1) * HD]
                scores = jnp.where(valid_keys[i], mm_nt(q, key), masked_fill)
                e = jnp.exp(scores - jnp.max(scores, axis=-1, keepdims=True))
                p = e * (1.0 / jnp.sum(e, axis=-1, keepdims=True))
                p_s[l, i, head] = p
                o_s[l, at, head * HD:(head + 1) * HD] = mm(p.astype(bf16), val).astype(bf16)
        x1 = x + (mm(o_s[l], w_all[l, :d, 3 * d:4 * d]) + v_of(l, 4))
        h2, hat, inv = norm_forward(x1, v_of(l, 5), v_of(l, 6))
        hat2_s[l], h2_s[l], inv_s[l, 1] = hat, h2, inv
        u = mm(h2, w_one_s[l]) + b_one[l]
        phi = 0.5 * (1.0 + lax.erf(u * (1.0 / math.sqrt(2.0))))
        a_s[l] = (u * phi).astype(bf16)
        slope_s[l] = phi + u * (jnp.exp(-0.5 * u * u) * (1.0 / math.sqrt(2.0 * math.pi)))
        x = x1 + (mm(a_s[l], w_two_s[l]) + v_of(l, 7))

    x_low = x.astype(bf16)
    act_own[...] = mm_tn(x_low, pick[:, :slots]).astype(bf16)
    act_up[...] = mm_tn(x_low, pick[:, slots:]).astype(bf16)

    dx = mm_nt(pick[:, :slots], cot[...]) + mm_nt(pick[:, slots:], cot_up[...])
    for l in reversed(range(layers)):
        dm = dx.astype(bf16)
        g_two = mm_tn(a_s[l], dm)
        for j in range(4):
            grad_s[l, :d, (8 + j) * d:(9 + j) * d] = g_two[j * d:(j + 1) * d, :].astype(bf16)
        g_b2 = rows_sum(dm.astype(f32))
        du = (mm_nt(dm, w_two_s[l]) * slope_s[l]).astype(bf16)
        g_b1 = mm_nt(jnp.broadcast_to(rows_sum(du.astype(f32)), (BLOCK, hidden_units)).astype(bf16),
                     perm[...])[0:1, :]
        g_one = mm_tn(h2_s[l], du).astype(bf16)
        grad_s[l, :d, 4 * d:8 * d] = mm_nt(g_one, perm[...]).astype(bf16)
        dh2 = mm_nt(du, w_one_s[l])
        dv, g_g2, g_c2 = norm_backward(dh2, hat2_s[l], inv_s[l, 1], v_of(l, 5))
        dx1 = dx + dv
        db = dx1.astype(bf16)
        g_bo = rows_sum(db.astype(f32))
        grad_s[l, :d, 3 * d:4 * d] = mm_tn(o_s[l], db).astype(bf16)
        do_s[...] = mm_nt(db, w_all[l, :d, 3 * d:4 * d]).astype(bf16)
        for i in range(IMAGES_HERE):
            at = slice(i * ROWS, (i + 1) * ROWS)
            for head in range(heads):
                q_at = slice(head * HD, (head + 1) * HD)
                k_at = slice(d + head * HD, d + (head + 1) * HD)
                v_at = slice(2 * d + head * HD, 2 * d + (head + 1) * HD)
                do = do_s[at, q_at]
                p = p_s[l, i, head]
                dp = mm_nt(do, qkv_s[l, at, v_at])
                ds = (p * (dp - jnp.sum(p * dp, axis=-1, keepdims=True))).astype(bf16)
                dqkv_s[at, q_at] = (mm(ds, qkv_s[l, at, k_at]) * (1.0 / math.sqrt(HD))).astype(bf16)
                dqkv_s[at, k_at] = mm_tn(ds, qkv_s[l, at, q_at]).astype(bf16)
                dqkv_s[at, v_at] = mm_tn(p.astype(bf16), do).astype(bf16)
        g_bq = rows_sum(dqkv_s[:, :d].astype(f32))
        g_bv = rows_sum(dqkv_s[:, 2 * d:].astype(f32))
        grad_s[l, :d, :3 * d] = mm_tn(h1_s[l], dqkv_s[...]).astype(bf16)
        dh = mm_nt(dqkv_s[...], w_all[l, :d, :3 * d])
        dv, g_g1, g_c1 = norm_backward(dh, hat1_s[l], inv_s[l, 0], v_of(l, 0))
        dx = dx1 + dv
        line = jnp.concatenate([g_g1, g_c1, g_bq, g_bv, g_bo, g_g2, g_c2, g_b2, g_b1], axis=1)
        grad_s[l, d:d + BLOCK, :] = jnp.broadcast_to(line, (BLOCK, line.shape[1])).astype(bf16)

    high = dx.astype(bf16)
    low = (dx - high.astype(f32)).astype(bf16)
    dx_own[...] = mm_tn(high, pick[:, :slots]) + mm_tn(low, pick[:, :slots])
    dx_up[...] = mm_tn(high, pick[:, slots:]).astype(bf16)
    grad_out[...] = grad_s[...]


def compute(n, ranges, weights, tok, cot, tok_up, cot_up, layers):
    d, slots = tok.shape
    hidden_units = 4 * d
    rows = IMAGES_HERE * ROWS
    tall = d + BLOCK
    wide = 12 * d
    args = list(weights) + [tok, cot, tok_up, cot_up]
    outs = [jax.ShapeDtypeStruct((layers, tall, wide), bf16)]
    outs += [
        jax.ShapeDtypeStruct((d, slots), kind) for kind in (bf16, bf16, f32, bf16)
    ]
    vm = pl.BlockSpec(memory_space=pltpu.VMEM)
    return pl.pallas_call(
        functools.partial(compute_kernel, n, layers, d, hidden_units),
        out_shape=tuple(outs),
        in_specs=[pl.BlockSpec(memory_space=pltpu.SMEM)] + [vm] * len(args),
        out_specs=(vm,) * len(outs),
        scratch_shapes=[
            pltpu.VMEM((layers, tall, wide), bf16),
            pltpu.VMEM((layers, d, hidden_units), bf16),
            pltpu.VMEM((layers, hidden_units, d), bf16),
            pltpu.VMEM((layers, rows, d), f32),
            pltpu.VMEM((layers, rows, d), bf16),
            pltpu.VMEM((layers, rows, 3 * d), bf16),
            pltpu.VMEM((layers, IMAGES_HERE, d // HD, ROWS, ROWS), f32),
            pltpu.VMEM((layers, rows, d), bf16),
            pltpu.VMEM((layers, rows, d), f32),
            pltpu.VMEM((layers, rows, d), bf16),
            pltpu.VMEM((layers, rows, hidden_units), f32),
            pltpu.VMEM((layers, rows, hidden_units), bf16),
            pltpu.VMEM((layers, 2, rows, 1), f32),
            pltpu.VMEM((rows, 3 * d), bf16),
            pltpu.VMEM((rows, d), bf16),
            pltpu.VMEM((layers, tall, wide), bf16),
            pltpu.VMEM((hidden_units, hidden_units), bf16),
        ],
        compiler_params=pltpu.CompilerParams(vmem_limit_bytes=vmem_bytes),
        name="two_layers",
    )(ranges, *args)


def rows_of(flats, d):
    w_in, w_out, w_one, w_two = flats
    layers = w_in.shape[0]
    return jnp.concatenate(
        [
            w_in.reshape(layers, -1, 3 * d),
            w_out.reshape(layers, -1, d),
            w_one.reshape(layers, -1, 4 * d),
            w_two.reshape(layers, -1, 4 * d),
        ],
        axis=2,
    )


def flats_of(block, d):
    layers = block.shape[0]
    ends = (0, 3 * d, 4 * d, 8 * d, 12 * d)
    return [block[:, :, lo:hi].reshape(layers, -1) for lo, hi in zip(ends, ends[1:])]


def local_other(tokens, ranges, attn_in, attn_out, mlp_in, mlp_out, vectors, cotangent):
    n = lax.axis_size("dev")
    slots, d = tokens.shape
    layers, part = vectors.shape
    tokens, cotangent = tokens.T, cotangent.T
    flats = (attn_in, attn_out, mlp_in, mlp_out)
    whole = [
        jnp.stack([lax.all_gather(flat[l], "dev", axis=0, tiled=True) for l in range(layers)])
        for flat in flats + (vectors,)
    ]
    line = whole.pop()
    spare = jnp.zeros((layers, BLOCK - 1, 12 * d), bf16)
    block = jnp.concatenate([rows_of(whole, d), line[:, None, :], spare], axis=1)
    down = [(i, (i + n - 1) % n) for i in range(n)]
    tok_up, cot_up = lax.ppermute(tokens, "dev", down), lax.ppermute(cotangent, "dev", down)
    grad, act, act_up, dx, dx_up = compute(
        n, ranges, (block,), tokens, cotangent, tok_up, cot_up, layers
    )
    up = [(i, (i + 1) % n) for i in range(n)]
    act = act + lax.ppermute(act_up, "dev", up)
    dx = dx + lax.ppermute(dx_up, "dev", up)
    terms = flats_of(grad[:, :d], d) + [grad[:, d]]
    grads = [
        jnp.stack([
            lax.psum_scatter(term[l].astype(f32), "dev", scatter_dimension=0, tiled=True)
            for l in range(layers)
        ])
        for term in terms
    ]
    return (act.T, dx.T, *grads)


def solution(mesh):
    flat = P(None, "dev")
    rows = P("dev", None)

    def local(*args):
        n = lax.axis_size("dev")
        slots, d = args[0].shape
        layers = args[2].shape[0]
        fast = n == 32 and d == 6 * n and layers == 2 and slots == 256
        return local_fused(*args) if fast else local_other(*args)

    return jax.shard_map(
        local,
        mesh=mesh,
        in_specs=(rows, P(), flat, flat, flat, flat, flat, rows),
        out_specs=(rows, rows, flat, flat, flat, flat, flat),
        check_vma=False,
    )
```

```python
import functools
import math

import jax
import jax.numpy as jnp
from jax import lax
from jax.experimental import pallas as pl
from jax.experimental.pallas import tpu as pltpu
from jax.sharding import PartitionSpec as P

HD = 64
IMG_LEN = 197
ROWS = 208
IMAGES_HERE = 2
BLOCK = 16
MESH_ID = pl.DeviceIdType.MESH
bf16, f32 = jnp.bfloat16, jnp.float32
eps_norm = 1e-06
masked_fill = -1e30
vmem_bytes = 56 * 2**20


def mm(a, b):
    return jnp.dot(a, b, preferred_element_type=f32)


def mm_nt(a, b):
    return lax.dot_general(a, b, (((1,), (1,)), ((), ())), preferred_element_type=f32)


def mm_tn(a, b):
    return lax.dot_general(a, b, (((0,), (0,)), ((), ())), preferred_element_type=f32)


def norm_forward(x, gain, bias):
    centered = x - jnp.mean(x, axis=-1, keepdims=True)
    inverse = lax.rsqrt(jnp.mean(centered * centered, axis=-1, keepdims=True) + eps_norm)
    hat = centered * inverse
    return (hat * gain + bias).astype(bf16), hat, inverse


def norm_backward(dh, hat, inverse, gain):
    scaled = dh * gain
    dv = inverse * (
        scaled
        - jnp.mean(scaled, axis=-1, keepdims=True)
        - hat * jnp.mean(scaled * hat, axis=-1, keepdims=True)
    )
    return dv, rows_sum(dh * hat), rows_sum(dh)


def rows_sum(x):
    return jnp.sum(x, axis=0, keepdims=True)


def remote(src, dst, send, recv, dev):
    return pltpu.make_async_remote_copy(
        src_ref=src, dst_ref=dst, send_sem=send, recv_sem=recv,
        device_id=(dev,), device_id_type=MESH_ID,
    )


class Place:
    def __init__(self, n):
        self.n = n
        me = self.me = lax.axis_index("dev")
        self.bits = [lax.rem(lax.div(me, 2**b), 2) for b in range(5)]
        self.c, self.x, self.y = self.bits[:3]
        self.z = lax.div(me, 8)
        self.core = self.flip(0)
        self.along_z = [self.flip(3), self.flip(4), self.flip(3, 4)]
        self.along_xy = [self.flip(1), self.flip(2), self.flip(1, 2)]
        self.chips = [self.flip(*[b + 1 for b in range(4) if m >> b & 1]) for m in range(1, 16)]
        self.up, self.down = lax.rem(me + 1, n), lax.rem(me + n - 1, n)

    def flip(self, *which):
        return self.me + sum((1 - 2 * self.bits[b]) * 2**b for b in which)

    def peers(self):
        return [self.core] + self.chips + [self.up, self.down]


def taken(ref, sem):
    pltpu.make_async_copy(ref, ref, sem).wait()


class Sender:
    def go(self, src, dst, k, dev):
        remote(src, dst, self.send.at[k], self.recv.at[k], dev).start()

    def arrived(self, k):
        taken(self.size_of[k], self.recv.at[k])

    def left(self):
        for k, ref in enumerate(self.size_of):
            if ref is not None:
                taken(ref, self.send.at[k])


class Gather(Sender):
    def __init__(self, place, buf, room, send, recv):
        self.place, self.buf, self.send, self.recv = place, buf, send, recv
        three, nine = buf.at[pl.ds(0, 3), 0, 0, 0], room.at[:, pl.ds(1, 3)]
        self.size_of = [three, three, nine, buf.at[:, :, :, 0]]

    def begin(self):
        p = self.place
        own = self.buf.at[0, p.y, p.x, p.c]
        for k, dev in enumerate(p.along_z):
            self.go(own, self.buf.at[k + 1, p.y, p.x, p.c], 0, dev)
        for dev in p.along_xy:
            self.go(own, own, 1, dev)

    def middle(self):
        p = self.place
        self.arrived(0)
        got = self.buf.at[pl.ds(1, 3), p.y, p.x, p.c]
        for dev in p.along_xy:
            self.go(got, got, 2, dev)

    def core(self):
        p = self.place
        self.arrived(1)
        self.arrived(2)
        half = self.buf.at[:, :, :, p.c]
        self.go(half, half, 3, p.core)

    def done(self):
        self.arrived(3)


class GatherAcross(Gather):
    def __init__(self, place, buf, room, send, recv):
        super().__init__(place, buf, room, send, recv)
        self.size_of = [room, self.size_of[1], None, self.size_of[3]]

    def begin(self):
        p = self.place
        own = self.buf.at[0, p.y, p.x, p.c]
        for dev in p.along_xy:
            self.go(own, own, 1, dev)

    def middle(self):
        self.arrived(1)
        c = self.place.c
        for k, dev in enumerate(self.place.along_z):
            self.go(self.buf.at[0, :, :, c], self.buf.at[k + 1, :, :, c], 0, dev)

    def core(self):
        p = self.place
        self.arrived(0)
        half = self.buf.at[:, :, :, p.c]
        self.go(half, half, 3, p.core)


class Scatter(Sender):
    def __init__(self, place, grads, half, out_xy, in_xy, out_z, in_z, send, recv, out):
        self.place, self.grads, self.half = place, grads, half
        self.out_xy, self.in_xy, self.out_z, self.in_z = out_xy, in_xy, out_z, in_z
        self.send, self.recv, self.out = send, recv, out
        self.size_of = self.sizes()

    def sizes(self):
        return [self.half, self.in_xy.at[:, pl.ds(1, 3)], self.in_xy.at[:, 0], self.in_z]

    def begin(self):
        p = self.place
        self.go(self.grads.at[:, :, :, 1 - p.c], self.half, 0, p.core)

    def pair(self):
        self.arrived(0)
        self.out_xy[...] = (
            self.grads[:, :, :, self.place.c].astype(f32) + self.half[...].astype(f32)
        ).astype(bf16)

    def middle(self):
        p = self.place
        self.pair()
        goals = [(p.y, 1 - p.x), (1 - p.y, p.x), (1 - p.y, 1 - p.x)]
        for k, (y, x) in enumerate(goals):
            self.go(self.out_xy.at[pl.ds(1, 3), y, x], self.in_xy.at[k, pl.ds(1, 3)], 1, p.along_xy[k])
        for k, (y, x) in enumerate(goals):
            self.go(self.out_xy.at[0, y, x], self.in_xy.at[k, 0], 2, p.along_xy[k])

    def ours(self, z):
        p = self.place
        return self.grads[z, p.y, p.x, p.c].astype(f32) + self.half[z, p.y, p.x].astype(f32)

    def end(self):
        p = self.place
        self.arrived(1)
        for z in range(1, 4):
            total = self.ours(z)
            for k in range(3):
                total += self.in_xy[k, z].astype(f32)
            self.out_z[z - 1] = total.astype(bf16)
            self.go(self.out_z.at[z - 1], self.in_z.at[z - 1], 3, p.along_z[z - 1])

    def done(self):
        self.arrived(2)
        total = self.ours(0)
        for k in range(3):
            total += self.in_xy[k, 0].astype(f32)
        self.arrived(3)
        for k in range(3):
            total += self.in_z[k].astype(f32)
        self.out[...] = total


class ScatterAcross(Scatter):
    def sizes(self):
        return [self.half, self.in_xy, None, self.in_z]

    def middle(self):
        self.pair()
        for k, dev in enumerate(self.place.along_z):
            self.go(self.out_xy.at[k + 1], self.in_xy.at[k], 1, dev)

    def end(self):
        p = self.place
        self.arrived(1)
        total = self.grads[0, :, :, p.c].astype(f32) + self.half[0].astype(f32)
        for k in range(3):
            total += self.in_xy[k].astype(f32)
        self.out_xy[0] = total.astype(bf16)
        for k, (y, x) in enumerate([(p.y, 1 - p.x), (1 - p.y, p.x), (1 - p.y, 1 - p.x)]):
            self.go(self.out_xy.at[0, y, x], self.in_z.at[k], 3, p.along_xy[k])

    def done(self):
        p = self.place
        total = self.ours(0)
        for k in range(3):
            total += self.in_xy[k, p.y, p.x].astype(f32)
        self.arrived(3)
        for k in range(3):
            total += self.in_z[k].astype(f32)
        self.out[...] = total


class Direct(Scatter):
    def sizes(self):
        return [self.half, self.in_xy]

    def middle(self):
        p = self.place
        self.pair()
        for m, dev in enumerate(p.chips, 1):
            y = 1 - p.y if m & 2 else p.y
            x = 1 - p.x if m & 1 else p.x
            self.go(self.out_xy.at[m >> 2, y, x], self.in_xy.at[m - 1], 1, dev)

    def done(self):
        total = self.ours(0)
        self.arrived(1)
        for k in range(15):
            total += self.in_xy[k].astype(f32)
        self.out[...] = total


def natural(c, z):
    return jnp.where((c & 7) < 6, 6 * ((c >> 3) ^ (8 * z)) + (c & 7), -1)


def iota(shape, dim):
    return lax.broadcasted_iota(jnp.int32, shape, dim)


def norm_padded(x, gain, bias, real, d):
    centered = (x - jnp.sum(x, axis=-1, keepdims=True) * (1.0 / d)) * real
    inverse = lax.rsqrt(jnp.sum(centered * centered, axis=-1, keepdims=True) * (1.0 / d) + eps_norm)
    hat = centered * inverse
    return (hat * gain + bias).astype(bf16), hat, inverse


def norm_padded_back(dh, hat, inverse, gain, d):
    scaled = dh * gain
    dv = inverse * (
        scaled
        - jnp.sum(scaled, axis=-1, keepdims=True) * (1.0 / d)
        - hat * (jnp.sum(scaled * hat, axis=-1, keepdims=True) * (1.0 / d))
    )
    return dv, rows_sum(dh * hat), rows_sum(dh)


def sublanes(x, shift):
    return pltpu.roll(x, shift, 1)


def unfold(tiles, s):
    a, b, c = tiles
    return jnp.where(s < 2, sublanes(a, 2), jnp.where(s < 4, sublanes(b, 4), sublanes(c, 6)))


def fold(tiles, extra, s):
    return [jnp.where(s < 6, t, sublanes(extra, 6 - 2 * k)) for k, t in enumerate(tiles)]


def fused_kernel(n, layers, d, ranges, *refs):
    refs = list(refs)
    take = lambda count: [refs.pop(0) for _ in range(count)]
    tok, cot, a_in, a_out, m_in, m_out, vecs = take(7)
    reds, (act_out, dx_out) = take(3), take(2)
    wires, grads, halves, outxys, inxys, outzs, inzs = [take(3) for _ in range(7)]
    in_direct, in_across = take(2)
    tok_near, cot_near, act_near, act_in, dx_near, dx_in = take(6)
    w_in_s, w_one_s, w_out_s, w_two_s, two_s, g_two_s = take(6)
    pick_s, x_s, dx_s, ds_s = take(4)
    vec_n, vec_g, b_one_s, line_n, line_g = take(5)
    hat1_s, h1_s, qkv_s, p_s, o_s, hat2_s, h2_s, slope_s, a_s, inv_s = take(10)
    dqkv_s, do_s, pack_a, pack_b, pack_c, flat_ai, flat_ao, flat_mi, flat_mo, vec_s = take(10)
    gsend, grecv, ssend, srecv, hsend, hrecv = take(6)
    wire_a, wire_b, wire_c = wires
    slots = tok.shape[1]
    heads = d // HD
    wide = 8 * n
    hidden_units = 4 * d
    rows = IMAGES_HERE * ROWS
    place = Place(n)
    me = place.me

    barrier = pltpu.get_barrier_semaphore()
    for other in place.peers():
        pl.semaphore_signal(barrier, inc=1, device_id=(other,), device_id_type=MESH_ID)

    part = vecs.shape[1]
    here = (0, place.y, place.x, place.c)
    z_of = [place.z] + [lax.div(dev, 8) for dev in place.along_z]
    vec_s[...] = jnp.zeros_like(vec_s)
    vec_s[0:layers, 0:part] = vecs[...].astype(f32)
    moved = pltpu.roll(vec_s[...], 8 * lax.rem(me, 8), 1)
    vec_s[...] = moved
    flat_ai[...] = a_in[...].astype(f32)
    flat_mo[...] = m_out[...].astype(f32)
    pack_b[...] = jnp.zeros_like(pack_b)

    def pack_first(l):
        row = slice(l, l + 1)
        for r in range(6):
            base, k, i = r * 3 * d, r // 2, r % 2
            pack_a[r:r + 1, :] = flat_ai[row, base:base + 256]
            pack_a[8 + r:9 + r, :128] = flat_ai[row, base + 256:base + 384]
            low, lanes = 6 + i + (8 if k == 2 else 0), slice(128 * (k % 2), 128 * (k % 2) + 128)
            pack_a[low:low + 1, lanes] = flat_ai[row, base + 384:base + 512]
            pack_a[8 + r:9 + r, 128:192] = flat_ai[row, base + 512:base + 576]
        pack_a[14:15, 128:192] = vec_s[row, :64]
        pack_a[15:16, 128:192] = vec_s[row, 64:128]
        for r in range(8):
            pack_a[8 + r:9 + r, 192:] = flat_mo[row, (16 + r) * d + 128:(17 + r) * d]
        wire_a[(l,) + here] = pack_a[...].astype(bf16)

    def pack_second(l):
        row = slice(l, l + 1)
        for r in range(6):
            base, k, i = r * 4 * d, r // 2, r % 2
            lanes = slice(128 * k, 128 * k + 128)
            pack_b[r:r + 1, :] = flat_mi[row, base:base + 384]
            pack_b[6 + i:7 + i, lanes] = flat_mi[row, base + 384:base + 512]
            pack_b[8 + r:9 + r, :256] = flat_mi[row, base + 512:base + 768]
            pack_b[8 + r:9 + r, 256:] = flat_ao[row, r * d:r * d + 128]
            pack_b[14 + i:15 + i, 128 * k:128 * k + 64] = flat_ao[row, r * d + 128:(r + 1) * d]
        wire_b[(l,) + here] = pack_b[...].astype(bf16)

    def pack_third(l):
        row = slice(l, l + 1)
        for r in range(24):
            g, i = r // 8, r % 8
            low, lane = i + (8 if g == 2 else 0), 128 * (g % 2)
            pack_c[low:low + 1, lane:lane + 128] = flat_mo[row, r * d:r * d + 128]
            if g < 2:
                pack_c[8 + i:9 + i, 128 + 64 * g:192 + 64 * g] = flat_mo[row, r * d + 128:(r + 1) * d]
        wire_c[(l,) + here] = pack_c[...].astype(bf16)

    across = [(1, 2)]
    gathers = [
        [
            (GatherAcross if (l, k) in across else Gather)(
                place, wires[k].at[l], inxys[k].at[l], gsend.at[l, k], grecv.at[l, k]
            )
            for k in range(3)
        ]
        for l in range(layers)
    ]
    scatters = [
        [
            (Direct if k == 0 and l == 0 else ScatterAcross if (l, k) in across else Scatter)(
                place, grads[k].at[l], halves[k].at[l], outxys[k].at[l],
                in_direct if k == 0 and l == 0 else in_across if (l, k) in across else inxys[k].at[l],
                outzs[k].at[l], inzs[k].at[l], ssend.at[l, k], srecv.at[l, k], reds[k].at[l],
            )
            for k in range(3)
        ]
        for l in range(layers)
    ]
    side = slots // 2
    first_half, second_half = pl.ds(0, side), pl.ds(side, side)

    def pair(src, dst, at):
        return [
            remote(src.at[:, a], dst.at[:, b], hsend.at[at + i], hrecv.at[at + i], dev)
            for i, (a, b, dev) in enumerate((
                (first_half, first_half, place.down), (second_half, second_half, place.up),
            ))
        ]

    tok_halo, cot_halo = pair(tok, tok_near, 0), pair(cot, cot_near, 2)
    back = lambda src, dst, at: [
        remote(src.at[:, first_half], dst.at[:, first_half], hsend.at[at], hrecv.at[at], place.up),
        remote(src.at[:, second_half], dst.at[:, second_half], hsend.at[at + 1], hrecv.at[at + 1], place.down),
    ]
    act_halo, dx_halo = back(act_near, act_in, 4), back(dx_near, dx_in, 6)
    (ga0, gb0, gc0), (ga1, gb1, gc1) = gathers
    (sa0, sb0, sc0), (sa1, sb1, sc1) = scatters

    pack_first(0)
    pl.semaphore_wait(barrier, len(place.peers()))
    ga0.begin()
    for copy in tok_halo:
        copy.start()
    flat_ao[...] = a_out[...].astype(f32)
    flat_mi[...] = m_in[...].astype(f32)
    pack_second(0)
    gb0.begin()
    pack_third(0)
    gc0.begin()
    pack_first(1)
    ga1.begin()
    pack_second(1)
    gb1.begin()
    pack_third(1)
    gc1.begin()
    for copy in cot_halo:
        copy.start()

    lane = iota((1, wide), 1)
    real = jnp.where((lane & 7) < 6, 1.0, 0.0)
    spread = jnp.where(iota((d, wide), 0) == natural(iota((1, wide), 1), place.z), 1.0, 0.0).astype(bf16)
    owner = (lane >> 3) ^ (8 * place.z)
    window = jnp.where((lane & 7) >= 6, owner + (owner >> 3) + (lane & 1), -1)
    windows = [
        jnp.where(3 * iota((BLOCK, wide), 0) + k == window, 1.0, 0.0).astype(bf16) for k in range(3)
    ]
    sub = iota((1, 8, 1), 1)

    first, last, below = ranges[0, me], ranges[1, me], ranges[0, place.down]
    total = ranges[1, n - 1]
    centre = IMG_LEN // 2
    image = (first + IMG_LEN - 1 - centre) // IMG_LEN
    picks, valid_keys = [], []
    for k in range(IMAGES_HERE):
        begin = (image + k) * IMG_LEN
        mine = (begin < total) & (jnp.minimum(begin + centre, total - 1) < last)
        count = jnp.where(mine, jnp.minimum(IMG_LEN, total - begin), 0)
        r = iota((ROWS, 2 * slots), 0)
        c = iota((ROWS, 2 * slots), 1)
        t = begin + r
        column = jnp.where(
            t < first, t - below + slots, jnp.where(t < last, t - first, t - last + slots)
        )
        column = jnp.where(r < count, column, -1)
        picks.append(jnp.where(column == c, 1.0, 0.0).astype(bf16))
        valid_keys.append(iota((ROWS, ROWS), 1) < count)
    pick = jnp.concatenate(picks, axis=0)
    x = mm_nt(pick[:, :slots], mm_tn(spread, tok[...]).astype(bf16))

    ga0.middle()
    gb0.middle()
    gc0.middle()
    ga0.core()
    gc1.middle()
    ga1.middle()
    gb1.middle()
    for copy in tok_halo:
        copy.wait_recv()
    x += mm_nt(pick[:, slots:], mm_tn(spread, tok_near[...]).astype(bf16))
    dx = mm_nt(pick[:, :slots], mm_tn(spread, cot[...]).astype(bf16))
    pick_s[...] = pick
    dx_s[...] = dx

    def add_near():
        for copy in cot_halo:
            copy.wait_recv()
        dx_s[...] += mm_nt(pick_s[:, slots:], mm_tn(spread, cot_near[...]).astype(bf16))


    def tiles_of(wire, l):
        v = wire[l]
        width = v.shape[-1]
        v = v.reshape(n * BLOCK, width).astype(f32).reshape(n, 2, 8, width)
        return [v[:, i, :, k:k + 128] for i in range(2) for k in range(0, width, 128)]

    def flat(t):
        return t.reshape(wide, t.shape[-1]).astype(bf16)

    def unpack_a(l):
        t0, t1, t2, t4 = tiles_of(wire_a, l)
        for k, t in enumerate((t0, t1, t2, unfold((t0, t1, t2), sub), t4)):
            w_in_s[l, :, 128 * k:128 * k + 128] = flat(t)
        t4 = flat(t4)
        lines = jnp.concatenate([mm(each, t4)[:, :64] for each in windows], axis=1)
        vec_n[l] = lines
        vec_g[l] = mm(lines.astype(bf16), spread)
        for k in range(4):
            b_one_s[l, 0:1, k * d:(k + 1) * d] = lines[8 + k:9 + k]

    def unpack_b(l):
        t0, t1, t2, t4, t5, t6 = tiles_of(wire_b, l)
        for k, t in enumerate((t0, t1, t2, unfold((t0, t1, t2), sub), t4, t5)):
            w_one_s[l, :, 128 * k:128 * k + 128] = flat(t)
        t7 = unfold((t4, t5, t6), sub)
        out = jnp.concatenate([flat(t6), flat(t7)], axis=1)
        out = mm(spread, out)[:, :d].astype(bf16)
        w_out_s[l] = mm(out, spread).astype(bf16)

    def unpack_c(l):
        t0, t1, t2, t3 = tiles_of(wire_c, l)
        last = tiles_of(wire_a, l)[3]
        side = pltpu.roll(t3, 64, 2), pltpu.roll(last, 64, 2)
        pile = lambda ts: jnp.stack(ts, axis=1).reshape(4, d, 128).astype(bf16)
        left, right = pile((t0, t1, t2)), pile((t3,) + side)
        for k in range(4):
            at = pl.ds(pl.multiple_of(z_of[k] * d, BLOCK), d)
            two_s[at, :128] = left[k]
            two_s[at, 128:] = right[k]
        w_two_s[l] = mm(two_s[:, :d], spread).astype(bf16)

    beats = [
        [lambda: None, lambda: None, lambda: (gb0.core(), add_near()), lambda: gc0.core(), lambda: ga1.core()],
        [lambda: gb1.core(), lambda: gc1.core(), lambda: None, lambda: None, lambda: None],
    ]
    for l in range(layers):
        ga, gb, gc = gathers[l]
        ga.done()
        unpack_a(l)
        h, hat, inv = norm_padded(x, vec_g[l, 0:1], vec_g[l, 1:2], real, d)
        hat1_s[l], h1_s[l], inv_s[l, 0] = hat, h, inv
        projected = mm(h, w_in_s[l, :, :3 * d])
        qkv_s[l, :, :d] = ((projected[:, :d] + vec_n[l, 2:3]).astype(bf16).astype(f32)
                           * (1.0 / math.sqrt(HD))).astype(bf16)
        qkv_s[l, :, d:2 * d] = projected[:, d:2 * d].astype(bf16)
        qkv_s[l, :, 2 * d:] = (projected[:, 2 * d:] + vec_n[l, 3:4]).astype(bf16)
        beats[l][0]()
        parts = [(i, head) for i in range(IMAGES_HERE) for head in range(heads)]
        at_of = lambda i: slice(i * ROWS, (i + 1) * ROWS)
        lanes = lambda group, head: slice(group * d + head * HD, group * d + (head + 1) * HD)
        for i, head in parts:
            scores = mm_nt(qkv_s[l, at_of(i), lanes(0, head)], qkv_s[l, at_of(i), lanes(1, head)])
            scores = jnp.where(valid_keys[i], scores, masked_fill)
            e = jnp.exp(scores - jnp.max(scores, axis=-1, keepdims=True))
            p = e * (1.0 / jnp.sum(e, axis=-1, keepdims=True))
            p_s[l, i, head] = p
            ds_s[i, head] = p.astype(bf16)
        beats[l][1]()
        for i, head in parts:
            o_s[l, at_of(i), lanes(0, head)] = mm(
                ds_s[i, head], qkv_s[l, at_of(i), lanes(2, head)]
            ).astype(bf16)
        beats[l][2]()
        gb.done()
        beats[l][3]()
        unpack_b(l)
        x1 = x + (mm(o_s[l], w_out_s[l]) + vec_g[l, 4:5])
        h2, hat, inv = norm_padded(x1, vec_g[l, 5:6], vec_g[l, 6:7], real, d)
        hat2_s[l], h2_s[l], inv_s[l, 1] = hat, h2, inv
        u = mm(h2, w_one_s[l]) + b_one_s[l, 0:1]
        phi = 0.5 * (1.0 + lax.erf(u * (1.0 / math.sqrt(2.0))))
        a_s[l] = (u * phi).astype(bf16)
        slope_s[l] = phi + u * (jnp.exp(-0.5 * u * u) * (1.0 / math.sqrt(2.0 * math.pi)))
        beats[l][4]()
        gc.done()
        unpack_c(l)
        x = x1 + (mm(a_s[l], w_two_s[l]) + vec_g[l, 7:8])

    x_s[...] = x.astype(bf16)
    dx = dx_s[...]

    def cut(w, pieces):
        return [w[:, 128 * k:128 * k + 128].reshape(n, 8, 128) for k in range(pieces)]

    def block(tiles):
        half = len(tiles) // 2
        v = [jnp.concatenate(tiles[i * half:(i + 1) * half], axis=-1)[:, None] for i in range(2)]
        v = jnp.concatenate(v, axis=1).reshape(n * BLOCK, 128 * half).astype(bf16)
        return v.reshape(4, 2, 2, 2, BLOCK, 128 * half)

    beats = [
        [lambda: sa1.middle(), lambda: (sc0.middle(), sc1.end()),
         lambda: (sb1.end(), sb0.middle()), lambda: None],
        [lambda: None, lambda: sc1.middle(), lambda: sb1.middle(), lambda: None],
    ]
    dqkv_s[:, 3 * d:] = jnp.zeros((rows, d), bf16)
    low_lanes = iota((1, 1, 128), 2) < 64
    line_g[...] = jnp.zeros_like(line_g)
    line_n[...] = jnp.zeros_like(line_n)
    for l in reversed(range(layers)):
        sa, sb, sc = scatters[l]
        dm = dx.astype(bf16)
        line_g[7:8] = rows_sum(dm.astype(f32))
        g_two_s[...] = mm_tn(a_s[l], mm_nt(dm, spread).astype(bf16))
        g_two = jnp.concatenate(
            [g_two_s[pl.ds(pl.multiple_of(z * d, BLOCK), d), :] for z in z_of], axis=0
        ).reshape(n, 3, 8, d)
        side = jnp.concatenate([g_two[..., 128:], jnp.zeros((n, 3, 8, 256 - d), f32)], axis=-1)
        turned = pltpu.roll(side[:, 1], 64, 2)
        tail = pltpu.roll(side[:, 2], 64, 2)
        grads[2][l] = block([g_two[:, 0, :, :128], g_two[:, 1, :, :128], g_two[:, 2, :, :128],
                             jnp.where(low_lanes, side[:, 0], turned)])
        sc.begin()
        du = (mm_nt(dm, w_two_s[l]) * slope_s[l]).astype(bf16)
        beats[l][0]()
        g_b1 = rows_sum(du.astype(f32))
        for k in range(4):
            line_n[8 + k:9 + k] = g_b1[:, k * d:(k + 1) * d]
        dh2 = mm_nt(du, w_one_s[l])
        dv, g_g2, g_c2 = norm_padded_back(dh2, hat2_s[l], inv_s[l, 1], vec_g[l, 5:6], d)
        line_g[5:6], line_g[6:7] = g_g2, g_c2
        dx1 = dx + dv
        db = dx1.astype(bf16)
        line_g[4:5] = rows_sum(db.astype(f32))
        g_out = mm_tn(o_s[l], mm_nt(db, spread).astype(bf16))
        g_out = jnp.concatenate([g_out, jnp.zeros((d, 256 - d), f32)], axis=1).astype(bf16)
        t6, t7 = cut(mm_tn(spread, g_out), 2)
        t0, t1, t2, t3, t4, t5 = cut(mm_tn(h2_s[l], du), 6)
        grads[1][l] = block(fold((t0, t1, t2), t3, sub) + fold((t4, t5, t6), t7, sub))
        beats[l][1]()
        sb.begin()
        do_s[...] = mm_nt(db, w_out_s[l]).astype(bf16)
        parts = [(i, head) for i in range(IMAGES_HERE) for head in range(heads)]
        at_of = lambda i: slice(i * ROWS, (i + 1) * ROWS)
        lanes = lambda group, head: slice(group * d + head * HD, group * d + (head + 1) * HD)
        for i, head in parts:
            p = p_s[l, i, head]
            dp = mm_nt(do_s[at_of(i), lanes(0, head)], qkv_s[l, at_of(i), lanes(2, head)])
            ds_s[i, head] = (p * (dp - jnp.sum(p * dp, axis=-1, keepdims=True))).astype(bf16)
        beats[l][2]()
        for i, head in parts:
            at = at_of(i)
            ds = ds_s[i, head]
            dqkv_s[at, lanes(0, head)] = (
                mm(ds, qkv_s[l, at, lanes(1, head)]) * (1.0 / math.sqrt(HD))
            ).astype(bf16)
            dqkv_s[at, lanes(1, head)] = mm_tn(ds, qkv_s[l, at, lanes(0, head)]).astype(bf16)
            dqkv_s[at, lanes(2, head)] = mm_tn(
                p_s[l, i, head].astype(bf16), do_s[at, lanes(0, head)]
            ).astype(bf16)
        beats[l][3]()
        dqkv = dqkv_s[:, :640]
        line_n[2:3] = rows_sum(dqkv_s[:, :d].astype(f32))
        line_n[3:4] = rows_sum(dqkv_s[:, 2 * d:3 * d].astype(f32))
        dh = mm_nt(dqkv, w_in_s[l])
        dv, g_g1, g_c1 = norm_padded_back(dh, hat1_s[l], inv_s[l, 0], vec_g[l, 0:1], d)
        line_g[0:1], line_g[1:2] = g_g1, g_c1
        lines = (line_n[...] + mm_nt(line_g[...].astype(bf16), spread)).astype(bf16)
        vec_rows = sum(mm_tn(windows[k], lines[:, 64 * k:64 * k + 64]) for k in range(3))
        vec_rows = jnp.concatenate([vec_rows, jnp.zeros((wide, 64), f32)], axis=1).reshape(n, 8, 128)
        t0, t1, t2, t3, t4 = cut(mm_tn(h1_s[l], dqkv), 5)
        t4 = jnp.where(low_lanes, t4 + vec_rows, tail)
        grads[0][l] = block(fold((t0, t1, t2), t3, sub) + [t4])
        sa.begin()
        dx = dx1 + dv

    high = dx.astype(bf16)
    low = (dx - high.astype(f32)).astype(bf16)
    high = mm_nt(high, spread).astype(bf16)
    dx_near[...] = mm_tn(high, pick_s[:, slots:]).astype(bf16)
    for copy in dx_halo:
        copy.start()
    sa1.end()
    sa0.middle()
    x_low = mm_nt(x_s[...], spread).astype(bf16)
    act_near[...] = mm_tn(x_low, pick_s[:, slots:]).astype(bf16)
    for copy in act_halo:
        copy.start()
    sc0.end()
    low = mm_nt(low, spread).astype(bf16)
    dx_own = mm_tn(high, pick_s[:, :slots]) + mm_tn(low, pick_s[:, :slots])
    act_own = mm_tn(x_low, pick_s[:, :slots]).astype(bf16)
    sb0.end()
    sc1.done()
    sb1.done()
    for copy in dx_halo:
        copy.wait_recv()
    dx_out[...] = dx_own + dx_in[...].astype(f32)
    for copy in act_halo:
        copy.wait_recv()
    act_out[...] = act_own + act_in[...]
    sa1.done()
    sc0.done()
    sa0.done()
    sb0.done()
    for copy in tok_halo + cot_halo + act_halo + dx_halo:
        copy.wait_send()
    for group in gathers + scatters:
        for each in group:
            each.left()


def fused(n, ranges, tok, cot, flats):
    d, slots = tok.shape
    layers = flats[0].shape[0]
    wide = 8 * n
    hidden_units = 4 * d
    rows = IMAGES_HERE * ROWS
    shapes = ((BLOCK, 256), (BLOCK, 384), (BLOCK, 256))
    boxes = lambda lead, kind: [pltpu.VMEM((layers,) + lead + s, kind) for s in shapes]
    vm = pl.BlockSpec(memory_space=pltpu.VMEM)
    scratch = (
        boxes((4, 2, 2, 2), bf16) + boxes((4, 2, 2, 2), bf16)
        + boxes((4, 2, 2), bf16) + boxes((4, 2, 2), bf16) + boxes((3, 4), bf16)
        + boxes((3,), bf16) + boxes((3,), bf16)
        + [pltpu.VMEM((15,) + shapes[0], bf16), pltpu.VMEM((3, 2, 2) + shapes[2], bf16)]
        + [pltpu.VMEM((d, slots), bf16)] * 6
        + [
            pltpu.VMEM((layers, wide, 640), bf16),
            pltpu.VMEM((layers, wide, hidden_units), bf16),
            pltpu.VMEM((layers, d, wide), bf16),
            pltpu.VMEM((layers, hidden_units, wide), bf16),
            pltpu.VMEM((hidden_units, 256), bf16),
            pltpu.VMEM((hidden_units, d), f32),
            pltpu.VMEM((rows, 2 * slots), bf16),
            pltpu.VMEM((rows, wide), bf16),
            pltpu.VMEM((rows, wide), f32),
            pltpu.VMEM((IMAGES_HERE, d // HD, ROWS, ROWS), bf16),
            pltpu.VMEM((layers, BLOCK, d), f32),
            pltpu.VMEM((layers, BLOCK, wide), f32),
            pltpu.VMEM((layers, 8, hidden_units), f32),
            pltpu.VMEM((BLOCK, d), f32),
            pltpu.VMEM((BLOCK, wide), f32),
            pltpu.VMEM((layers, rows, wide), f32),
            pltpu.VMEM((layers, rows, wide), bf16),
            pltpu.VMEM((layers, rows, 3 * d), bf16),
            pltpu.VMEM((layers, IMAGES_HERE, d // HD, ROWS, ROWS), f32),
            pltpu.VMEM((layers, rows, d), bf16),
            pltpu.VMEM((layers, rows, wide), f32),
            pltpu.VMEM((layers, rows, wide), bf16),
            pltpu.VMEM((layers, rows, hidden_units), f32),
            pltpu.VMEM((layers, rows, hidden_units), bf16),
            pltpu.VMEM((layers, 2, rows, 1), f32),
            pltpu.VMEM((rows, 4 * d), bf16),
            pltpu.VMEM((rows, d), bf16),
        ]
        + [pltpu.VMEM(s, f32) for s in shapes]
        + [pltpu.VMEM(f.shape, f32) for f in flats[:4]]
        + [pltpu.VMEM((8, 128), f32)]
        + [pltpu.SemaphoreType.DMA((layers, 3, 4))] * 4
        + [pltpu.SemaphoreType.DMA((8,))] * 2
    )
    return pl.pallas_call(
        functools.partial(fused_kernel, n, layers, d),
        out_shape=tuple(jax.ShapeDtypeStruct((layers,) + s, f32) for s in shapes)
        + (jax.ShapeDtypeStruct((d, slots), bf16), jax.ShapeDtypeStruct((d, slots), f32)),
        in_specs=[pl.BlockSpec(memory_space=pltpu.SMEM)] + [vm] * 7,
        out_specs=(vm,) * 5,
        scratch_shapes=scratch,
        compiler_params=pltpu.CompilerParams(
            collective_id=0, has_side_effects=True, vmem_limit_bytes=vmem_bytes
        ),
        name="two_layers",
    )(ranges.T, tok, cot, *flats)


def flatten_kernel(n, layers, d, red_a, red_b, red_c, act_in, dx_in, act, dx, g_in, g_out, g_one, g_two, g_vec, vec_s):
    me = lax.axis_index("dev")
    act[...] = act_in[...]
    dx[...] = dx_in[...]
    vec_s[...] = jnp.zeros_like(vec_s)
    for l in range(layers):
        row = slice(l, l + 1)
        for r in range(6):
            k, i = r // 2, r % 2
            base = r * 3 * d
            g_in[row, base:base + 256] = red_a[l, r:r + 1, :]
            g_in[row, base + 256:base + 384] = red_a[l, 8 + r:9 + r, :128]
            low, lane = 6 + i + (8 if k == 2 else 0), 128 * (k % 2)
            g_in[row, base + 384:base + 512] = red_a[l, low:low + 1, lane:lane + 128]
            g_in[row, base + 512:base + 576] = red_a[l, 8 + r:9 + r, 128:192]
            base = r * 4 * d
            g_one[row, base:base + 384] = red_b[l, r:r + 1, :]
            g_one[row, base + 384:base + 512] = red_b[l, 6 + i:7 + i, 128 * k:128 * k + 128]
            g_one[row, base + 512:base + 768] = red_b[l, 8 + r:9 + r, :256]
            base = r * d
            g_out[row, base:base + 128] = red_b[l, 8 + r:9 + r, 256:]
            g_out[row, base + 128:base + 192] = red_b[l, 14 + i:15 + i, 128 * k:128 * k + 64]
        for r in range(24):
            g, i = r // 8, r % 8
            base, low, lane = r * d, i + (8 if g == 2 else 0), 128 * (g % 2)
            g_two[row, base:base + 128] = red_c[l, low:low + 1, lane:lane + 128]
            if g < 2:
                g_two[row, base + 128:base + 192] = red_c[l, 8 + i:9 + i, 128 + 64 * g:192 + 64 * g]
            else:
                g_two[row, base + 128:base + 192] = red_a[l, 8 + i:9 + i, 192:]
        vec_s[row, :64] = red_a[l, 14:15, 128:192]
        vec_s[row, 64:] = red_a[l, 15:16, 128:192]
    part = g_vec.shape[1]
    moved = pltpu.roll(vec_s[...], lax.rem(128 - 8 * lax.rem(me, 8), 128), 1)
    g_vec[...] = moved[0:layers, 0:part]


def local_fused(tokens, ranges, attn_in, attn_out, mlp_in, mlp_out, vectors, cotangent):
    n = lax.axis_size("dev")
    slots, d = tokens.shape
    layers, part = vectors.shape
    flats = (attn_in, attn_out, mlp_in, mlp_out, vectors)
    sums = fused(n, ranges, tokens.T, cotangent.T, flats)
    vm = pl.BlockSpec(memory_space=pltpu.VMEM)
    act, dx, *grads = pl.pallas_call(
        functools.partial(flatten_kernel, n, layers, d),
        out_shape=(
            jax.ShapeDtypeStruct((d, slots), bf16), jax.ShapeDtypeStruct((d, slots), f32),
        ) + tuple(jax.ShapeDtypeStruct(f.shape, f32) for f in flats),
        in_specs=[vm] * 5,
        out_specs=(vm,) * 7,
        scratch_shapes=[pltpu.VMEM((8, 128), f32)],
        compiler_params=pltpu.CompilerParams(vmem_limit_bytes=vmem_bytes),
        name="flatten",
    )(*sums)
    return (act.T, dx.T, *grads)


def compute_kernel(n, layers, width, hidden_units, ranges, *refs):
    refs = list(refs)
    take = lambda count: [refs.pop(0) for _ in range(count)]
    (w_full,) = take(1)
    tok, cot, tok_up, cot_up = take(4)
    (grad_out,) = take(1)
    act_own, act_up, dx_own, dx_up = take(4)
    w_all, w_one_s, w_two_s, hat1_s, h1_s, qkv_s, p_s, o_s, hat2_s, h2_s, slope_s, a_s = take(12)
    inv_s, dqkv_s, do_s, grad_s, perm = take(5)
    slots = tok.shape[1]
    heads = width // HD
    d = width
    me = lax.axis_index("dev")
    first, last = ranges[me, 0], ranges[me, 1]
    total = ranges[n - 1, 1]
    image = (first + IMG_LEN - 1) // IMG_LEN
    rows = IMAGES_HERE * ROWS

    picks, valid_keys = [], []
    for k in range(IMAGES_HERE):
        begin = (image + k) * IMG_LEN
        count = jnp.where(begin < last, jnp.minimum(IMG_LEN, total - begin), 0)
        r = lax.broadcasted_iota(jnp.int32, (ROWS, 2 * slots), 0)
        c = lax.broadcasted_iota(jnp.int32, (ROWS, 2 * slots), 1)
        t = begin + r
        column = jnp.where(t < last, t - first, t - last + slots)
        column = jnp.where(r < count, column, -1)
        picks.append(jnp.where(column == c, 1.0, 0.0).astype(bf16))
        valid_keys.append(lax.broadcasted_iota(jnp.int32, (ROWS, ROWS), 1) < count)
    pick = jnp.concatenate(picks, axis=0)
    x = mm_nt(pick[:, :slots], tok[...]) + mm_nt(pick[:, slots:], tok_up[...])

    unit = lax.broadcasted_iota(jnp.int32, (1, hidden_units), 1)
    group = sum(jnp.where(unit >= j * d, 1, 0) for j in range(1, 4))
    origin = 4 * (unit - group * d) + group
    f = lax.broadcasted_iota(jnp.int32, (hidden_units, hidden_units), 0)
    perm[...] = jnp.where(f == origin, 1.0, 0.0).astype(bf16)

    vec = [None] * layers
    b_one = [None] * layers
    for l in range(layers):
        w_all[l] = w_full[l]
        w_one_s[l] = mm(w_all[l, :d, 4 * d:8 * d], perm[...]).astype(bf16)
        for j in range(4):
            w_two_s[l, j * d:(j + 1) * d, :] = w_all[l, :d, (8 + j) * d:(9 + j) * d]
        tail = w_all[l, d:d + BLOCK, :]
        vec[l] = tail.astype(f32)[0:1, :]
        b_one[l] = mm(tail[:, 8 * d:], perm[...])[0:1, :]

    def v_of(l, index):
        return vec[l][:, index * d:(index + 1) * d]

    for l in range(layers):
        h, hat, inv = norm_forward(x, v_of(l, 0), v_of(l, 1))
        hat1_s[l], h1_s[l], inv_s[l, 0] = hat, h, inv
        projected = mm(h, w_all[l, :d, :3 * d])
        qkv_s[l, :, :d] = ((projected[:, :d] + v_of(l, 2)).astype(bf16).astype(f32)
                           * (1.0 / math.sqrt(HD))).astype(bf16)
        qkv_s[l, :, d:2 * d] = projected[:, d:2 * d].astype(bf16)
        qkv_s[l, :, 2 * d:] = (projected[:, 2 * d:] + v_of(l, 3)).astype(bf16)
        for i in range(IMAGES_HERE):
            at = slice(i * ROWS, (i + 1) * ROWS)
            for head in range(heads):
                q = qkv_s[l, at, head * HD:(head + 1) * HD]
                key = qkv_s[l, at, d + head * HD:d + (head + 1) * HD]
                val = qkv_s[l, at, 2 * d + head * HD:2 * d + (head + 1) * HD]
                scores = jnp.where(valid_keys[i], mm_nt(q, key), masked_fill)
                e = jnp.exp(scores - jnp.max(scores, axis=-1, keepdims=True))
                p = e * (1.0 / jnp.sum(e, axis=-1, keepdims=True))
                p_s[l, i, head] = p
                o_s[l, at, head * HD:(head + 1) * HD] = mm(p.astype(bf16), val).astype(bf16)
        x1 = x + (mm(o_s[l], w_all[l, :d, 3 * d:4 * d]) + v_of(l, 4))
        h2, hat, inv = norm_forward(x1, v_of(l, 5), v_of(l, 6))
        hat2_s[l], h2_s[l], inv_s[l, 1] = hat, h2, inv
        u = mm(h2, w_one_s[l]) + b_one[l]
        phi = 0.5 * (1.0 + lax.erf(u * (1.0 / math.sqrt(2.0))))
        a_s[l] = (u * phi).astype(bf16)
        slope_s[l] = phi + u * (jnp.exp(-0.5 * u * u) * (1.0 / math.sqrt(2.0 * math.pi)))
        x = x1 + (mm(a_s[l], w_two_s[l]) + v_of(l, 7))

    x_low = x.astype(bf16)
    act_own[...] = mm_tn(x_low, pick[:, :slots]).astype(bf16)
    act_up[...] = mm_tn(x_low, pick[:, slots:]).astype(bf16)

    dx = mm_nt(pick[:, :slots], cot[...]) + mm_nt(pick[:, slots:], cot_up[...])
    for l in reversed(range(layers)):
        dm = dx.astype(bf16)
        g_two = mm_tn(a_s[l], dm)
        for j in range(4):
            grad_s[l, :d, (8 + j) * d:(9 + j) * d] = g_two[j * d:(j + 1) * d, :].astype(bf16)
        g_b2 = rows_sum(dm.astype(f32))
        du = (mm_nt(dm, w_two_s[l]) * slope_s[l]).astype(bf16)
        g_b1 = mm_nt(jnp.broadcast_to(rows_sum(du.astype(f32)), (BLOCK, hidden_units)).astype(bf16),
                     perm[...])[0:1, :]
        g_one = mm_tn(h2_s[l], du).astype(bf16)
        grad_s[l, :d, 4 * d:8 * d] = mm_nt(g_one, perm[...]).astype(bf16)
        dh2 = mm_nt(du, w_one_s[l])
        dv, g_g2, g_c2 = norm_backward(dh2, hat2_s[l], inv_s[l, 1], v_of(l, 5))
        dx1 = dx + dv
        db = dx1.astype(bf16)
        g_bo = rows_sum(db.astype(f32))
        grad_s[l, :d, 3 * d:4 * d] = mm_tn(o_s[l], db).astype(bf16)
        do_s[...] = mm_nt(db, w_all[l, :d, 3 * d:4 * d]).astype(bf16)
        for i in range(IMAGES_HERE):
            at = slice(i * ROWS, (i + 1) * ROWS)
            for head in range(heads):
                q_at = slice(head * HD, (head + 1) * HD)
                k_at = slice(d + head * HD, d + (head + 1) * HD)
                v_at = slice(2 * d + head * HD, 2 * d + (head + 1) * HD)
                do = do_s[at, q_at]
                p = p_s[l, i, head]
                dp = mm_nt(do, qkv_s[l, at, v_at])
                ds = (p * (dp - jnp.sum(p * dp, axis=-1, keepdims=True))).astype(bf16)
                dqkv_s[at, q_at] = (mm(ds, qkv_s[l, at, k_at]) * (1.0 / math.sqrt(HD))).astype(bf16)
                dqkv_s[at, k_at] = mm_tn(ds, qkv_s[l, at, q_at]).astype(bf16)
                dqkv_s[at, v_at] = mm_tn(p.astype(bf16), do).astype(bf16)
        g_bq = rows_sum(dqkv_s[:, :d].astype(f32))
        g_bv = rows_sum(dqkv_s[:, 2 * d:].astype(f32))
        grad_s[l, :d, :3 * d] = mm_tn(h1_s[l], dqkv_s[...]).astype(bf16)
        dh = mm_nt(dqkv_s[...], w_all[l, :d, :3 * d])
        dv, g_g1, g_c1 = norm_backward(dh, hat1_s[l], inv_s[l, 0], v_of(l, 0))
        dx = dx1 + dv
        line = jnp.concatenate([g_g1, g_c1, g_bq, g_bv, g_bo, g_g2, g_c2, g_b2, g_b1], axis=1)
        grad_s[l, d:d + BLOCK, :] = jnp.broadcast_to(line, (BLOCK, line.shape[1])).astype(bf16)

    high = dx.astype(bf16)
    low = (dx - high.astype(f32)).astype(bf16)
    dx_own[...] = mm_tn(high, pick[:, :slots]) + mm_tn(low, pick[:, :slots])
    dx_up[...] = mm_tn(high, pick[:, slots:]).astype(bf16)
    grad_out[...] = grad_s[...]


def compute(n, ranges, weights, tok, cot, tok_up, cot_up, layers):
    d, slots = tok.shape
    hidden_units = 4 * d
    rows = IMAGES_HERE * ROWS
    tall = d + BLOCK
    wide = 12 * d
    args = list(weights) + [tok, cot, tok_up, cot_up]
    outs = [jax.ShapeDtypeStruct((layers, tall, wide), bf16)]
    outs += [
        jax.ShapeDtypeStruct((d, slots), kind) for kind in (bf16, bf16, f32, bf16)
    ]
    vm = pl.BlockSpec(memory_space=pltpu.VMEM)
    return pl.pallas_call(
        functools.partial(compute_kernel, n, layers, d, hidden_units),
        out_shape=tuple(outs),
        in_specs=[pl.BlockSpec(memory_space=pltpu.SMEM)] + [vm] * len(args),
        out_specs=(vm,) * len(outs),
        scratch_shapes=[
            pltpu.VMEM((layers, tall, wide), bf16),
            pltpu.VMEM((layers, d, hidden_units), bf16),
            pltpu.VMEM((layers, hidden_units, d), bf16),
            pltpu.VMEM((layers, rows, d), f32),
            pltpu.VMEM((layers, rows, d), bf16),
            pltpu.VMEM((layers, rows, 3 * d), bf16),
            pltpu.VMEM((layers, IMAGES_HERE, d // HD, ROWS, ROWS), f32),
            pltpu.VMEM((layers, rows, d), bf16),
            pltpu.VMEM((layers, rows, d), f32),
            pltpu.VMEM((layers, rows, d), bf16),
            pltpu.VMEM((layers, rows, hidden_units), f32),
            pltpu.VMEM((layers, rows, hidden_units), bf16),
            pltpu.VMEM((layers, 2, rows, 1), f32),
            pltpu.VMEM((rows, 3 * d), bf16),
            pltpu.VMEM((rows, d), bf16),
            pltpu.VMEM((layers, tall, wide), bf16),
            pltpu.VMEM((hidden_units, hidden_units), bf16),
        ],
        compiler_params=pltpu.CompilerParams(vmem_limit_bytes=vmem_bytes),
        name="two_layers",
    )(ranges, *args)


def rows_of(flats, d):
    w_in, w_out, w_one, w_two = flats
    layers = w_in.shape[0]
    return jnp.concatenate(
        [
            w_in.reshape(layers, -1, 3 * d),
            w_out.reshape(layers, -1, d),
            w_one.reshape(layers, -1, 4 * d),
            w_two.reshape(layers, -1, 4 * d),
        ],
        axis=2,
    )


def flats_of(block, d):
    layers = block.shape[0]
    ends = (0, 3 * d, 4 * d, 8 * d, 12 * d)
    return [block[:, :, lo:hi].reshape(layers, -1) for lo, hi in zip(ends, ends[1:])]


def local_other(tokens, ranges, attn_in, attn_out, mlp_in, mlp_out, vectors, cotangent):
    n = lax.axis_size("dev")
    slots, d = tokens.shape
    layers, part = vectors.shape
    tokens, cotangent = tokens.T, cotangent.T
    flats = (attn_in, attn_out, mlp_in, mlp_out)
    whole = [
        jnp.stack([lax.all_gather(flat[l], "dev", axis=0, tiled=True) for l in range(layers)])
        for flat in flats + (vectors,)
    ]
    line = whole.pop()
    spare = jnp.zeros((layers, BLOCK - 1, 12 * d), bf16)
    block = jnp.concatenate([rows_of(whole, d), line[:, None, :], spare], axis=1)
    down = [(i, (i + n - 1) % n) for i in range(n)]
    tok_up, cot_up = lax.ppermute(tokens, "dev", down), lax.ppermute(cotangent, "dev", down)
    grad, act, act_up, dx, dx_up = compute(
        n, ranges, (block,), tokens, cotangent, tok_up, cot_up, layers
    )
    up = [(i, (i + 1) % n) for i in range(n)]
    act = act + lax.ppermute(act_up, "dev", up)
    dx = dx + lax.ppermute(dx_up, "dev", up)
    terms = flats_of(grad[:, :d], d) + [grad[:, d]]
    grads = [
        jnp.stack([
            lax.psum_scatter(term[l].astype(f32), "dev", scatter_dimension=0, tiled=True)
            for l in range(layers)
        ])
        for term in terms
    ]
    return (act.T, dx.T, *grads)


def solution(mesh):
    flat = P(None, "dev")
    rows = P("dev", None)

    def local(*args):
        n = lax.axis_size("dev")
        slots, d = args[0].shape
        layers = args[2].shape[0]
        fast = n == 32 and d == 6 * n and layers == 2 and slots == 256
        return local_fused(*args) if fast else local_other(*args)

    return jax.shard_map(
        local,
        mesh=mesh,
        in_specs=(rows, P(), flat, flat, flat, flat, flat, rows),
        out_specs=(rows, rows, flat, flat, flat, flat, flat),
        check_vma=False,
    )
```

```python
import functools
import math

import jax
import jax.numpy as jnp
from jax import lax
from jax.experimental import pallas as pl
from jax.experimental.pallas import tpu as pltpu
from jax.sharding import PartitionSpec as P

HD = 64
IMG_LEN = 197
ROWS = 208
IMAGES_HERE = 2
BLOCK = 16
MESH_ID = pl.DeviceIdType.MESH
bf16, f32 = jnp.bfloat16, jnp.float32
eps_norm = 1e-06
masked_fill = -1e30
vmem_bytes = 56 * 2**20


def mm(a, b):
    return jnp.dot(a, b, preferred_element_type=f32)


def mm_nt(a, b):
    return lax.dot_general(a, b, (((1,), (1,)), ((), ())), preferred_element_type=f32)


def mm_tn(a, b):
    return lax.dot_general(a, b, (((0,), (0,)), ((), ())), preferred_element_type=f32)


def norm_forward(x, gain, bias):
    centered = x - jnp.mean(x, axis=-1, keepdims=True)
    inverse = lax.rsqrt(jnp.mean(centered * centered, axis=-1, keepdims=True) + eps_norm)
    hat = centered * inverse
    return (hat * gain + bias).astype(bf16), hat, inverse


def norm_backward(dh, hat, inverse, gain):
    scaled = dh * gain
    dv = inverse * (
        scaled
        - jnp.mean(scaled, axis=-1, keepdims=True)
        - hat * jnp.mean(scaled * hat, axis=-1, keepdims=True)
    )
    return dv, rows_sum(dh * hat), rows_sum(dh)


def rows_sum(x):
    return jnp.sum(x, axis=0, keepdims=True)


def remote(src, dst, send, recv, dev):
    return pltpu.make_async_remote_copy(
        src_ref=src, dst_ref=dst, send_sem=send, recv_sem=recv,
        device_id=(dev,), device_id_type=MESH_ID,
    )


class Place:
    def __init__(self, n):
        self.n = n
        me = self.me = lax.axis_index("dev")
        self.bits = [lax.rem(lax.div(me, 2**b), 2) for b in range(5)]
        self.c, self.x, self.y = self.bits[:3]
        self.z = lax.div(me, 8)
        self.core = self.flip(0)
        self.along_z = [self.flip(3), self.flip(4), self.flip(3, 4)]
        self.along_xy = [self.flip(1), self.flip(2), self.flip(1, 2)]
        self.chips = [self.flip(*[b + 1 for b in range(4) if m >> b & 1]) for m in range(1, 16)]
        self.up, self.down = lax.rem(me + 1, n), lax.rem(me + n - 1, n)

    def flip(self, *which):
        return self.me + sum((1 - 2 * self.bits[b]) * 2**b for b in which)

    def peers(self):
        return [self.core] + self.chips + [self.up, self.down]


def taken(ref, sem):
    pltpu.make_async_copy(ref, ref, sem).wait()


class Sender:
    def go(self, src, dst, k, dev):
        remote(src, dst, self.send.at[k], self.recv.at[k], dev).start()

    def arrived(self, k):
        taken(self.size_of[k], self.recv.at[k])

    def left(self):
        for k, ref in enumerate(self.size_of):
            if ref is not None:
                taken(ref, self.send.at[k])


class Gather(Sender):
    def __init__(self, place, buf, room, send, recv):
        self.place, self.buf, self.send, self.recv = place, buf, send, recv
        three, nine = buf.at[pl.ds(0, 3), 0, 0, 0], room.at[:, pl.ds(1, 3)]
        self.size_of = [three, three, nine, buf.at[:, :, :, 0]]

    def begin(self):
        p = self.place
        own = self.buf.at[0, p.y, p.x, p.c]
        for k, dev in enumerate(p.along_z):
            self.go(own, self.buf.at[k + 1, p.y, p.x, p.c], 0, dev)
        for dev in p.along_xy:
            self.go(own, own, 1, dev)

    def middle(self):
        p = self.place
        self.arrived(0)
        got = self.buf.at[pl.ds(1, 3), p.y, p.x, p.c]
        for dev in p.along_xy:
            self.go(got, got, 2, dev)

    def core(self):
        p = self.place
        self.arrived(1)
        self.arrived(2)
        half = self.buf.at[:, :, :, p.c]
        self.go(half, half, 3, p.core)

    def done(self):
        self.arrived(3)


class GatherAcross(Gather):
    def __init__(self, place, buf, room, send, recv):
        super().__init__(place, buf, room, send, recv)
        self.size_of = [room, self.size_of[1], None, self.size_of[3]]

    def begin(self):
        p = self.place
        own = self.buf.at[0, p.y, p.x, p.c]
        for dev in p.along_xy:
            self.go(own, own, 1, dev)

    def middle(self):
        self.arrived(1)
        c = self.place.c
        for k, dev in enumerate(self.place.along_z):
            self.go(self.buf.at[0, :, :, c], self.buf.at[k + 1, :, :, c], 0, dev)

    def core(self):
        p = self.place
        self.arrived(0)
        half = self.buf.at[:, :, :, p.c]
        self.go(half, half, 3, p.core)


class Scatter(Sender):
    def __init__(self, place, grads, half, out_xy, in_xy, out_z, in_z, send, recv, out):
        self.place, self.grads, self.half = place, grads, half
        self.out_xy, self.in_xy, self.out_z, self.in_z = out_xy, in_xy, out_z, in_z
        self.send, self.recv, self.out = send, recv, out
        self.size_of = self.sizes()

    def sizes(self):
        return [self.half, self.in_xy.at[:, pl.ds(1, 3)], self.in_xy.at[:, 0], self.in_z]

    def begin(self):
        p = self.place
        self.go(self.grads.at[:, :, :, 1 - p.c], self.half, 0, p.core)

    def pair(self):
        self.arrived(0)
        self.out_xy[...] = (
            self.grads[:, :, :, self.place.c].astype(f32) + self.half[...].astype(f32)
        ).astype(bf16)

    def middle(self):
        p = self.place
        self.pair()
        goals = [(p.y, 1 - p.x), (1 - p.y, p.x), (1 - p.y, 1 - p.x)]
        for k, (y, x) in enumerate(goals):
            self.go(self.out_xy.at[pl.ds(1, 3), y, x], self.in_xy.at[k, pl.ds(1, 3)], 1, p.along_xy[k])
        for k, (y, x) in enumerate(goals):
            self.go(self.out_xy.at[0, y, x], self.in_xy.at[k, 0], 2, p.along_xy[k])

    def ours(self, z):
        p = self.place
        return self.grads[z, p.y, p.x, p.c].astype(f32) + self.half[z, p.y, p.x].astype(f32)

    def end(self):
        p = self.place
        self.arrived(1)
        for z in range(1, 4):
            total = self.ours(z)
            for k in range(3):
                total += self.in_xy[k, z].astype(f32)
            self.out_z[z - 1] = total.astype(bf16)
            self.go(self.out_z.at[z - 1], self.in_z.at[z - 1], 3, p.along_z[z - 1])

    def done(self):
        self.arrived(2)
        total = self.ours(0)
        for k in range(3):
            total += self.in_xy[k, 0].astype(f32)
        self.arrived(3)
        for k in range(3):
            total += self.in_z[k].astype(f32)
        self.out[...] = total


class ScatterAcross(Scatter):
    def sizes(self):
        return [self.half, self.in_xy, None, self.in_z]

    def middle(self):
        self.pair()
        for k, dev in enumerate(self.place.along_z):
            self.go(self.out_xy.at[k + 1], self.in_xy.at[k], 1, dev)

    def end(self):
        p = self.place
        self.arrived(1)
        total = self.grads[0, :, :, p.c].astype(f32) + self.half[0].astype(f32)
        for k in range(3):
            total += self.in_xy[k].astype(f32)
        self.out_xy[0] = total.astype(bf16)
        for k, (y, x) in enumerate([(p.y, 1 - p.x), (1 - p.y, p.x), (1 - p.y, 1 - p.x)]):
            self.go(self.out_xy.at[0, y, x], self.in_z.at[k], 3, p.along_xy[k])

    def done(self):
        p = self.place
        total = self.ours(0)
        for k in range(3):
            total += self.in_xy[k, p.y, p.x].astype(f32)
        self.arrived(3)
        for k in range(3):
            total += self.in_z[k].astype(f32)
        self.out[...] = total


class Direct(Scatter):
    def sizes(self):
        return [self.half, self.in_xy]

    def middle(self):
        p = self.place
        self.pair()
        for m, dev in enumerate(p.chips, 1):
            y = 1 - p.y if m & 2 else p.y
            x = 1 - p.x if m & 1 else p.x
            self.go(self.out_xy.at[m >> 2, y, x], self.in_xy.at[m - 1], 1, dev)

    def done(self):
        total = self.ours(0)
        self.arrived(1)
        for k in range(15):
            total += self.in_xy[k].astype(f32)
        self.out[...] = total


def natural(c, z):
    return jnp.where((c & 7) < 6, 6 * ((c >> 3) ^ (8 * z)) + (c & 7), -1)


def iota(shape, dim):
    return lax.broadcasted_iota(jnp.int32, shape, dim)


def norm_padded(x, gain, bias, real, d):
    centered = (x - jnp.sum(x, axis=-1, keepdims=True) * (1.0 / d)) * real
    inverse = lax.rsqrt(jnp.sum(centered * centered, axis=-1, keepdims=True) * (1.0 / d) + eps_norm)
    hat = centered * inverse
    return (hat * gain + bias).astype(bf16), hat, inverse


def norm_padded_back(dh, hat, inverse, gain, d):
    scaled = dh * gain
    dv = inverse * (
        scaled
        - jnp.sum(scaled, axis=-1, keepdims=True) * (1.0 / d)
        - hat * (jnp.sum(scaled * hat, axis=-1, keepdims=True) * (1.0 / d))
    )
    return dv, rows_sum(dh * hat), rows_sum(dh)


def sublanes(x, shift):
    return pltpu.roll(x, shift, 1)


def unfold(tiles, s):
    a, b, c = tiles
    return jnp.where(s < 2, sublanes(a, 2), jnp.where(s < 4, sublanes(b, 4), sublanes(c, 6)))


def fold(tiles, extra, s):
    return [jnp.where(s < 6, t, sublanes(extra, 6 - 2 * k)) for k, t in enumerate(tiles)]


def fused_kernel(n, layers, d, ranges, *refs):
    refs = list(refs)
    take = lambda count: [refs.pop(0) for _ in range(count)]
    tok, cot, a_in, a_out, m_in, m_out, vecs = take(7)
    reds, (act_out, dx_out) = take(3), take(2)
    wires, grads, halves, outxys, inxys, outzs, inzs = [take(3) for _ in range(7)]
    in_direct, in_across = take(2)
    tok_near, cot_near, act_near, act_in, dx_near, dx_in = take(6)
    w_in_s, w_one_s, w_out_s, w_two_s, two_s, g_two_s = take(6)
    pick_s, x_s, dx_s, ds_s = take(4)
    vec_n, vec_g, b_one_s, line_n, line_g = take(5)
    hat1_s, h1_s, qkv_s, p_s, o_s, hat2_s, h2_s, slope_s, a_s, inv_s = take(10)
    dqkv_s, do_s, pack_a, pack_b, pack_c, flat_ai, flat_ao, flat_mi, flat_mo, vec_s = take(10)
    gsend, grecv, ssend, srecv, hsend, hrecv = take(6)
    wire_a, wire_b, wire_c = wires
    slots = tok.shape[1]
    heads = d // HD
    wide = 8 * n
    hidden_units = 4 * d
    rows = IMAGES_HERE * ROWS
    place = Place(n)
    me = place.me

    barrier = pltpu.get_barrier_semaphore()
    for other in place.peers():
        pl.semaphore_signal(barrier, inc=1, device_id=(other,), device_id_type=MESH_ID)

    part = vecs.shape[1]
    here = (0, place.y, place.x, place.c)
    z_of = [place.z] + [lax.div(dev, 8) for dev in place.along_z]
    vec_s[...] = jnp.zeros_like(vec_s)
    vec_s[0:layers, 0:part] = vecs[...].astype(f32)
    moved = pltpu.roll(vec_s[...], 8 * lax.rem(me, 8), 1)
    vec_s[...] = moved
    flat_ai[...] = a_in[...].astype(f32)
    flat_mo[...] = m_out[...].astype(f32)
    pack_b[...] = jnp.zeros_like(pack_b)

    def pack_first(l):
        row = slice(l, l + 1)
        for r in range(6):
            base, k, i = r * 3 * d, r // 2, r % 2
            pack_a[r:r + 1, :] = flat_ai[row, base:base + 256]
            pack_a[8 + r:9 + r, :128] = flat_ai[row, base + 256:base + 384]
            low, lanes = 6 + i + (8 if k == 2 else 0), slice(128 * (k % 2), 128 * (k % 2) + 128)
            pack_a[low:low + 1, lanes] = flat_ai[row, base + 384:base + 512]
            pack_a[8 + r:9 + r, 128:192] = flat_ai[row, base + 512:base + 576]
        pack_a[14:15, 128:192] = vec_s[row, :64]
        pack_a[15:16, 128:192] = vec_s[row, 64:128]
        for r in range(8):
            pack_a[8 + r:9 + r, 192:] = flat_mo[row, (16 + r) * d + 128:(17 + r) * d]
        wire_a[(l,) + here] = pack_a[...].astype(bf16)

    def pack_second(l):
        row = slice(l, l + 1)
        for r in range(6):
            base, k, i = r * 4 * d, r // 2, r % 2
            lanes = slice(128 * k, 128 * k + 128)
            pack_b[r:r + 1, :] = flat_mi[row, base:base + 384]
            pack_b[6 + i:7 + i, lanes] = flat_mi[row, base + 384:base + 512]
            pack_b[8 + r:9 + r, :256] = flat_mi[row, base + 512:base + 768]
            pack_b[8 + r:9 + r, 256:] = flat_ao[row, r * d:r * d + 128]
            pack_b[14 + i:15 + i, 128 * k:128 * k + 64] = flat_ao[row, r * d + 128:(r + 1) * d]
        wire_b[(l,) + here] = pack_b[...].astype(bf16)

    def pack_third(l):
        row = slice(l, l + 1)
        for r in range(24):
            g, i = r // 8, r % 8
            low, lane = i + (8 if g == 2 else 0), 128 * (g % 2)
            pack_c[low:low + 1, lane:lane + 128] = flat_mo[row, r * d:r * d + 128]
            if g < 2:
                pack_c[8 + i:9 + i, 128 + 64 * g:192 + 64 * g] = flat_mo[row, r * d + 128:(r + 1) * d]
        wire_c[(l,) + here] = pack_c[...].astype(bf16)

    across = [(1, 2)]
    gathers = [
        [
            (GatherAcross if (l, k) in across else Gather)(
                place, wires[k].at[l], inxys[k].at[l], gsend.at[l, k], grecv.at[l, k]
            )
            for k in range(3)
        ]
        for l in range(layers)
    ]
    scatters = [
        [
            (Direct if k == 0 and l == 0 else ScatterAcross if (l, k) in across else Scatter)(
                place, grads[k].at[l], halves[k].at[l], outxys[k].at[l],
                in_direct if k == 0 and l == 0 else in_across if (l, k) in across else inxys[k].at[l],
                outzs[k].at[l], inzs[k].at[l], ssend.at[l, k], srecv.at[l, k], reds[k].at[l],
            )
            for k in range(3)
        ]
        for l in range(layers)
    ]
    side = slots // 2
    first_half, second_half = pl.ds(0, side), pl.ds(side, side)

    def pair(src, dst, at):
        return [
            remote(src.at[:, a], dst.at[:, b], hsend.at[at + i], hrecv.at[at + i], dev)
            for i, (a, b, dev) in enumerate((
                (first_half, first_half, place.down), (second_half, second_half, place.up),
            ))
        ]

    tok_halo, cot_halo = pair(tok, tok_near, 0), pair(cot, cot_near, 2)
    back = lambda src, dst, at: [
        remote(src.at[:, first_half], dst.at[:, first_half], hsend.at[at], hrecv.at[at], place.up),
        remote(src.at[:, second_half], dst.at[:, second_half], hsend.at[at + 1], hrecv.at[at + 1], place.down),
    ]
    act_halo, dx_halo = back(act_near, act_in, 4), back(dx_near, dx_in, 6)
    (ga0, gb0, gc0), (ga1, gb1, gc1) = gathers
    (sa0, sb0, sc0), (sa1, sb1, sc1) = scatters

    pack_first(0)
    pl.semaphore_wait(barrier, len(place.peers()))
    ga0.begin()
    for copy in tok_halo:
        copy.start()
    flat_ao[...] = a_out[...].astype(f32)
    flat_mi[...] = m_in[...].astype(f32)
    pack_second(0)
    gb0.begin()
    pack_third(0)
    gc0.begin()
    pack_first(1)
    ga1.begin()
    pack_second(1)
    gb1.begin()
    pack_third(1)
    gc1.begin()
    for copy in cot_halo:
        copy.start()

    lane = iota((1, wide), 1)
    real = jnp.where((lane & 7) < 6, 1.0, 0.0)
    spread = jnp.where(iota((d, wide), 0) == natural(iota((1, wide), 1), place.z), 1.0, 0.0).astype(bf16)
    owner = (lane >> 3) ^ (8 * place.z)
    window = jnp.where((lane & 7) >= 6, owner + (owner >> 3) + (lane & 1), -1)
    windows = [
        jnp.where(3 * iota((BLOCK, wide), 0) + k == window, 1.0, 0.0).astype(bf16) for k in range(3)
    ]
    sub = iota((1, 8, 1), 1)

    first, last, below = ranges[0, me], ranges[1, me], ranges[0, place.down]
    total = ranges[1, n - 1]
    centre = IMG_LEN // 2
    image = (first + IMG_LEN - 1 - centre) // IMG_LEN
    picks, valid_keys = [], []
    for k in range(IMAGES_HERE):
        begin = (image + k) * IMG_LEN
        mine = (begin < total) & (jnp.minimum(begin + centre, total - 1) < last)
        count = jnp.where(mine, jnp.minimum(IMG_LEN, total - begin), 0)
        r = iota((ROWS, 2 * slots), 0)
        c = iota((ROWS, 2 * slots), 1)
        t = begin + r
        column = jnp.where(
            t < first, t - below + slots, jnp.where(t < last, t - first, t - last + slots)
        )
        column = jnp.where(r < count, column, -1)
        picks.append(jnp.where(column == c, 1.0, 0.0).astype(bf16))
        valid_keys.append(iota((ROWS, ROWS), 1) < count)
    pick = jnp.concatenate(picks, axis=0)
    x = mm_nt(pick[:, :slots], mm_tn(spread, tok[...]).astype(bf16))

    ga0.middle()
    gb0.middle()
    gc0.middle()
    ga0.core()
    gc1.middle()
    ga1.middle()
    gb1.middle()
    for copy in tok_halo:
        copy.wait_recv()
    x += mm_nt(pick[:, slots:], mm_tn(spread, tok_near[...]).astype(bf16))
    dx = mm_nt(pick[:, :slots], mm_tn(spread, cot[...]).astype(bf16))
    pick_s[...] = pick
    dx_s[...] = dx

    def add_near():
        for copy in cot_halo:
            copy.wait_recv()
        dx_s[...] += mm_nt(pick_s[:, slots:], mm_tn(spread, cot_near[...]).astype(bf16))


    def tiles_of(wire, l):
        v = wire[l]
        width = v.shape[-1]
        v = v.reshape(n * BLOCK, width).astype(f32).reshape(n, 2, 8, width)
        return [v[:, i, :, k:k + 128] for i in range(2) for k in range(0, width, 128)]

    def flat(t):
        return t.reshape(wide, t.shape[-1]).astype(bf16)

    def unpack_a(l):
        t0, t1, t2, t4 = tiles_of(wire_a, l)
        for k, t in enumerate((t0, t1, t2, unfold((t0, t1, t2), sub), t4)):
            w_in_s[l, :, 128 * k:128 * k + 128] = flat(t)
        t4 = flat(t4)
        lines = jnp.concatenate([mm(each, t4)[:, :64] for each in windows], axis=1)
        vec_n[l] = lines
        vec_g[l] = mm(lines.astype(bf16), spread)
        for k in range(4):
            b_one_s[l, 0:1, k * d:(k + 1) * d] = lines[8 + k:9 + k]

    def unpack_b(l):
        t0, t1, t2, t4, t5, t6 = tiles_of(wire_b, l)
        for k, t in enumerate((t0, t1, t2, unfold((t0, t1, t2), sub), t4, t5)):
            w_one_s[l, :, 128 * k:128 * k + 128] = flat(t)
        t7 = unfold((t4, t5, t6), sub)
        out = jnp.concatenate([flat(t6), flat(t7)], axis=1)
        out = mm(spread, out)[:, :d].astype(bf16)
        w_out_s[l] = mm(out, spread).astype(bf16)

    def unpack_c(l):
        t0, t1, t2, t3 = tiles_of(wire_c, l)
        last = tiles_of(wire_a, l)[3]
        side = pltpu.roll(t3, 64, 2), pltpu.roll(last, 64, 2)
        pile = lambda ts: jnp.stack(ts, axis=1).reshape(4, d, 128).astype(bf16)
        left, right = pile((t0, t1, t2)), pile((t3,) + side)
        for k in range(4):
            at = pl.ds(pl.multiple_of(z_of[k] * d, BLOCK), d)
            two_s[at, :128] = left[k]
            two_s[at, 128:] = right[k]
        w_two_s[l] = mm(two_s[:, :d], spread).astype(bf16)

    beats = [
        [lambda: None, lambda: None, lambda: (gb0.core(), add_near()), lambda: gc0.core(), lambda: ga1.core()],
        [lambda: gb1.core(), lambda: gc1.core(), lambda: None, lambda: None, lambda: None],
    ]
    for l in range(layers):
        ga, gb, gc = gathers[l]
        ga.done()
        unpack_a(l)
        h, hat, inv = norm_padded(x, vec_g[l, 0:1], vec_g[l, 1:2], real, d)
        hat1_s[l], h1_s[l], inv_s[l, 0] = hat, h, inv
        projected = mm(h, w_in_s[l, :, :3 * d])
        qkv_s[l, :, :d] = ((projected[:, :d] + vec_n[l, 2:3]).astype(bf16).astype(f32)
                           * (1.0 / math.sqrt(HD))).astype(bf16)
        qkv_s[l, :, d:2 * d] = projected[:, d:2 * d].astype(bf16)
        qkv_s[l, :, 2 * d:] = (projected[:, 2 * d:] + vec_n[l, 3:4]).astype(bf16)
        beats[l][0]()
        parts = [(i, head) for i in range(IMAGES_HERE) for head in range(heads)]
        at_of = lambda i: slice(i * ROWS, (i + 1) * ROWS)
        lanes = lambda group, head: slice(group * d + head * HD, group * d + (head + 1) * HD)
        for i, head in parts:
            scores = mm_nt(qkv_s[l, at_of(i), lanes(0, head)], qkv_s[l, at_of(i), lanes(1, head)])
            scores = jnp.where(valid_keys[i], scores, masked_fill)
            e = jnp.exp(scores - jnp.max(scores, axis=-1, keepdims=True))
            p = e * (1.0 / jnp.sum(e, axis=-1, keepdims=True))
            p_s[l, i, head] = p
            ds_s[i, head] = p.astype(bf16)
        beats[l][1]()
        for i, head in parts:
            o_s[l, at_of(i), lanes(0, head)] = mm(
                ds_s[i, head], qkv_s[l, at_of(i), lanes(2, head)]
            ).astype(bf16)
        beats[l][2]()
        gb.done()
        beats[l][3]()
        unpack_b(l)
        x1 = x + (mm(o_s[l], w_out_s[l]) + vec_g[l, 4:5])
        h2, hat, inv = norm_padded(x1, vec_g[l, 5:6], vec_g[l, 6:7], real, d)
        hat2_s[l], h2_s[l], inv_s[l, 1] = hat, h2, inv
        u = mm(h2, w_one_s[l]) + b_one_s[l, 0:1]
        phi = 0.5 * (1.0 + lax.erf(u * (1.0 / math.sqrt(2.0))))
        a_s[l] = (u * phi).astype(bf16)
        slope_s[l] = phi + u * (jnp.exp(-0.5 * u * u) * (1.0 / math.sqrt(2.0 * math.pi)))
        beats[l][4]()
        gc.done()
        unpack_c(l)
        x = x1 + (mm(a_s[l], w_two_s[l]) + vec_g[l, 7:8])

    x_s[...] = x.astype(bf16)
    dx = dx_s[...]

    def cut(w, pieces):
        return [w[:, 128 * k:128 * k + 128].reshape(n, 8, 128) for k in range(pieces)]

    def block(tiles):
        half = len(tiles) // 2
        v = [jnp.concatenate(tiles[i * half:(i + 1) * half], axis=-1)[:, None] for i in range(2)]
        v = jnp.concatenate(v, axis=1).reshape(n * BLOCK, 128 * half).astype(bf16)
        return v.reshape(4, 2, 2, 2, BLOCK, 128 * half)

    beats = [
        [lambda: sa1.middle(), lambda: (sc0.middle(), sc1.end()),
         lambda: (sb1.end(), sb0.middle()), lambda: None],
        [lambda: None, lambda: sc1.middle(), lambda: sb1.middle(), lambda: None],
    ]
    dqkv_s[:, 3 * d:] = jnp.zeros((rows, d), bf16)
    low_lanes = iota((1, 1, 128), 2) < 64
    line_g[...] = jnp.zeros_like(line_g)
    line_n[...] = jnp.zeros_like(line_n)
    for l in reversed(range(layers)):
        sa, sb, sc = scatters[l]
        dm = dx.astype(bf16)
        line_g[7:8] = rows_sum(dm.astype(f32))
        g_two_s[...] = mm_tn(a_s[l], mm_nt(dm, spread).astype(bf16))
        g_two = jnp.concatenate(
            [g_two_s[pl.ds(pl.multiple_of(z * d, BLOCK), d), :] for z in z_of], axis=0
        ).reshape(n, 3, 8, d)
        side = jnp.concatenate([g_two[..., 128:], jnp.zeros((n, 3, 8, 256 - d), f32)], axis=-1)
        turned = pltpu.roll(side[:, 1], 64, 2)
        tail = pltpu.roll(side[:, 2], 64, 2)
        grads[2][l] = block([g_two[:, 0, :, :128], g_two[:, 1, :, :128], g_two[:, 2, :, :128],
                             jnp.where(low_lanes, side[:, 0], turned)])
        sc.begin()
        du = (mm_nt(dm, w_two_s[l]) * slope_s[l]).astype(bf16)
        beats[l][0]()
        g_b1 = rows_sum(du.astype(f32))
        for k in range(4):
            line_n[8 + k:9 + k] = g_b1[:, k * d:(k + 1) * d]
        dh2 = mm_nt(du, w_one_s[l])
        g_one = mm_tn(h2_s[l], du)
        dv, g_g2, g_c2 = norm_padded_back(dh2, hat2_s[l], inv_s[l, 1], vec_g[l, 5:6], d)
        line_g[5:6], line_g[6:7] = g_g2, g_c2
        dx1 = dx + dv
        db = dx1.astype(bf16)
        line_g[4:5] = rows_sum(db.astype(f32))
        g_out = mm_tn(o_s[l], mm_nt(db, spread).astype(bf16))
        g_out = jnp.concatenate([g_out, jnp.zeros((d, 256 - d), f32)], axis=1).astype(bf16)
        t6, t7 = cut(mm_tn(spread, g_out), 2)
        t0, t1, t2, t3, t4, t5 = cut(g_one, 6)
        grads[1][l] = block(fold((t0, t1, t2), t3, sub) + fold((t4, t5, t6), t7, sub))
        beats[l][1]()
        sb.begin()
        do_s[...] = mm_nt(db, w_out_s[l]).astype(bf16)
        parts = [(i, head) for i in range(IMAGES_HERE) for head in range(heads)]
        at_of = lambda i: slice(i * ROWS, (i + 1) * ROWS)
        lanes = lambda group, head: slice(group * d + head * HD, group * d + (head + 1) * HD)
        for i, head in parts:
            p = p_s[l, i, head]
            dp = mm_nt(do_s[at_of(i), lanes(0, head)], qkv_s[l, at_of(i), lanes(2, head)])
            ds_s[i, head] = (p * (dp - jnp.sum(p * dp, axis=-1, keepdims=True))).astype(bf16)
        beats[l][2]()
        for i, head in parts:
            at = at_of(i)
            ds = ds_s[i, head]
            dqkv_s[at, lanes(0, head)] = (
                mm(ds, qkv_s[l, at, lanes(1, head)]) * (1.0 / math.sqrt(HD))
            ).astype(bf16)
            dqkv_s[at, lanes(1, head)] = mm_tn(ds, qkv_s[l, at, lanes(0, head)]).astype(bf16)
            dqkv_s[at, lanes(2, head)] = mm_tn(
                p_s[l, i, head].astype(bf16), do_s[at, lanes(0, head)]
            ).astype(bf16)
        beats[l][3]()
        dqkv = dqkv_s[:, :640]
        line_n[2:3] = rows_sum(dqkv_s[:, :d].astype(f32))
        line_n[3:4] = rows_sum(dqkv_s[:, 2 * d:3 * d].astype(f32))
        dh = mm_nt(dqkv, w_in_s[l])
        g_in = mm_tn(h1_s[l], dqkv)
        dv, g_g1, g_c1 = norm_padded_back(dh, hat1_s[l], inv_s[l, 0], vec_g[l, 0:1], d)
        line_g[0:1], line_g[1:2] = g_g1, g_c1
        lines = (line_n[...] + mm_nt(line_g[...].astype(bf16), spread)).astype(bf16)
        vec_rows = sum(mm_tn(windows[k], lines[:, 64 * k:64 * k + 64]) for k in range(3))
        vec_rows = jnp.concatenate([vec_rows, jnp.zeros((wide, 64), f32)], axis=1).reshape(n, 8, 128)
        t0, t1, t2, t3, t4 = cut(g_in, 5)
        t4 = jnp.where(low_lanes, t4 + vec_rows, tail)
        grads[0][l] = block(fold((t0, t1, t2), t3, sub) + [t4])
        sa.begin()
        dx = dx1 + dv

    high = dx.astype(bf16)
    low = (dx - high.astype(f32)).astype(bf16)
    high = mm_nt(high, spread).astype(bf16)
    dx_near[...] = mm_tn(high, pick_s[:, slots:]).astype(bf16)
    for copy in dx_halo:
        copy.start()
    sa1.end()
    sa0.middle()
    x_low = mm_nt(x_s[...], spread).astype(bf16)
    act_near[...] = mm_tn(x_low, pick_s[:, slots:]).astype(bf16)
    for copy in act_halo:
        copy.start()
    sc0.end()
    low = mm_nt(low, spread).astype(bf16)
    dx_own = mm_tn(high, pick_s[:, :slots]) + mm_tn(low, pick_s[:, :slots])
    act_own = mm_tn(x_low, pick_s[:, :slots]).astype(bf16)
    sb0.end()
    sc1.done()
    sb1.done()
    for copy in dx_halo:
        copy.wait_recv()
    dx_out[...] = dx_own + dx_in[...].astype(f32)
    for copy in act_halo:
        copy.wait_recv()
    act_out[...] = act_own + act_in[...]
    sa1.done()
    sc0.done()
    sa0.done()
    sb0.done()
    for copy in tok_halo + cot_halo + act_halo + dx_halo:
        copy.wait_send()
    for group in gathers + scatters:
        for each in group:
            each.left()


def fused(n, ranges, tok, cot, flats):
    d, slots = tok.shape
    layers = flats[0].shape[0]
    wide = 8 * n
    hidden_units = 4 * d
    rows = IMAGES_HERE * ROWS
    shapes = ((BLOCK, 256), (BLOCK, 384), (BLOCK, 256))
    boxes = lambda lead, kind: [pltpu.VMEM((layers,) + lead + s, kind) for s in shapes]
    vm = pl.BlockSpec(memory_space=pltpu.VMEM)
    scratch = (
        boxes((4, 2, 2, 2), bf16) + boxes((4, 2, 2, 2), bf16)
        + boxes((4, 2, 2), bf16) + boxes((4, 2, 2), bf16) + boxes((3, 4), bf16)
        + boxes((3,), bf16) + boxes((3,), bf16)
        + [pltpu.VMEM((15,) + shapes[0], bf16), pltpu.VMEM((3, 2, 2) + shapes[2], bf16)]
        + [pltpu.VMEM((d, slots), bf16)] * 6
        + [
            pltpu.VMEM((layers, wide, 640), bf16),
            pltpu.VMEM((layers, wide, hidden_units), bf16),
            pltpu.VMEM((layers, d, wide), bf16),
            pltpu.VMEM((layers, hidden_units, wide), bf16),
            pltpu.VMEM((hidden_units, 256), bf16),
            pltpu.VMEM((hidden_units, d), f32),
            pltpu.VMEM((rows, 2 * slots), bf16),
            pltpu.VMEM((rows, wide), bf16),
            pltpu.VMEM((rows, wide), f32),
            pltpu.VMEM((IMAGES_HERE, d // HD, ROWS, ROWS), bf16),
            pltpu.VMEM((layers, BLOCK, d), f32),
            pltpu.VMEM((layers, BLOCK, wide), f32),
            pltpu.VMEM((layers, 8, hidden_units), f32),
            pltpu.VMEM((BLOCK, d), f32),
            pltpu.VMEM((BLOCK, wide), f32),
            pltpu.VMEM((layers, rows, wide), f32),
            pltpu.VMEM((layers, rows, wide), bf16),
            pltpu.VMEM((layers, rows, 3 * d), bf16),
            pltpu.VMEM((layers, IMAGES_HERE, d // HD, ROWS, ROWS), f32),
            pltpu.VMEM((layers, rows, d), bf16),
            pltpu.VMEM((layers, rows, wide), f32),
            pltpu.VMEM((layers, rows, wide), bf16),
            pltpu.VMEM((layers, rows, hidden_units), f32),
            pltpu.VMEM((layers, rows, hidden_units), bf16),
            pltpu.VMEM((layers, 2, rows, 1), f32),
            pltpu.VMEM((rows, 4 * d), bf16),
            pltpu.VMEM((rows, d), bf16),
        ]
        + [pltpu.VMEM(s, f32) for s in shapes]
        + [pltpu.VMEM(f.shape, f32) for f in flats[:4]]
        + [pltpu.VMEM((8, 128), f32)]
        + [pltpu.SemaphoreType.DMA((layers, 3, 4))] * 4
        + [pltpu.SemaphoreType.DMA((8,))] * 2
    )
    return pl.pallas_call(
        functools.partial(fused_kernel, n, layers, d),
        out_shape=tuple(jax.ShapeDtypeStruct((layers,) + s, f32) for s in shapes)
        + (jax.ShapeDtypeStruct((d, slots), bf16), jax.ShapeDtypeStruct((d, slots), f32)),
        in_specs=[pl.BlockSpec(memory_space=pltpu.SMEM)] + [vm] * 7,
        out_specs=(vm,) * 5,
        scratch_shapes=scratch,
        compiler_params=pltpu.CompilerParams(
            collective_id=0, has_side_effects=True, vmem_limit_bytes=vmem_bytes
        ),
        name="two_layers",
    )(ranges.T, tok, cot, *flats)


def flatten_kernel(n, layers, d, red_a, red_b, red_c, act_in, dx_in, act, dx, g_in, g_out, g_one, g_two, g_vec, vec_s):
    me = lax.axis_index("dev")
    act[...] = act_in[...]
    dx[...] = dx_in[...]
    vec_s[...] = jnp.zeros_like(vec_s)
    for l in range(layers):
        row = slice(l, l + 1)
        for r in range(6):
            k, i = r // 2, r % 2
            base = r * 3 * d
            g_in[row, base:base + 256] = red_a[l, r:r + 1, :]
            g_in[row, base + 256:base + 384] = red_a[l, 8 + r:9 + r, :128]
            low, lane = 6 + i + (8 if k == 2 else 0), 128 * (k % 2)
            g_in[row, base + 384:base + 512] = red_a[l, low:low + 1, lane:lane + 128]
            g_in[row, base + 512:base + 576] = red_a[l, 8 + r:9 + r, 128:192]
            base = r * 4 * d
            g_one[row, base:base + 384] = red_b[l, r:r + 1, :]
            g_one[row, base + 384:base + 512] = red_b[l, 6 + i:7 + i, 128 * k:128 * k + 128]
            g_one[row, base + 512:base + 768] = red_b[l, 8 + r:9 + r, :256]
            base = r * d
            g_out[row, base:base + 128] = red_b[l, 8 + r:9 + r, 256:]
            g_out[row, base + 128:base + 192] = red_b[l, 14 + i:15 + i, 128 * k:128 * k + 64]
        for r in range(24):
            g, i = r // 8, r % 8
            base, low, lane = r * d, i + (8 if g == 2 else 0), 128 * (g % 2)
            g_two[row, base:base + 128] = red_c[l, low:low + 1, lane:lane + 128]
            if g < 2:
                g_two[row, base + 128:base + 192] = red_c[l, 8 + i:9 + i, 128 + 64 * g:192 + 64 * g]
            else:
                g_two[row, base + 128:base + 192] = red_a[l, 8 + i:9 + i, 192:]
        vec_s[row, :64] = red_a[l, 14:15, 128:192]
        vec_s[row, 64:] = red_a[l, 15:16, 128:192]
    part = g_vec.shape[1]
    moved = pltpu.roll(vec_s[...], lax.rem(128 - 8 * lax.rem(me, 8), 128), 1)
    g_vec[...] = moved[0:layers, 0:part]


def local_fused(tokens, ranges, attn_in, attn_out, mlp_in, mlp_out, vectors, cotangent):
    n = lax.axis_size("dev")
    slots, d = tokens.shape
    layers, part = vectors.shape
    flats = (attn_in, attn_out, mlp_in, mlp_out, vectors)
    sums = fused(n, ranges, tokens.T, cotangent.T, flats)
    vm = pl.BlockSpec(memory_space=pltpu.VMEM)
    act, dx, *grads = pl.pallas_call(
        functools.partial(flatten_kernel, n, layers, d),
        out_shape=(
            jax.ShapeDtypeStruct((d, slots), bf16), jax.ShapeDtypeStruct((d, slots), f32),
        ) + tuple(jax.ShapeDtypeStruct(f.shape, f32) for f in flats),
        in_specs=[vm] * 5,
        out_specs=(vm,) * 7,
        scratch_shapes=[pltpu.VMEM((8, 128), f32)],
        compiler_params=pltpu.CompilerParams(vmem_limit_bytes=vmem_bytes),
        name="flatten",
    )(*sums)
    return (act.T, dx.T, *grads)


def compute_kernel(n, layers, width, hidden_units, ranges, *refs):
    refs = list(refs)
    take = lambda count: [refs.pop(0) for _ in range(count)]
    (w_full,) = take(1)
    tok, cot, tok_up, cot_up = take(4)
    (grad_out,) = take(1)
    act_own, act_up, dx_own, dx_up = take(4)
    w_all, w_one_s, w_two_s, hat1_s, h1_s, qkv_s, p_s, o_s, hat2_s, h2_s, slope_s, a_s = take(12)
    inv_s, dqkv_s, do_s, grad_s, perm = take(5)
    slots = tok.shape[1]
    heads = width // HD
    d = width
    me = lax.axis_index("dev")
    first, last = ranges[me, 0], ranges[me, 1]
    total = ranges[n - 1, 1]
    image = (first + IMG_LEN - 1) // IMG_LEN
    rows = IMAGES_HERE * ROWS

    picks, valid_keys = [], []
    for k in range(IMAGES_HERE):
        begin = (image + k) * IMG_LEN
        count = jnp.where(begin < last, jnp.minimum(IMG_LEN, total - begin), 0)
        r = lax.broadcasted_iota(jnp.int32, (ROWS, 2 * slots), 0)
        c = lax.broadcasted_iota(jnp.int32, (ROWS, 2 * slots), 1)
        t = begin + r
        column = jnp.where(t < last, t - first, t - last + slots)
        column = jnp.where(r < count, column, -1)
        picks.append(jnp.where(column == c, 1.0, 0.0).astype(bf16))
        valid_keys.append(lax.broadcasted_iota(jnp.int32, (ROWS, ROWS), 1) < count)
    pick = jnp.concatenate(picks, axis=0)
    x = mm_nt(pick[:, :slots], tok[...]) + mm_nt(pick[:, slots:], tok_up[...])

    unit = lax.broadcasted_iota(jnp.int32, (1, hidden_units), 1)
    group = sum(jnp.where(unit >= j * d, 1, 0) for j in range(1, 4))
    origin = 4 * (unit - group * d) + group
    f = lax.broadcasted_iota(jnp.int32, (hidden_units, hidden_units), 0)
    perm[...] = jnp.where(f == origin, 1.0, 0.0).astype(bf16)

    vec = [None] * layers
    b_one = [None] * layers
    for l in range(layers):
        w_all[l] = w_full[l]
        w_one_s[l] = mm(w_all[l, :d, 4 * d:8 * d], perm[...]).astype(bf16)
        for j in range(4):
            w_two_s[l, j * d:(j + 1) * d, :] = w_all[l, :d, (8 + j) * d:(9 + j) * d]
        tail = w_all[l, d:d + BLOCK, :]
        vec[l] = tail.astype(f32)[0:1, :]
        b_one[l] = mm(tail[:, 8 * d:], perm[...])[0:1, :]

    def v_of(l, index):
        return vec[l][:, index * d:(index + 1) * d]

    for l in range(layers):
        h, hat, inv = norm_forward(x, v_of(l, 0), v_of(l, 1))
        hat1_s[l], h1_s[l], inv_s[l, 0] = hat, h, inv
        projected = mm(h, w_all[l, :d, :3 * d])
        qkv_s[l, :, :d] = ((projected[:, :d] + v_of(l, 2)).astype(bf16).astype(f32)
                           * (1.0 / math.sqrt(HD))).astype(bf16)
        qkv_s[l, :, d:2 * d] = projected[:, d:2 * d].astype(bf16)
        qkv_s[l, :, 2 * d:] = (projected[:, 2 * d:] + v_of(l, 3)).astype(bf16)
        for i in range(IMAGES_HERE):
            at = slice(i * ROWS, (i + 1) * ROWS)
            for head in range(heads):
                q = qkv_s[l, at, head * HD:(head + 1) * HD]
                key = qkv_s[l, at, d + head * HD:d + (head + 1) * HD]
                val = qkv_s[l, at, 2 * d + head * HD:2 * d + (head + 1) * HD]
                scores = jnp.where(valid_keys[i], mm_nt(q, key), masked_fill)
                e = jnp.exp(scores - jnp.max(scores, axis=-1, keepdims=True))
                p = e * (1.0 / jnp.sum(e, axis=-1, keepdims=True))
                p_s[l, i, head] = p
                o_s[l, at, head * HD:(head + 1) * HD] = mm(p.astype(bf16), val).astype(bf16)
        x1 = x + (mm(o_s[l], w_all[l, :d, 3 * d:4 * d]) + v_of(l, 4))
        h2, hat, inv = norm_forward(x1, v_of(l, 5), v_of(l, 6))
        hat2_s[l], h2_s[l], inv_s[l, 1] = hat, h2, inv
        u = mm(h2, w_one_s[l]) + b_one[l]
        phi = 0.5 * (1.0 + lax.erf(u * (1.0 / math.sqrt(2.0))))
        a_s[l] = (u * phi).astype(bf16)
        slope_s[l] = phi + u * (jnp.exp(-0.5 * u * u) * (1.0 / math.sqrt(2.0 * math.pi)))
        x = x1 + (mm(a_s[l], w_two_s[l]) + v_of(l, 7))

    x_low = x.astype(bf16)
    act_own[...] = mm_tn(x_low, pick[:, :slots]).astype(bf16)
    act_up[...] = mm_tn(x_low, pick[:, slots:]).astype(bf16)

    dx = mm_nt(pick[:, :slots], cot[...]) + mm_nt(pick[:, slots:], cot_up[...])
    for l in reversed(range(layers)):
        dm = dx.astype(bf16)
        g_two = mm_tn(a_s[l], dm)
        for j in range(4):
            grad_s[l, :d, (8 + j) * d:(9 + j) * d] = g_two[j * d:(j + 1) * d, :].astype(bf16)
        g_b2 = rows_sum(dm.astype(f32))
        du = (mm_nt(dm, w_two_s[l]) * slope_s[l]).astype(bf16)
        g_b1 = mm_nt(jnp.broadcast_to(rows_sum(du.astype(f32)), (BLOCK, hidden_units)).astype(bf16),
                     perm[...])[0:1, :]
        g_one = mm_tn(h2_s[l], du).astype(bf16)
        grad_s[l, :d, 4 * d:8 * d] = mm_nt(g_one, perm[...]).astype(bf16)
        dh2 = mm_nt(du, w_one_s[l])
        g_one = mm_tn(h2_s[l], du)
        dv, g_g2, g_c2 = norm_backward(dh2, hat2_s[l], inv_s[l, 1], v_of(l, 5))
        dx1 = dx + dv
        db = dx1.astype(bf16)
        g_bo = rows_sum(db.astype(f32))
        grad_s[l, :d, 3 * d:4 * d] = mm_tn(o_s[l], db).astype(bf16)
        do_s[...] = mm_nt(db, w_all[l, :d, 3 * d:4 * d]).astype(bf16)
        for i in range(IMAGES_HERE):
            at = slice(i * ROWS, (i + 1) * ROWS)
            for head in range(heads):
                q_at = slice(head * HD, (head + 1) * HD)
                k_at = slice(d + head * HD, d + (head + 1) * HD)
                v_at = slice(2 * d + head * HD, 2 * d + (head + 1) * HD)
                do = do_s[at, q_at]
                p = p_s[l, i, head]
                dp = mm_nt(do, qkv_s[l, at, v_at])
                ds = (p * (dp - jnp.sum(p * dp, axis=-1, keepdims=True))).astype(bf16)
                dqkv_s[at, q_at] = (mm(ds, qkv_s[l, at, k_at]) * (1.0 / math.sqrt(HD))).astype(bf16)
                dqkv_s[at, k_at] = mm_tn(ds, qkv_s[l, at, q_at]).astype(bf16)
                dqkv_s[at, v_at] = mm_tn(p.astype(bf16), do).astype(bf16)
        g_bq = rows_sum(dqkv_s[:, :d].astype(f32))
        g_bv = rows_sum(dqkv_s[:, 2 * d:].astype(f32))
        grad_s[l, :d, :3 * d] = mm_tn(h1_s[l], dqkv_s[...]).astype(bf16)
        dh = mm_nt(dqkv_s[...], w_all[l, :d, :3 * d])
        dv, g_g1, g_c1 = norm_backward(dh, hat1_s[l], inv_s[l, 0], v_of(l, 0))
        dx = dx1 + dv
        line = jnp.concatenate([g_g1, g_c1, g_bq, g_bv, g_bo, g_g2, g_c2, g_b2, g_b1], axis=1)
        grad_s[l, d:d + BLOCK, :] = jnp.broadcast_to(line, (BLOCK, line.shape[1])).astype(bf16)

    high = dx.astype(bf16)
    low = (dx - high.astype(f32)).astype(bf16)
    dx_own[...] = mm_tn(high, pick[:, :slots]) + mm_tn(low, pick[:, :slots])
    dx_up[...] = mm_tn(high, pick[:, slots:]).astype(bf16)
    grad_out[...] = grad_s[...]


def compute(n, ranges, weights, tok, cot, tok_up, cot_up, layers):
    d, slots = tok.shape
    hidden_units = 4 * d
    rows = IMAGES_HERE * ROWS
    tall = d + BLOCK
    wide = 12 * d
    args = list(weights) + [tok, cot, tok_up, cot_up]
    outs = [jax.ShapeDtypeStruct((layers, tall, wide), bf16)]
    outs += [
        jax.ShapeDtypeStruct((d, slots), kind) for kind in (bf16, bf16, f32, bf16)
    ]
    vm = pl.BlockSpec(memory_space=pltpu.VMEM)
    return pl.pallas_call(
        functools.partial(compute_kernel, n, layers, d, hidden_units),
        out_shape=tuple(outs),
        in_specs=[pl.BlockSpec(memory_space=pltpu.SMEM)] + [vm] * len(args),
        out_specs=(vm,) * len(outs),
        scratch_shapes=[
            pltpu.VMEM((layers, tall, wide), bf16),
            pltpu.VMEM((layers, d, hidden_units), bf16),
            pltpu.VMEM((layers, hidden_units, d), bf16),
            pltpu.VMEM((layers, rows, d), f32),
            pltpu.VMEM((layers, rows, d), bf16),
            pltpu.VMEM((layers, rows, 3 * d), bf16),
            pltpu.VMEM((layers, IMAGES_HERE, d // HD, ROWS, ROWS), f32),
            pltpu.VMEM((layers, rows, d), bf16),
            pltpu.VMEM((layers, rows, d), f32),
            pltpu.VMEM((layers, rows, d), bf16),
            pltpu.VMEM((layers, rows, hidden_units), f32),
            pltpu.VMEM((layers, rows, hidden_units), bf16),
            pltpu.VMEM((layers, 2, rows, 1), f32),
            pltpu.VMEM((rows, 3 * d), bf16),
            pltpu.VMEM((rows, d), bf16),
            pltpu.VMEM((layers, tall, wide), bf16),
            pltpu.VMEM((hidden_units, hidden_units), bf16),
        ],
        compiler_params=pltpu.CompilerParams(vmem_limit_bytes=vmem_bytes),
        name="two_layers",
    )(ranges, *args)


def rows_of(flats, d):
    w_in, w_out, w_one, w_two = flats
    layers = w_in.shape[0]
    return jnp.concatenate(
        [
            w_in.reshape(layers, -1, 3 * d),
            w_out.reshape(layers, -1, d),
            w_one.reshape(layers, -1, 4 * d),
            w_two.reshape(layers, -1, 4 * d),
        ],
        axis=2,
    )


def flats_of(block, d):
    layers = block.shape[0]
    ends = (0, 3 * d, 4 * d, 8 * d, 12 * d)
    return [block[:, :, lo:hi].reshape(layers, -1) for lo, hi in zip(ends, ends[1:])]


def local_other(tokens, ranges, attn_in, attn_out, mlp_in, mlp_out, vectors, cotangent):
    n = lax.axis_size("dev")
    slots, d = tokens.shape
    layers, part = vectors.shape
    tokens, cotangent = tokens.T, cotangent.T
    flats = (attn_in, attn_out, mlp_in, mlp_out)
    whole = [
        jnp.stack([lax.all_gather(flat[l], "dev", axis=0, tiled=True) for l in range(layers)])
        for flat in flats + (vectors,)
    ]
    line = whole.pop()
    spare = jnp.zeros((layers, BLOCK - 1, 12 * d), bf16)
    block = jnp.concatenate([rows_of(whole, d), line[:, None, :], spare], axis=1)
    down = [(i, (i + n - 1) % n) for i in range(n)]
    tok_up, cot_up = lax.ppermute(tokens, "dev", down), lax.ppermute(cotangent, "dev", down)
    grad, act, act_up, dx, dx_up = compute(
        n, ranges, (block,), tokens, cotangent, tok_up, cot_up, layers
    )
    up = [(i, (i + 1) % n) for i in range(n)]
    act = act + lax.ppermute(act_up, "dev", up)
    dx = dx + lax.ppermute(dx_up, "dev", up)
    terms = flats_of(grad[:, :d], d) + [grad[:, d]]
    grads = [
        jnp.stack([
            lax.psum_scatter(term[l].astype(f32), "dev", scatter_dimension=0, tiled=True)
            for l in range(layers)
        ])
        for term in terms
    ]
    return (act.T, dx.T, *grads)


def solution(mesh):
    flat = P(None, "dev")
    rows = P("dev", None)

    def local(*args):
        n = lax.axis_size("dev")
        slots, d = args[0].shape
        layers = args[2].shape[0]
        fast = n == 32 and d == 6 * n and layers == 2 and slots == 256
        return local_fused(*args) if fast else local_other(*args)

    return jax.shard_map(
        local,
        mesh=mesh,
        in_specs=(rows, P(), flat, flat, flat, flat, flat, rows),
        out_specs=(rows, rows, flat, flat, flat, flat, flat),
        check_vma=False,
    )
```
